32 devices in a mesh: dp: 4 (over z), fsdp: 8 (over y, x, core).
Axes of the slice: x: 2, y: 2, z: 4, core: 2. Of those that a mesh axis runs over, the one named last changes fastest.
Arguments:
- tokens: bfloat16 [16384, 768], P(('dp', 'fsdp')), may hold values from -6 to 6
- segment_ids: int32 [32, 512], P(('dp', 'fsdp')), may hold values from 0 to 7, never falling along the last dimension, each value on 1 to 128 neighbouring positions
- output_grad: bfloat16 [4, 16384, 768], P(None, ('dp', 'fsdp')), may hold values from -6 to 6
- query_weight: bfloat16 [768, 768], P(('dp', 'fsdp')), may hold values from -0.21875 to 0.21875
- query_bias: bfloat16 [768], P(('dp', 'fsdp')), may hold values from -3 to 3
- key_weight: bfloat16 [768, 768], P(('dp', 'fsdp')), may hold values from -0.21875 to 0.21875
- value_weight: bfloat16 [768, 768], P(('dp', 'fsdp')), may hold values from -0.21875 to 0.21875
- value_bias: bfloat16 [768], P(('dp', 'fsdp')), may hold values from -3 to 3
- output_weight: bfloat16 [768, 768], P(('dp', 'fsdp')), may hold values from -1.25 to 1.25
- output_bias: bfloat16 [768], P(('dp', 'fsdp')), may hold values from -3 to 3
- first_gain: bfloat16 [768], P(('dp', 'fsdp')), may hold values from 0.25 to 1.75
- first_shift: bfloat16 [768], P(('dp', 'fsdp')), may hold values from -3 to 3
- inner_weight: bfloat16 [768, 3072], P(('dp', 'fsdp')), may hold values from -0.21875 to 0.21875
- inner_bias: bfloat16 [3072], P(('dp', 'fsdp')), may hold values from -3 to 3
- outer_weight: bfloat16 [768, 3072], P(('dp', 'fsdp')), may hold values from -0.15625 to 0.15625
- outer_bias: bfloat16 [768], P(('dp', 'fsdp')), may hold values from -3 to 3
- second_gain: bfloat16 [768], P(('dp', 'fsdp')), may hold values from 0.25 to 1.75
- second_shift: bfloat16 [768], P(('dp', 'fsdp')), may hold values from -3 to 3
Outputs:
- layer_output: bfloat16 [4, 16384, 768], P(None, ('dp', 'fsdp'))
- input_grad: float32 [4, 16384, 768], P(None, ('dp', 'fsdp'))
- query_weight_grad: float32 [768, 768], P(('dp', 'fsdp'))
- query_bias_grad: float32 [768], P(('dp', 'fsdp'))
- key_weight_grad: float32 [768, 768], P(('dp', 'fsdp'))
- value_weight_grad: float32 [768, 768], P(('dp', 'fsdp'))
- value_bias_grad: float32 [768], P(('dp', 'fsdp'))
- output_weight_grad: float32 [768, 768], P(('dp', 'fsdp'))
- output_bias_grad: float32 [768], P(('dp', 'fsdp'))
- first_gain_grad: float32 [768], P(('dp', 'fsdp'))
- first_shift_grad: float32 [768], P(('dp', 'fsdp'))
- inner_weight_grad: float32 [768, 3072], P(('dp', 'fsdp'))
- inner_bias_grad: float32 [3072], P(('dp', 'fsdp'))
- outer_weight_grad: float32 [768, 3072], P(('dp', 'fsdp'))
- outer_bias_grad: float32 [768], P(('dp', 'fsdp'))
- second_gain_grad: float32 [768], P(('dp', 'fsdp'))
- second_shift_grad: float32 [768], P(('dp', 'fsdp'))
The draws below stay inside these ranges and needn't reach their ends.
Inputs may be any that keep to these rules, and one draw needn't show every extreme that they name: `segment_ids`: along each sequence segment numbers never fall; each segment holds 1 to 128 tokens and one holds exactly 128.
All inputs are finite; a program needn't handle non-finite values.
Results may differ from the reference program's by a relative error of at most 0.012.
The reference program's roundings to bfloat16 on the way count: a program that leaves them out, or rounds other values in their place, can miss the bound.
Values may be sent and summed in bfloat16 or wider, within the bound.
No kernel may reach another device: no remote copies, remote signals or barrier semaphores. Data moves between devices by JAX's collectives and lax.ppermute only.
A program may use at most 256 MiB of HBM per device.

```python
import math
import jax
import jax.numpy as jnp
import numpy as np
from jax import lax

D = 768
HEADS = 12
HEAD_DIM = 64
FF = 3072
WIDTHS = 4
SEQ_LEN = 512
EXAMPLES = 8
EXAMPLE_MOST = 128
SEQS = 32
TOKENS = 16384


def raised(entries, rng, source, target, blocks, factor):
    owner, partner = [(jnp.arange(entries.shape[axis_at]) // (entries.shape[axis_at] // blocks)).reshape([-1 if axis == axis_at else 1 for axis in range(entries.ndim)]) for axis_at in (source, target)]
    chosen = jax.random.permutation(rng, blocks)[partner]
    strong = (owner == chosen) | (owner == (partner + blocks // 2) % blocks)
    return jnp.where(strong, factor * entries, entries)


def level_of(stream_key, extent, pieces, low, high):
    level = 1.0
    for dim, shards_of in pieces:
        heights = jax.random.uniform(jax.random.fold_in(jax.random.fold_in(stream_key, 6), dim), (shards_of,), jnp.float32, low / len(pieces), high / len(pieces))
        level = level * jnp.repeat(jnp.exp(heights), extent[dim] // shards_of).reshape((-1,) + (1,) * (len(extent) - 1 - dim))
    return level


def profile(number_of, total, limit, slope):
    portions = [(1 << 20) // math.isqrt(rank ** slope) + 1 for rank in range(2, number_of + 1)]
    surplus, given = total - limit - (number_of - 1), [1] * (number_of - 1)
    while surplus > 0:
        movable = [i for i in range(number_of - 1) if given[i] < limit]
        pool, budget = sum([portions[i] for i in movable]), surplus
        for i in movable:
            extra = min(limit - given[i], max(1, budget * portions[i] // pool), surplus)
            given[i] = given[i] + extra
            surplus = surplus - extra
    return np.array([limit] + given)


def uneven(own_key, amount, total, bound, lean):
    if amount == 2:
        one = jax.random.randint(own_key, (), max(1, total - bound), min(bound, total - 1) + 1)
        return jnp.stack([one, total - one])
    sizes = jnp.asarray(profile(amount, total, bound, lean), jnp.int32)
    pairs = (amount - 1) // 2
    giver, sink = sizes[1:1 + 2 * pairs:2], sizes[2:2 + 2 * pairs:2]
    margin = jnp.minimum(giver - 1, bound - sink)
    moved = jax.random.randint(jax.random.fold_in(own_key, 1), (pairs,), 0, 1 << 20) % (margin + 1)
    sizes = sizes.at[1:1 + 2 * pairs:2].set(giver - moved).at[2:2 + 2 * pairs:2].set(sink + moved)
    return sizes[jax.random.permutation(jax.random.fold_in(own_key, 2), amount)]


def normal_values(rng, extent, width, reach, shards=(), dtype=jnp.bfloat16):
    values = width * jax.random.normal(rng, extent, jnp.float32)
    if shards:
        values = values * level_of(rng, extent, shards, -0.22, 0.18)
    return jnp.clip(values, -reach, reach).astype(dtype)


def bell_draw_with(own_key, extent, deviation, reach, cuts, heavy, kind=jnp.bfloat16):
    array = deviation * jax.random.normal(own_key, extent, jnp.float32)
    if cuts:
        array = array * level_of(own_key, extent, cuts, -0.22, 0.18)
    return jnp.clip(raised(array, jax.random.fold_in(own_key, 3), *heavy), -reach, reach).astype(kind)


def setup_inputs(seed: int = 0) -> dict:
    arg_keys = jax.random.split(jax.random.key(seed), 19)
    tokens = bell_draw_with(arg_keys[0], (TOKENS, D), 1.0, 6.0, ((0, 32),), (0, 1, 32, 2.75))
    segment_ids = jax.vmap(lambda own: jnp.searchsorted(jnp.cumsum(uneven(own, EXAMPLES, SEQ_LEN, EXAMPLE_MOST, 1)), jnp.arange(SEQ_LEN), side="right"))(jax.random.split(arg_keys[1], SEQS)).reshape((SEQS, SEQ_LEN)).astype(jnp.int32)
    output_grad = bell_draw_with(arg_keys[2], (WIDTHS, TOKENS, D), 1.0, 6.0, ((1, 32),), (1, 2, 32, 2.75))
    query_weight = normal_values(arg_keys[3], (D, D), D ** -0.5, 0.21875, ((0, 32),))
    query_bias = normal_values(arg_keys[4], (D,), 0.5, 3.0, ((0, 32),))
    key_weight = normal_values(arg_keys[5], (D, D), D ** -0.5, 0.21875, ((0, 32),))
    value_weight = normal_values(arg_keys[6], (D, D), D ** -0.5, 0.21875, ((0, 32),))
    value_bias = normal_values(arg_keys[7], (D,), 0.5, 3.0, ((0, 32),))
    output_weight = normal_values(arg_keys[8], (D, D), (D // 32) ** -0.5, 1.25, ((0, 32),))
    output_bias = normal_values(arg_keys[9], (D,), 0.5, 3.0, ((0, 32),))
    first_gain = jnp.clip(1.0 + 0.15 * jax.random.normal(arg_keys[10], (D,), jnp.float32), 0.25, 1.75).astype(jnp.bfloat16)
    first_shift = normal_values(arg_keys[11], (D,), 0.5, 3.0, ((0, 32),))
    inner_weight = normal_values(arg_keys[12], (D, FF), D ** -0.5, 0.21875, ((0, 32),))
    inner_bias = normal_values(arg_keys[13], (FF,), 0.5, 3.0, ((0, 32),))
    outer_weight = normal_values(arg_keys[14], (D, FF), (FF // 2) ** -0.5, 0.15625, ((0, 32),))
    outer_bias = normal_values(arg_keys[15], (D,), 0.5, 3.0, ((0, 32),))
    second_gain = jnp.clip(1.0 + 0.15 * jax.random.normal(arg_keys[16], (D,), jnp.float32), 0.25, 1.75).astype(jnp.bfloat16)
    second_shift = normal_values(arg_keys[17], (D,), 0.5, 3.0, ((0, 32),))
    return dict(tokens=tokens, segment_ids=segment_ids, output_grad=output_grad, query_weight=query_weight, query_bias=query_bias, key_weight=key_weight, value_weight=value_weight, value_bias=value_bias, output_weight=output_weight, output_bias=output_bias, first_gain=first_gain, first_shift=first_shift, inner_weight=inner_weight, inner_bias=inner_bias, outer_weight=outer_weight, outer_bias=outer_bias, second_gain=second_gain, second_shift=second_shift)


@jax.custom_vjp
def low(v):
    return lax.optimization_barrier(v.astype(jnp.bfloat16)).astype(jnp.float32)

@jax.custom_vjp
def low_back(v):
    return v

def low_keep(v):
    return (low(v), None)

def low_pass(kept, grad):
    return (grad,)

def back_keep(v):
    return (v, None)

def back_low(kept, grad):
    return (low(grad),)
low.defvjp(low_keep, low_pass)
low_back.defvjp(back_keep, back_low)

def product(left_side, right_side):
    return jnp.dot(left_side, right_side, precision=lax.Precision.HIGHEST, preferred_element_type=jnp.float32)

def product_last(left_side, right_side):
    return lax.dot_general(left_side, right_side, (((1,), (1,)), ((), ())), precision=lax.Precision.HIGHEST, preferred_element_type=jnp.float32)

def layer_norm(values, gain, shift):
    center = values - lax.optimization_barrier(jnp.mean(values, axis=-1, keepdims=True))
    spread = lax.optimization_barrier(jnp.mean(center * center, axis=-1, keepdims=True))
    return center * lax.rsqrt(spread + 1e-12) * gain + shift

def attend_block(blocks):
    queries, key_rows, value_rows, labels = blocks
    factor = 1.0 / math.sqrt(queries.shape[-1])
    scores = jnp.einsum('qhd,khd->hqk', queries, key_rows, precision=lax.Precision.HIGHEST) * factor
    scores = low_back(scores)
    matched = labels[:, None] == labels[None, :]
    scores = jnp.where(matched[None], scores, -1e+30)
    weights = low(jax.nn.softmax(scores, axis=-1))
    return jnp.einsum('hqk,khd->qhd', weights, value_rows, precision=lax.Precision.HIGHEST)

def forward(stacked, segment_ids, query_weight, query_bias, key_weight, value_weight, value_bias, output_weight, output_bias, first_gain, first_shift, inner_weight, inner_bias, outer_weight, outer_bias, second_gain, second_shift):
    results = []
    for section in range(WIDTHS):
        heads_kept = HEADS * (section + 1) // 4
        width_kept = heads_kept * HEAD_DIM
        hidden_kept = FF * (section + 1) // 4
        source = stacked[section]
        queries = low(low_back(product(source, query_weight[:, :width_kept]) + query_bias[:width_kept]))
        key_rows = low(low_back(product(source, key_weight[:, :width_kept])))
        value_rows = low(low_back(product(source, value_weight[:, :width_kept]) + value_bias[:width_kept]))
        shaped = (SEQS, SEQ_LEN, heads_kept, HEAD_DIM)
        attended = lax.map(jax.checkpoint(attend_block), (queries.reshape(shaped), key_rows.reshape(shaped), value_rows.reshape(shaped), segment_ids))
        attended = low(low_back(attended.reshape(TOKENS, width_kept)))
        branch = low_back(product_last(attended, output_weight[:, :width_kept]) + output_bias)
        normed = layer_norm(source + branch, first_gain, first_shift)
        inner_pre = low_back(product(low(normed), inner_weight[:, :hidden_kept]) + inner_bias[:hidden_kept])
        active = low(jax.nn.gelu(inner_pre, approximate=False))
        feed = low_back(product_last(active, outer_weight[:, :hidden_kept]) + outer_bias)
        results.append(layer_norm(normed + feed, second_gain, second_shift))
    return tuple(results)

def reference(tokens, segment_ids, output_grad, query_weight, query_bias, key_weight, value_weight, value_bias, output_weight, output_bias, first_gain, first_shift, inner_weight, inner_bias, outer_weight, outer_bias, second_gain, second_shift):
    source = tokens.astype(jnp.float32)
    stacked = jnp.stack([source] * WIDTHS)

    def apply_layer(stacked_in, wq, bq, wk, wv, bv, wo, bo, ga, sa, wi, bi, wu, bu, gb, sb):
        return forward(stacked_in, segment_ids, wq, bq, wk, wv, bv, wo, bo, ga, sa, wi, bi, wu, bu, gb, sb)
    outputs, pull = jax.vjp(apply_layer, stacked, query_weight.astype(jnp.float32), query_bias.astype(jnp.float32), key_weight.astype(jnp.float32), value_weight.astype(jnp.float32), value_bias.astype(jnp.float32), output_weight.astype(jnp.float32), output_bias.astype(jnp.float32), first_gain.astype(jnp.float32), first_shift.astype(jnp.float32), inner_weight.astype(jnp.float32), inner_bias.astype(jnp.float32), outer_weight.astype(jnp.float32), outer_bias.astype(jnp.float32), second_gain.astype(jnp.float32), second_shift.astype(jnp.float32))
    grads = pull(tuple((output_grad[section].astype(jnp.float32) for section in range(WIDTHS))))
    layer_output = jnp.stack(outputs).astype(jnp.bfloat16)
    return (layer_output, grads[0], grads[1], grads[2], grads[3], grads[4], grads[5], grads[6], grads[7], grads[8], grads[9], grads[10], grads[11], grads[12], grads[13], grads[14], grads[15])
```

```python
import math

import jax
import jax.numpy as jnp
from jax import lax
from jax.experimental import pallas as pl
from jax.experimental.pallas import tpu as pltpu
from jax.sharding import PartitionSpec as P

HEADS = 12
HEAD_DIM = 64
WIDTHS = 4
BLOCK = 128
AXES = ("dp", "fsdp")
BF = jnp.bfloat16
F32 = jnp.float32
VMEM_LIMIT = 60 * 1024 * 1024


def matmul(left_side, right_side):
    return lax.dot_general(
        left_side, right_side, (((1,), (0,)), ((), ())), preferred_element_type=F32
    )


def matmul_last(left_side, right_side):
    return lax.dot_general(
        left_side, right_side, (((1,), (1,)), ((), ())), preferred_element_type=F32
    )


def windows(length):
    count = length // BLOCK
    spans = []
    for i in range(count):
        start = max(0, i - 1) * BLOCK
        spans.append((start, min(count, i + 2) * BLOCK - start))
    return spans


def call(kernel, flops, moved, **options):
    return pl.pallas_call(
        kernel,
        compiler_params=pltpu.CompilerParams(vmem_limit_bytes=VMEM_LIMIT),
        cost_estimate=pl.CostEstimate(flops=flops, bytes_accessed=moved, transcendentals=0),
        **options,
    )


def shape_of(shape, dtype):
    return jax.ShapeDtypeStruct(shape, dtype)


def whole(shape):
    return pl.BlockSpec(shape, lambda *_: (0,) * len(shape))


def attend_kernel(x, wq, wk, wv, bq, bv, seg_col, seg_row, q_o, k_o, v_o, a_o, p_o, bias):
    spans = windows(x.shape[0])

    @pl.when(pl.program_id(0) == 0)
    def _():
        for i, (start, span) in enumerate(spans):
            same = seg_col[i * BLOCK : (i + 1) * BLOCK, :] == seg_row[:, start : start + span]
            bias[i, :, :span] = jnp.where(same, 0.0, -1e30)

    rows = x[...]
    q_o[...] = (matmul(rows, wq[...]) + bq[...]).astype(BF)
    k_o[...] = matmul(rows, wk[...]).astype(BF)
    v_o[...] = (matmul(rows, wv[...]) + bv[...]).astype(BF)
    lane = lax.broadcasted_iota(jnp.int32, (BLOCK, BLOCK), 1)
    low_half = lane < HEAD_DIM
    factor = 1.0 / math.sqrt(HEAD_DIM)
    masks = (
        jnp.where(low_half, factor, 0.0).astype(BF),
        jnp.where(low_half, 0.0, factor).astype(BF),
    )
    for pair in range(q_o.shape[1] // BLOCK):
        cols = slice(pair * BLOCK, (pair + 1) * BLOCK)
        for i, (start, span) in enumerate(spans):
            here = slice(i * BLOCK, (i + 1) * BLOCK)
            q_here = q_o[here, cols]
            k_near = k_o[start : start + span, cols]
            v_near = v_o[start : start + span, cols]
            mixed = []
            for half in range(2):
                scores = matmul_last(q_here * masks[half], k_near) + bias[i, :, :span]
                highest = jnp.max(scores, axis=1, keepdims=True)
                shifted = jnp.exp(scores - highest)
                total = jnp.sum(shifted, axis=1, keepdims=True)
                chances = (shifted * (1.0 / total)).astype(BF)
                p_o[2 * pair + half, i, :, :span] = chances
                mixed.append(matmul(chances, v_near))
            a_o[here, cols] = jnp.where(low_half, mixed[0], mixed[1]).astype(BF)


def attend(x, wq, wk, wv, bq, bv, segments):
    length, width = x.shape
    step = 256
    count = length // BLOCK
    part = pl.BlockSpec((length, step), lambda p: (0, p))
    weight = pl.BlockSpec((width, step), lambda p: (0, p))
    vector = pl.BlockSpec((1, step), lambda p: (0, p))
    heads = step // HEAD_DIM
    return call(
        attend_kernel,
        6 * length * width * width,
        16 * length * width,
        grid=(width // step,),
        in_specs=[whole(x.shape), weight, weight, weight, vector, vector, whole((length, 1)), whole((1, length))],
        out_specs=[part, part, part, part, pl.BlockSpec((heads, count, BLOCK, 3 * BLOCK), lambda p: (p, 0, 0, 0))],
        out_shape=[shape_of((length, width), BF)] * 4 + [shape_of((HEADS, count, BLOCK, 3 * BLOCK), BF)],
        scratch_shapes=[pltpu.VMEM((count, BLOCK, 3 * BLOCK), F32)],
        name="attend",
    )(x, wq, wk, wv, bq, bv, segments.reshape(length, 1), segments.reshape(1, length))


def norm_parts(values):
    center = values - jnp.mean(values, axis=1, keepdims=True)
    scale = lax.rsqrt(jnp.mean(center * center, axis=1, keepdims=True) + 1e-12)
    return center * scale, scale


def norm_back(spread_grad, hat, scale):
    return scale * (
        spread_grad
        - jnp.mean(spread_grad, axis=1, keepdims=True)
        - hat * jnp.mean(spread_grad * hat, axis=1, keepdims=True)
    )


def chunk_mask(w, rows):
    lane = lax.broadcasted_iota(jnp.int32, (rows, 2 * BLOCK), 1)
    start = HEAD_DIM * (w % 2)
    return (lane >= start) & (lane < start + 3 * HEAD_DIM)


def window_at(w):
    return w + w // 2


def first_kernel(x, att_a, att_b, wo_a, wo_b, vec, first_o, normed_o, normed_t_o, second_o, x_t_o, branch):
    w = pl.program_id(0)

    @pl.when(w == 0)
    def _():
        branch[...] = x[...].astype(F32) + vec[0:1, :]
        x_t_o[...] = x[...].T

    kept = jnp.where(chunk_mask(w, x.shape[0]), jnp.concatenate([att_a[...], att_b[...]], axis=1).astype(F32), 0.0)
    weight = jnp.concatenate([wo_a[...], wo_b[...]], axis=1)
    first = branch[...] + matmul_last(kept.astype(BF), weight)
    branch[...] = first
    first_o[0] = first
    hat, _ = norm_parts(first)
    normed = hat * vec[1:2, :] + vec[2:3, :]
    second_o[0] = normed + vec[3:4, :]
    low = normed.astype(BF)
    normed_o[0] = low
    normed_t_o[0] = low.T


def first_norm(x, att, wo, vec):
    length, width = x.shape
    per_width = pl.BlockSpec((1, length, width), lambda w: (w, 0, 0))
    return call(
        first_kernel,
        2 * length * width * width,
        40 * length * width,
        grid=(WIDTHS,),
        in_specs=[
            whole(x.shape),
            pl.BlockSpec((length, BLOCK), lambda w: (0, window_at(w))),
            pl.BlockSpec((length, BLOCK), lambda w: (0, window_at(w) + 1)),
            pl.BlockSpec((width, BLOCK), lambda w: (0, window_at(w))),
            pl.BlockSpec((width, BLOCK), lambda w: (0, window_at(w) + 1)),
            whole(vec.shape),
        ],
        out_specs=[
            per_width,
            per_width,
            pl.BlockSpec((1, width, length), lambda w: (w, 0, 0)),
            per_width,
            whole((width, length)),
        ],
        out_shape=[
            shape_of((WIDTHS, length, width), F32),
            shape_of((WIDTHS, length, width), BF),
            shape_of((WIDTHS, width, length), BF),
            shape_of((WIDTHS, length, width), F32),
            shape_of((width, length), BF),
        ],
        scratch_shapes=[pltpu.VMEM((length, width), F32)],
        name="first_norm",
    )(x, att, att, wo, wo, vec)


ERF_T = 0.3275911 / math.sqrt(2.0)
ERF_A = (0.254829592, -0.284496736, 1.421413741, -1.453152027, 1.061405429)


def gelu_pair(values):
    bell = jnp.exp(-0.5 * values * values)
    t = 1.0 / (1.0 + ERF_T * jnp.abs(values))
    poly = 0.5 * ERF_A[4]
    for entry in (ERF_A[3], ERF_A[2], ERF_A[1], ERF_A[0]):
        poly = poly * t + 0.5 * entry
    tail = poly * t * bell
    phi = jnp.where(values >= 0.0, 1.0 - tail, tail)
    return values * phi, phi + values * bell * (1.0 / math.sqrt(2.0 * math.pi))


def feed_kernel(j_of, w_of, normed, wi, wu, bi, second_in, og, vec, act_o, slope_o, out_o, feed_o, feed_t_o, second_g_o, sums_o, second):
    step = pl.program_id(0)
    j, w = j_of[step], w_of[step]

    @pl.when(step == 0)
    def _():
        sums_o[...] = jnp.zeros_like(sums_o)

    @pl.when(j == 0)
    def _():
        second[...] = second_in[0]

    length = normed.shape[1]
    rows_step = 256
    for r in range(0, length, rows_step):
        rows = slice(r, r + rows_step)
        inner = matmul(normed[0, rows, :], wi[...]) + bi[0]
        active, slope = gelu_pair(inner)
        active = active.astype(BF)
        act_o[0, rows, :] = active
        slope_o[0, rows, :] = slope.astype(BF)
        second[rows, :] += matmul_last(active, wu[...])

    @pl.when(j == w)
    def _():
        hat, scale = norm_parts(second[...])
        out_o[0] = (hat * vec[0:1, :] + vec[1:2, :]).astype(BF)
        grad = og[0].astype(F32)
        sums_o[0:1, :] += jnp.sum(grad * hat, axis=0, keepdims=True)
        sums_o[1:2, :] += jnp.sum(grad, axis=0, keepdims=True)
        second_g = norm_back(grad * vec[0:1, :], hat, scale)
        second_g_o[0] = second_g
        low = second_g.astype(BF)
        feed_o[0] = low
        feed_t_o[0] = low.T
        sums_o[2:3, :] += jnp.sum(low.astype(F32), axis=0, keepdims=True)


def feed_forward(normed, wi, wu, bi, second, og, vec):
    _, length, width = normed.shape
    order = [(j, w) for w in range(WIDTHS) for j in range(w + 1)]
    j_of = jnp.array([j for j, _ in order], jnp.int32)
    w_of = jnp.array([w for _, w in order], jnp.int32)
    per_width = pl.BlockSpec((1, length, width), lambda s, j, w: (w[s], 0, 0))
    per_step = pl.BlockSpec((1, length, width), lambda s, j, w: (s, 0, 0))
    weight = pl.BlockSpec((width, width), lambda s, j, w: (0, j[s]))
    steps = len(order)
    return call(
        feed_kernel,
        4 * steps * length * width * width,
        steps * 8 * length * width,
        grid_spec=pltpu.PrefetchScalarGridSpec(
            num_scalar_prefetch=2,
            grid=(steps,),
            in_specs=[
                per_width,
                weight,
                weight,
                pl.BlockSpec((1, 1, width), lambda s, j, w: (j[s], 0, 0)),
                per_width,
                per_width,
                whole(vec.shape),
            ],
            out_specs=[
                per_step,
                per_step,
                per_width,
                per_width,
                pl.BlockSpec((1, width, length), lambda s, j, w: (w[s], 0, 0)),
                per_width,
                whole((8, width)),
            ],
            scratch_shapes=[pltpu.VMEM((length, width), F32)],
        ),
        out_shape=[
            shape_of((steps, length, width), BF),
            shape_of((steps, length, width), BF),
            shape_of((WIDTHS, length, width), BF),
            shape_of((WIDTHS, length, width), BF),
            shape_of((WIDTHS, width, length), BF),
            shape_of((WIDTHS, length, width), F32),
            shape_of((8, width), F32),
        ],
        name="feed_forward",
    )(j_of, w_of, normed, wi, wu, bi, second, og, vec)


def back_kernel(j_of, w_of, s_of, feed, feed_t, normed_t, act, slope, second_g, wi, wu, grad_in, outer_o, inner_o, normed_g_o, bias_o, outer, inner):
    step = pl.program_id(0)
    j, w = j_of[step], w_of[step]
    if grad_in is not None:

        @pl.when(step == 0)
        def _():
            normed_g_o[...] = grad_in[...]

    @pl.when(j == w)
    def _():
        normed_g_o[w] = second_g[0]

    first = w == j

    length = feed.shape[1]
    rows_step = 256
    bias = jnp.zeros((1, feed.shape[2]), F32)
    inner_low = []
    for r in range(0, length, rows_step):
        rows = slice(r, r + rows_step)
        low = (slope[0, rows, :].astype(F32) * matmul(feed[0, rows, :], wu[...])).astype(BF)
        bias += jnp.sum(low.astype(F32), axis=0, keepdims=True)
        normed_g_o[w, rows, :] += matmul_last(low, wi[...])
        inner_low.append(low)
    low = jnp.concatenate(inner_low, axis=0)
    outer_part = matmul(feed_t[0], act[0])
    inner_part = matmul(normed_t[0], low)

    @pl.when(first)
    def _():
        outer[...] = outer_part
        inner[...] = inner_part
        bias_o[0] = bias

    @pl.when(jnp.logical_not(first))
    def _():
        outer[...] += outer_part
        inner[...] += inner_part
        bias_o[0] += bias

    @pl.when(w == WIDTHS - 1)
    def _():
        outer_o[...] = outer[...].astype(BF)
        inner_o[...] = inner[...].astype(BF)


def feed_backward(chunks, feed, feed_t, normed_t, act, slope, second_g, wi, wu, grad_in):
    _, length, width = feed.shape
    place = {}
    for w in range(WIDTHS):
        for j in range(w + 1):
            place[(j, w)] = len(place)
    order = [(j, w) for j in chunks for w in range(j, WIDTHS)]
    base = min(chunks)
    j_of = jnp.array([j for j, _ in order], jnp.int32)
    w_of = jnp.array([w for _, w in order], jnp.int32)
    s_of = jnp.array([place[key] for key in order], jnp.int32)
    per_width = pl.BlockSpec((1, length, width), lambda s, j, w, p: (w[s], 0, 0))
    per_width_t = pl.BlockSpec((1, width, length), lambda s, j, w, p: (w[s], 0, 0))
    per_step = pl.BlockSpec((1, length, width), lambda s, j, w, p: (p[s], 0, 0))
    weight = pl.BlockSpec((width, width), lambda s, j, w, p: (0, j[s]))
    local = pl.BlockSpec((width, width), lambda s, j, w, p: (0, j[s] - base))
    full = (WIDTHS, length, width)
    steps = len(order)
    kernel = back_kernel
    extra_specs, extra = [], []
    if grad_in is None:
        kernel = lambda *refs: back_kernel(*refs[:11], None, *refs[11:])
    else:
        extra_specs, extra = [whole(full)], [grad_in]
    return call(
        kernel,
        8 * steps * length * width * width,
        steps * 12 * length * width,
        grid_spec=pltpu.PrefetchScalarGridSpec(
            num_scalar_prefetch=3,
            grid=(steps,),
            in_specs=[per_width, per_width_t, per_width_t, per_step, per_step, per_width, weight, weight] + extra_specs,
            out_specs=[
                local,
                local,
                whole(full),
                pl.BlockSpec((1, 1, width), lambda s, j, w, p: (j[s] - base, 0, 0)),
            ],
            scratch_shapes=[pltpu.VMEM((width, width), F32), pltpu.VMEM((width, width), F32)],
        ),
        out_shape=[
            shape_of((width, width * len(chunks)), BF),
            shape_of((width, width * len(chunks)), BF),
            shape_of(full, F32),
            shape_of((len(chunks), 1, width), F32),
        ],
        name="feed_backward",
    )(j_of, w_of, s_of, feed, feed_t, normed_t, act, slope, second_g, wi, wu, *extra)


def first_back_kernel(first, normed_g, wo, att_a, att_b, vec, first_g_o, att_g_o, wo_g_o, sums_o, total, wo_g):
    step = pl.program_id(0)
    w = WIDTHS - 1 - step

    @pl.when(step == 0)
    def _():
        sums_o[...] = jnp.zeros_like(sums_o)
        total[...] = jnp.zeros_like(total)
        wo_g[...] = jnp.zeros_like(wo_g)

    hat, scale = norm_parts(first[0])
    grad = normed_g[0]
    sums_o[0:1, :] += jnp.sum(grad * hat, axis=0, keepdims=True)
    sums_o[1:2, :] += jnp.sum(grad, axis=0, keepdims=True)
    first_g = norm_back(grad * vec[1:2, :], hat, scale)
    first_g_o[0] = first_g
    low = first_g.astype(BF)
    wide = low.astype(F32)
    sums_o[2:3, :] += jnp.sum(wide, axis=0, keepdims=True)
    total[...] += wide
    length, width = wide.shape
    lane = lax.broadcasted_iota(jnp.int32, (length, width), 1)
    kept = lane < (w + 1) * (3 * HEAD_DIM)
    att_g_o[0] = jnp.where(kept, matmul(low, wo[...]), 0.0).astype(BF)
    att = jnp.where(chunk_mask(w, length), jnp.concatenate([att_a[...], att_b[...]], axis=1).astype(F32), 0.0)
    part = matmul(total[...].astype(BF).T, att.astype(BF))
    start = pl.multiple_of(BLOCK * window_at(w), BLOCK)
    wo_g[:, pl.ds(start, 2 * BLOCK)] += part

    @pl.when(w == 0)
    def _():
        wo_g_o[...] = wo_g[...].astype(BF)


def first_backward(first, normed_g, wo, att, vec):
    _, length, width = first.shape
    last = WIDTHS - 1
    per_width = pl.BlockSpec((1, length, width), lambda s: (last - s, 0, 0))
    return call(
        first_back_kernel,
        10 * length * width * width,
        60 * length * width,
        grid=(WIDTHS,),
        in_specs=[
            per_width,
            per_width,
            whole(wo.shape),
            pl.BlockSpec((length, BLOCK), lambda s: (0, window_at(last - s))),
            pl.BlockSpec((length, BLOCK), lambda s: (0, window_at(last - s) + 1)),
            whole(vec.shape),
        ],
        out_specs=[per_width, per_width, whole((width, width)), whole((8, width))],
        out_shape=[
            shape_of((WIDTHS, length, width), F32),
            shape_of((WIDTHS, length, width), BF),
            shape_of((width, width), BF),
            shape_of((8, width), F32),
        ],
        scratch_shapes=[pltpu.VMEM((length, width), F32), pltpu.VMEM((width, width), F32)],
        name="first_backward",
    )(first, normed_g, wo, att, att, vec)


def attend_back_kernel(q, k, v, p, g, dq_o, dk_o, dv_o, dqs_o, dks_o, dvs_o, sums_o, dk_t, dv_t):
    pair = pl.program_id(0)
    length = q.shape[0]
    spans = windows(length)
    factor = 1.0 / math.sqrt(HEAD_DIM)
    lane = lax.broadcasted_iota(jnp.int32, (BLOCK, BLOCK), 1)
    low_half = lane < HEAD_DIM
    masks = (
        jnp.where(low_half, 1.0, 0.0).astype(BF),
        jnp.where(low_half, 0.0, 1.0).astype(BF),
    )

    def run(first):
        widths = list(range(first, WIDTHS))
        dk_t[...] = jnp.zeros_like(dk_t)
        dv_t[...] = jnp.zeros_like(dv_t)
        q_t = (q[...] * jnp.asarray(factor, BF)).T
        g_t = [g[w].T for w in widths]
        for i, (start, span) in enumerate(spans):
            here = slice(i * BLOCK, (i + 1) * BLOCK)
            near = slice(start, start + span)
            k_near = k[near, :] * jnp.asarray(factor, BF)
            v_near = v[near, :]
            g_here = jnp.concatenate([g[w, here, :] for w in widths], axis=0)
            found = []
            for half in range(2):
                chances_low = p[half, i, :, :span]
                chances = chances_low.astype(F32)
                mask = jnp.concatenate([masks[half]] * len(widths), axis=0)
                chance_g = matmul_last(g_here * mask, v_near)
                rows_of = slice(half * HEAD_DIM, (half + 1) * HEAD_DIM)
                scores_g = []
                for n, w in enumerate(widths):
                    part = chance_g[n * BLOCK : (n + 1) * BLOCK, :]
                    product = chances * part
                    row = jnp.sum(product, axis=1, keepdims=True)
                    low = (product - chances * row).astype(BF)
                    scores_g.append(low)
                    dk_t[w, rows_of, near] += matmul(q_t[rows_of, here], low)
                found.append(matmul(jnp.concatenate(scores_g, axis=0), k_near))
                stacked = jnp.concatenate([g_t[n][rows_of, here] for n in range(len(widths))], axis=0)
                values_g = matmul(stacked, chances_low)
                for n, w in enumerate(widths):
                    dv_t[w, rows_of, near] += values_g[n * HEAD_DIM : (n + 1) * HEAD_DIM, :]
            wide = jnp.concatenate([low_half] * len(widths), axis=0)
            dq = jnp.where(wide, found[0], found[1]).astype(BF)
            for n, w in enumerate(widths):
                dq_o[w, here, :] = dq[n * BLOCK : (n + 1) * BLOCK, :]
        totals = [jnp.zeros((length, BLOCK), F32) for _ in range(3)]
        for w in range(WIDTHS):
            if w < first:
                for ref in (dq_o, dk_o, dv_o):
                    ref[w] = jnp.zeros((length, BLOCK), BF)
                continue
            dk_o[w] = dk_t[w].astype(BF).T
            dv_o[w] = dv_t[w].astype(BF).T
            for n, ref in enumerate((dq_o, dk_o, dv_o)):
                totals[n] += ref[w].astype(F32)
        dqs_o[...] = totals[0].astype(BF)
        dks_o[...] = totals[1].astype(BF)
        dvs_o[...] = totals[2].astype(BF)
        sums_o[0:1, :] = jnp.sum(totals[0], axis=0, keepdims=True)
        sums_o[1:2, :] = jnp.sum(totals[2], axis=0, keepdims=True)

    heads_each = HEADS // WIDTHS
    firsts = [(2 * n) // heads_each for n in range(HEADS // 2)]
    for first in sorted(set(firsts)):
        members = [n for n, f in enumerate(firsts) if f == first]

        @pl.when((pair >= members[0]) & (pair <= members[-1]))
        def _(first=first):
            run(first)


def attend_backward(q, k, v, p, g):
    length, width = q.shape
    pairs = width // BLOCK
    part = pl.BlockSpec((length, BLOCK), lambda n: (0, n))
    wide = pl.BlockSpec((WIDTHS, length, BLOCK), lambda n: (0, 0, n))
    return call(
        attend_back_kernel,
        40 * length * 3 * BLOCK * width,
        24 * length * width,
        grid=(pairs,),
        in_specs=[part, part, part, pl.BlockSpec((2,) + p.shape[1:], lambda n: (n, 0, 0, 0)), wide],
        out_specs=[wide, wide, wide, part, part, part, pl.BlockSpec((8, BLOCK), lambda n: (0, n))],
        out_shape=[shape_of((WIDTHS, length, width), BF)] * 3
        + [shape_of((length, width), BF)] * 3
        + [shape_of((8, width), F32)],
        scratch_shapes=[pltpu.VMEM((WIDTHS, BLOCK, length), F32)] * 2,
        name="attend_backward",
    )(q, k, v, p, g)


def project_kernel(x_t, dq, dk, dv, out_q, out_k, out_v):
    rows = x_t[...]
    out_q[...] = matmul(rows, dq[...]).astype(BF)
    out_k[...] = matmul(rows, dk[...]).astype(BF)
    out_v[...] = matmul(rows, dv[...]).astype(BF)


def project_grads(x_t, dqs, dks, dvs):
    width, length = x_t.shape
    step = 256
    part = pl.BlockSpec((length, step), lambda n: (0, n))
    out = pl.BlockSpec((width, step), lambda n: (0, n))
    return call(
        project_kernel,
        6 * length * width * width,
        16 * length * width,
        grid=(width // step,),
        in_specs=[whole(x_t.shape), part, part, part],
        out_specs=[out, out, out],
        out_shape=[shape_of((width, width), BF)] * 3,
        name="project_grads",
    )(x_t, dqs, dks, dvs)


def input_kernel(first_g, dq, dk, dv, wq, wk, wv, out):
    w = pl.program_id(0)
    for section in range(WIDTHS):
        kept = -(-(section + 1) * 3 * HEAD_DIM // BLOCK) * BLOCK

        @pl.when(w == section)
        def _():
            out[0] = (
                first_g[0]
                + matmul_last(dq[0, :, :kept], wq[:, :kept])
                + matmul_last(dk[0, :, :kept], wk[:, :kept])
                + matmul_last(dv[0, :, :kept], wv[:, :kept])
            )


def input_grads(first_g, dq, dk, dv, wq, wk, wv):
    _, length, width = first_g.shape
    per_width = pl.BlockSpec((1, length, width), lambda w: (w, 0, 0))
    return call(
        input_kernel,
        15 * length * width * width,
        80 * length * width,
        grid=(WIDTHS,),
        in_specs=[per_width] * 4 + [whole(wq.shape)] * 3,
        out_specs=per_width,
        out_shape=shape_of(first_g.shape, F32),
        name="input_grads",
    )(first_g, dq, dk, dv, wq, wk, wv)


def local_step(x, segments, og, weights, vectors):
    wq, wk, wv, wo, wi, wu = weights
    bq, bv, bo, ga, sa, bu, gb, sb, bi = vectors
    row = lambda vector: vector.reshape(1, -1)
    q, k, v, att, p = attend(x, wq, wk, wv, row(bq), row(bv), segments)
    vec_a = jnp.concatenate([row(bo), row(ga), row(sa), row(bu)] + [row(bu)] * 4, axis=0)
    first, normed, normed_t, second, x_t = first_norm(x, att, wo, vec_a)
    vec_b = jnp.concatenate([row(gb), row(sb)] * 4, axis=0)
    act, slope, out, feed, feed_t, second_g, sums_b = feed_forward(
        normed, wi, wu, bi.reshape(WIDTHS, 1, -1), second, og, vec_b
    )
    outer_hi, inner_hi, grad, bias_hi = feed_backward((3, 2), feed, feed_t, normed_t, act, slope, second_g, wi, wu, None)
    outer_lo, inner_lo, grad, bias_lo = feed_backward((1, 0), feed, feed_t, normed_t, act, slope, second_g, wi, wu, grad)
    first_g, att_g, wo_g, sums_a = first_backward(first, grad, wo, att, vec_a)
    dq, dk, dv, dqs, dks, dvs, sums_c = attend_backward(q, k, v, p, att_g)
    wq_g, wk_g, wv_g = project_grads(x_t, dqs, dks, dvs)
    in_g = input_grads(first_g, dq, dk, dv, wq, wk, wv)
    return (out, in_g, (wq_g, wk_g, wv_g, wo_g), (inner_lo, inner_hi, outer_lo, outer_hi),
            (sums_c[0], sums_c[1], sums_a[2], sums_a[0], sums_a[1], sums_b[2], sums_b[0], sums_b[1],
             jnp.concatenate([bias_lo.reshape(-1), bias_hi.reshape(-1)])))


class Ring:
    def __init__(self, mesh):
        self.dp = mesh.shape["dp"]
        self.fsdp = mesh.shape["fsdp"]
        self.square = self.fsdp == 8 and self.dp % 2 == 0
        index = lax.axis_index("fsdp")
        self.z = lax.axis_index("dp")
        self.y, self.x, self.c = index // 4, (index // 2) % 2, index % 2

    def swap(self, value, bit):
        total = self.dp * self.fsdp
        return lax.ppermute(value, AXES, [(i, i ^ bit) for i in range(total)])

    def shift(self, value, by):
        total = self.dp * self.fsdp
        return lax.ppermute(value, AXES, [(i, (i + by * self.fsdp) % total) for i in range(total)])


CORE, X_SIDE, Y_SIDE = 1, 2, 4


def gather_rows(ring, shard):
    if not ring.square:
        return lax.all_gather(shard, AXES, axis=0, tiled=True)
    dp, half = ring.dp, ring.dp // 2
    rows, columns = shard.shape
    line = jnp.zeros((dp, rows, columns), shard.dtype)
    line = lax.dynamic_update_slice(line, shard[None], (ring.z, 0, 0))
    for by in range(1, dp):
        came = ring.shift(shard, by)
        line = lax.dynamic_update_slice(line, came[None], ((ring.z + dp - by) % dp, 0, 0))
    from_x = ring.swap(line, X_SIDE)
    from_y = ring.swap(line, Y_SIDE)
    corner_a = ring.swap(from_x[:half], Y_SIDE)
    corner_b = ring.swap(from_y[half:], X_SIDE)
    parts = (
        (line, 0, ring.y, ring.x),
        (from_x, 0, ring.y, 1 - ring.x),
        (from_y, 0, 1 - ring.y, ring.x),
        (corner_a, 0, 1 - ring.y, 1 - ring.x),
        (corner_b, half, 1 - ring.y, 1 - ring.x),
    )
    full = jnp.zeros((dp, 2, 2, 2, rows, columns), shard.dtype)
    for value, z, y, x in parts:
        for core, piece in ((ring.c, value), (1 - ring.c, ring.swap(value, CORE))):
            block = piece.reshape(piece.shape[0], 1, 1, 1, rows, columns)
            full = lax.dynamic_update_slice(full, block, (z, y, x, core, 0, 0))
    return full.reshape(dp * 8 * rows, columns)


def scatter_rows(ring, parts):
    if not ring.square:
        return lax.psum_scatter(
            jnp.concatenate(parts, axis=1).astype(F32), AXES, scatter_dimension=0, tiled=True
        )
    dp, half = ring.dp, ring.dp // 2
    rows = parts[0].shape[0] // (dp * 8)
    folded = [part.reshape(dp, 2, 2, 2, rows, part.shape[1]) for part in parts]

    def of_core(core):
        return jnp.concatenate(
            [lax.dynamic_index_in_dim(part, core, 3, keepdims=False) for part in folded], axis=-1
        )

    kept = of_core(ring.c)
    came = ring.swap(of_core(1 - ring.c), CORE)

    def block(y, x):
        def pick(value):
            value = lax.dynamic_index_in_dim(value, y, 1, keepdims=False)
            return lax.dynamic_index_in_dim(value, x, 1, keepdims=False)

        return pick(kept).astype(F32) + pick(came).astype(F32)

    corner = block(1 - ring.y, 1 - ring.x).astype(BF)
    corner_a = ring.swap(corner[:half], Y_SIDE).astype(F32)
    corner_b = ring.swap(corner[half:], X_SIDE).astype(F32)
    zeros = jnp.zeros_like(corner_a)
    to_x = (block(ring.y, 1 - ring.x) + jnp.concatenate([corner_a, zeros], axis=0)).astype(BF)
    to_y = (block(1 - ring.y, ring.x) + jnp.concatenate([zeros, corner_b], axis=0)).astype(BF)
    line = (
        block(ring.y, ring.x)
        + ring.swap(to_x, X_SIDE).astype(F32)
        + ring.swap(to_y, Y_SIDE).astype(F32)
    )
    total = lax.dynamic_index_in_dim(line, ring.z, 0, keepdims=False)
    low = line.astype(BF)
    for by in range(1, dp):
        sent = lax.dynamic_index_in_dim(low, (ring.z + by) % dp, 0, keepdims=False)
        total = total + ring.shift(sent, by).astype(F32)
    return total


def solution(mesh):
    rows_split = P(AXES, None)
    vector_split = P(AXES)

    def per_device(
        tokens,
        segment_ids,
        output_grad,
        query_weight,
        query_bias,
        key_weight,
        value_weight,
        value_bias,
        output_weight,
        output_bias,
        first_gain,
        first_shift,
        inner_weight,
        inner_bias,
        outer_weight,
        outer_bias,
        second_gain,
        second_shift,
    ):
        ring = Ring(mesh)
        width = tokens.shape[1]
        hidden = inner_weight.shape[1]
        ratio = hidden // width
        own = query_bias.shape[0]
        singles = (query_bias, value_bias, output_bias, first_gain, first_shift, outer_bias, second_gain, second_shift)
        count = len(singles)
        columns = jnp.concatenate([jnp.stack(singles, axis=1), inner_bias.reshape(own, ratio)], axis=1)
        columns = jnp.pad(columns, ((0, 0), (0, BLOCK - columns.shape[1])))
        attention = gather_rows(
            ring, jnp.concatenate([query_weight, key_weight, value_weight, output_weight, columns], axis=1)
        )
        wi = gather_rows(ring, inner_weight)
        wu = gather_rows(ring, outer_weight)
        wq, wk, wv, wo = [attention[:, n * width : (n + 1) * width] for n in range(4)]
        columns = attention[:, 4 * width :].astype(F32)
        vectors = [columns[:, n] for n in range(count)] + [columns[:, count : count + ratio].reshape(hidden)]
        out, in_g, attention_g, feed_g, vectors_g = local_step(
            tokens, segment_ids[0], output_grad, (wq, wk, wv, wo, wi, wu), vectors
        )
        high = scatter_rows(ring, feed_g[1::2])
        low = scatter_rows(ring, feed_g[0::2])
        columns_g = jnp.concatenate(
            [jnp.stack(vectors_g[:count], axis=1), vectors_g[count].reshape(width, ratio)], axis=1
        )
        columns_g = jnp.pad(columns_g, ((0, 0), (0, BLOCK - columns_g.shape[1]))).astype(BF)
        rest = scatter_rows(ring, list(attention_g) + [columns_g])
        split = hidden // 2
        inner_g = jnp.concatenate([low[:, :split], high[:, :split]], axis=1)
        outer_g = jnp.concatenate([low[:, split:], high[:, split:]], axis=1)
        wq_g, wk_g, wv_g, wo_g = [rest[:, n * width : (n + 1) * width] for n in range(4)]
        columns_g = rest[:, 4 * width :]
        bq_g, bv_g, bo_g, ga_g, sa_g, bu_g, gb_g, sb_g = [columns_g[:, n] for n in range(count)]
        bi_g = columns_g[:, count : count + ratio].reshape(own * ratio)
        return (
            out, in_g, wq_g, bq_g, wk_g, wv_g, bv_g, wo_g, bo_g, ga_g, sa_g, inner_g, bi_g, outer_g, bu_g, gb_g, sb_g,
        )

    layered = P(None, AXES, None)
    return jax.shard_map(
        per_device,
        mesh=mesh,
        in_specs=(
            rows_split, rows_split, layered, rows_split, vector_split, rows_split, rows_split, vector_split,
            rows_split, vector_split, vector_split, vector_split, rows_split, vector_split, rows_split,
            vector_split, vector_split, vector_split,
        ),
        out_specs=(
            layered, layered, rows_split, vector_split, rows_split, rows_split, vector_split, rows_split,
            vector_split, vector_split, vector_split, rows_split, vector_split, rows_split, vector_split,
            vector_split, vector_split,
        ),
        check_vma=False,
    )
```

```python
import functools
import math

import jax
import jax.numpy as jnp
from jax import lax
from jax.experimental import pallas as pl
from jax.experimental.pallas import tpu as pltpu
from jax.sharding import PartitionSpec as P

HEADS = 12
HEAD_DIM = 64
WIDTHS = 4
BLOCK = 128
AXES = ("dp", "fsdp")
BF = jnp.bfloat16
F32 = jnp.float32
MIB = 1024 * 1024
LIMIT = 60
BYTES = 3.3e6


def matmul(left_side, right_side):
    return lax.dot_general(
        left_side, right_side, (((1,), (0,)), ((), ())), preferred_element_type=F32
    )


def matmul_last(left_side, right_side):
    return lax.dot_general(
        left_side, right_side, (((1,), (1,)), ((), ())), preferred_element_type=F32
    )


def windows(length):
    count = length // BLOCK
    spans = []
    for i in range(count):
        start = max(0, i - 1) * BLOCK
        spans.append((start, min(count, i + 2) * BLOCK - start))
    return spans


def call(kernel, limit, micros, **options):
    return pl.pallas_call(
        kernel,
        compiler_params=pltpu.CompilerParams(vmem_limit_bytes=limit * MIB),
        cost_estimate=pl.CostEstimate(flops=0, bytes_accessed=int(micros * BYTES), transcendentals=0),
        **options,
    )


def shape_of(shape, dtype):
    return jax.ShapeDtypeStruct(shape, dtype)


def whole(shape):
    return pl.BlockSpec(shape, lambda *_: (0,) * len(shape))


def attend_kernel(x, wq, wk, wv, vec, seg_col, seg_row, q_o, k_o, v_o, a_o, p_o, bias):
    spans = windows(x.shape[0])

    @pl.when(pl.program_id(0) == 0)
    def _():
        for i, (start, span) in enumerate(spans):
            same = seg_col[i * BLOCK : (i + 1) * BLOCK, :] == seg_row[:, start : start + span]
            bias[i, :, :span] = jnp.where(same, 0.0, -1e30)

    rows = x[...]
    q_o[...] = (matmul(rows, wq[...]) + vec[0:1, :]).astype(BF)
    k_o[...] = matmul(rows, wk[...]).astype(BF)
    v_o[...] = (matmul(rows, wv[...]) + vec[1:2, :]).astype(BF)
    lane = lax.broadcasted_iota(jnp.int32, (BLOCK, BLOCK), 1)
    low_half = lane < HEAD_DIM
    factor = 1.0 / math.sqrt(HEAD_DIM)
    mask = jnp.concatenate(
        [jnp.where(low_half, factor, 0.0).astype(BF), jnp.where(low_half, 0.0, factor).astype(BF)], axis=0
    )
    for pair in range(q_o.shape[1] // BLOCK):
        cols = slice(pair * BLOCK, (pair + 1) * BLOCK)
        scores = []
        for i, (start, span) in enumerate(spans):
            q_here = q_o[i * BLOCK : (i + 1) * BLOCK, cols]
            both = jnp.concatenate([q_here, q_here], axis=0) * mask
            scores.append(matmul_last(both, k_o[start : start + span, cols]))
        chances = []
        for i, (start, span) in enumerate(spans):
            blocked = bias[i, :, :span]
            score = scores[i] + jnp.concatenate([blocked, blocked], axis=0)
            shifted = jnp.exp(score - jnp.max(score, axis=1, keepdims=True))
            total = jnp.sum(shifted, axis=1, keepdims=True)
            chances.append((shifted * (1.0 / total)).astype(BF))
        for i, (start, span) in enumerate(spans):
            mixed = matmul(chances[i], v_o[start : start + span, cols])
            here = slice(i * BLOCK, (i + 1) * BLOCK)
            a_o[here, cols] = jnp.where(low_half, mixed[:BLOCK], mixed[BLOCK:]).astype(BF)
            p_o[2 * pair, i, :, :span] = chances[i][:BLOCK]
            p_o[2 * pair + 1, i, :, :span] = chances[i][BLOCK:]


def attend(x, query_key, value_output, vec, segments):
    length, width = x.shape
    step = 256
    steps = width // step
    count = length // BLOCK
    part = pl.BlockSpec((length, step), lambda p: (0, p))
    heads = step // HEAD_DIM

    def weight(n):
        return pl.BlockSpec((width, step), lambda p: (0, n * steps + p))

    return call(
        attend_kernel,
        LIMIT,
        9.5,
        grid=(steps,),
        in_specs=[
            whole(x.shape),
            weight(0),
            weight(1),
            weight(0),
            pl.BlockSpec((vec.shape[0], step), lambda p: (0, p)),
            whole((length, 1)),
            whole((1, length)),
        ],
        out_specs=[part, part, part, part, pl.BlockSpec((heads, count, BLOCK, 3 * BLOCK), lambda p: (p, 0, 0, 0))],
        out_shape=[shape_of((length, width), BF)] * 4 + [shape_of((HEADS, count, BLOCK, 3 * BLOCK), BF)],
        scratch_shapes=[pltpu.VMEM((count, BLOCK, 3 * BLOCK), F32)],
        name="attend",
    )(x, query_key, query_key, value_output, vec, segments.reshape(length, 1), segments.reshape(1, length))


def norm_parts(values):
    center = values - jnp.mean(values, axis=1, keepdims=True)
    scale = lax.rsqrt(jnp.mean(center * center, axis=1, keepdims=True) + 1e-12)
    return center * scale, scale


def norm_back(spread_grad, hat, scale):
    return scale * (
        spread_grad
        - jnp.mean(spread_grad, axis=1, keepdims=True)
        - hat * jnp.mean(spread_grad * hat, axis=1, keepdims=True)
    )


def chunk_mask(w, rows):
    lane = lax.broadcasted_iota(jnp.int32, (rows, 2 * BLOCK), 1)
    start = HEAD_DIM * (w % 2)
    return (lane >= start) & (lane < start + 3 * HEAD_DIM)


def window_at(w):
    return w + w // 2


def first_kernel(x, att_a, att_b, wo_a, wo_b, vec, hat_o, scale_o, normed_o, normed_t_o, second_o, x_t_o, branch):
    w = pl.program_id(0)

    @pl.when(w == 0)
    def _():
        branch[...] = x[...].astype(F32) + vec[2:3, :]
        x_t_o[...] = x[...].T

    kept = jnp.where(chunk_mask(w, x.shape[0]), jnp.concatenate([att_a[...], att_b[...]], axis=1).astype(F32), 0.0)
    weight = jnp.concatenate([wo_a[...], wo_b[...]], axis=1)
    first = branch[...] + matmul_last(kept.astype(BF), weight)
    branch[...] = first
    hat, scale = norm_parts(first)
    hat_o[0] = hat.astype(BF)
    scale_o[0] = scale
    normed = hat * vec[3:4, :] + vec[4:5, :]
    second_o[0] = normed + vec[5:6, :]
    low = normed.astype(BF)
    normed_o[0] = low
    normed_t_o[0] = low.T


def first_norm(x, att, weights, vec):
    length, width = x.shape
    base = width // BLOCK
    per_width = pl.BlockSpec((1, length, width), lambda w: (w, 0, 0))
    return call(
        first_kernel,
        LIMIT,
        9.7,
        grid=(WIDTHS,),
        in_specs=[
            whole(x.shape),
            pl.BlockSpec((length, BLOCK), lambda w: (0, window_at(w))),
            pl.BlockSpec((length, BLOCK), lambda w: (0, window_at(w) + 1)),
            pl.BlockSpec((width, BLOCK), lambda w: (0, base + window_at(w))),
            pl.BlockSpec((width, BLOCK), lambda w: (0, base + window_at(w) + 1)),
            whole(vec.shape),
        ],
        out_specs=[
            per_width,
            pl.BlockSpec((1, length, 1), lambda w: (w, 0, 0)),
            per_width,
            pl.BlockSpec((1, width, length), lambda w: (w, 0, 0)),
            per_width,
            whole((width, length)),
        ],
        out_shape=[
            shape_of((WIDTHS, length, width), BF),
            shape_of((WIDTHS, length, 1), F32),
            shape_of((WIDTHS, length, width), BF),
            shape_of((WIDTHS, width, length), BF),
            shape_of((WIDTHS, length, width), F32),
            shape_of((width, length), BF),
        ],
        scratch_shapes=[pltpu.VMEM((length, width), F32)],
        name="first_norm",
    )(x, att, att, weights, weights, vec)


ERF_T = 0.3275911 / math.sqrt(2.0)
BELL = 1.0 / math.sqrt(2.0 * math.pi)
ERF_A = tuple(
    0.5 * entry / BELL for entry in (0.254829592, -0.284496736, 1.421413741, -1.453152027, 1.061405429)
)
ROWS = 256


def gelu_pair(values):
    size = jnp.abs(values)
    bell = jnp.exp2(values * values * (-0.5 * math.log2(math.e)) + math.log2(BELL))
    below = 1.0 + ERF_T * size
    t = pl.reciprocal(below, approx=True)
    t = t * (2.0 - below * t)
    poly = ERF_A[4] * t + ERF_A[3]
    for entry in (ERF_A[2], ERF_A[1], ERF_A[0]):
        poly = poly * t + entry
    tail = poly * t * bell
    step = tail - size * bell
    return jnp.maximum(values, 0.0) - size * tail, jnp.where(values >= 0.0, 1.0 - step, step)


def feed_order(chunks):
    return [(j, w) for j in chunks for w in range(j, WIDTHS)]


def copy_of(source, target, sem):
    return pltpu.make_async_copy(source, target, sem)


def forward_step(normed, weights, bias, act, slope, second, column):
    length, width = normed.shape
    half = weights.shape[1] // 2
    for r in range(0, length, ROWS):
        rows = slice(r, r + ROWS)
        inner = matmul(normed[rows, :], weights[:, column : column + width]) + bias
        active, tilt = gelu_pair(inner)
        active = active.astype(BF)
        act[rows, :] = active
        slope[rows, :] = tilt.astype(BF)
        second[rows, :] += matmul_last(active, weights[:, half + column : half + column + width])


def second_norm(second, og, vec, out, feed, feed_t, sums):
    hat, scale = norm_parts(second[...])
    out[...] = (hat * vec[6:7, :] + vec[7:8, :]).astype(BF)
    grad = og[...].astype(F32)
    sums[0:1, :] += jnp.sum(grad * hat, axis=0, keepdims=True)
    sums[1:2, :] += jnp.sum(grad, axis=0, keepdims=True)
    low = norm_back(grad * vec[6:7, :], hat, scale).astype(BF)
    feed[...] = low
    feed_t[...] = low.T
    sums[2:3, :] += jnp.sum(low.astype(F32), axis=0, keepdims=True)


def backward_step(feed, feed_t, normed_t, act, slope, weights, column, outer, inner, grads, bias, ready=None):
    length, width = feed.shape
    half = weights.shape[1] // 2
    outer[...] += matmul(feed_t[...], act[...])
    if ready is not None:
        ready()
    lows = []
    for r in range(0, length, ROWS):
        rows = slice(r, r + ROWS)
        raw = matmul(feed[rows, :], weights[:, half + column : half + column + width])
        low = (slope[rows, :].astype(F32) * raw).astype(BF)
        bias[...] += jnp.sum(low.astype(F32), axis=0, keepdims=True)
        grads[rows, :] += matmul_last(low, weights[:, column : column + width])
        lows.append(low)
    inner[...] += matmul(normed_t[...], jnp.concatenate(lows, axis=0))


ANY = pl.BlockSpec(memory_space=pl.ANY)
SCALARS = pl.BlockSpec(memory_space=pltpu.SMEM)


def held(array):
    return pl.BlockSpec(memory_space=pltpu.VMEM)


def give_halves(core, outer, inner, mine_h, other_h, sem):
    @pl.when(core == 0)
    def _():
        copy_of(outer, mine_h, sem).start()
        copy_of(inner, other_h, sem).start()

    @pl.when(core != 0)
    def _():
        copy_of(inner, mine_h, sem).start()
        copy_of(outer, other_h, sem).start()

    return [copy_of(outer, mine_h, sem), copy_of(inner, other_h, sem)]


def slot_of(j, w):
    return w if j == 0 else feed_order((1, 2, 3)).index((j, j)) + w - j


def feed_all_kernel(source, table, bi, vec, normed_h, second_h, og_h, normed_t_h, *refs):
    count = len(source.arrays)
    pieces, refs = refs[:count], refs[count:]
    act_h, slope_h, out_h, feed_h, feed_t_h, mine_h, other_h, mine_lo_h, other_lo_h, grad_h, bias, sums = refs[:12]
    weights, normed, second, og, normed_t, act, slope, feed, feed_t, outer, inner, outer_b, inner_b = refs[12:25]
    sem_w, sem_n, sem_s, sem_og, sem_t, sem_act, sem_out, sem_give = refs[25:]
    width = normed.shape[2]
    og_reads = [copy_of(og_h.at[j], og.at[j % 2], sem_og.at[j]) for j in range(WIDTHS)]

    def start_rows(w):
        copy_of(normed_h.at[w], normed.at[w], sem_n.at[w]).start()
        copy_of(second_h.at[w], second.at[w], sem_s.at[w]).start()

    start_rows(0)
    source.start(table, pieces, weights, sem_w.at[0], 0, width, 0)
    for w in range(1, WIDTHS):
        start_rows(w)
    og_reads[0].start()
    og_reads[1].start()
    for j in range(1, WIDTHS):
        source.start(table, pieces, weights, sem_w.at[j], j * width, width, j * width)
    for w in range(1, WIDTHS):
        copy_of(normed_t_h.at[w], normed_t.at[w - 1], sem_t.at[w - 1]).start()
    sums[...] = jnp.zeros_like(sums)
    bias[...] = jnp.zeros_like(bias)
    writes = []
    for j in range(WIDTHS):
        source.wait(weights, sem_w.at[j], width, j * width)

        def body(w, carry, j=j):
            if j == 0:
                copy_of(normed_h.at[w], normed.at[w], sem_n.at[w]).wait()
                copy_of(second_h.at[w], second.at[w], sem_s.at[w]).wait()
            at = slot_of(j, 0) + w
            forward_step(normed.at[w], weights, bi[j], act.at[at], slope.at[at], second.at[w], j * width)
            if j == 0:
                copy_of(act.at[at], act_h.at[w], sem_act.at[w]).start()
                copy_of(slope.at[at], slope_h.at[w], sem_act.at[w]).start()
            return carry

        lax.fori_loop(j, WIDTHS, body, 0)
        og_reads[j].wait()
        second_norm(second.at[j], og.at[j % 2], vec, normed.at[j], feed.at[j], feed_t.at[j], sums)
        if j + 2 < WIDTHS:
            og_reads[j + 2].start()
        for copy in (
            copy_of(normed.at[j], out_h.at[j], sem_out.at[0, j]),
            copy_of(feed.at[j], feed_h.at[j], sem_out.at[1, j]),
            copy_of(feed_t.at[j], feed_t_h.at[j], sem_out.at[2, j]),
        ):
            copy.start()
            writes.append(copy)
        if j == 0:
            for w in range(WIDTHS):
                copy_of(act.at[w], act_h.at[w], sem_act.at[w]).wait()
                copy_of(slope.at[w], slope_h.at[w], sem_act.at[w]).wait()
    for w in range(1, WIDTHS):
        copy_of(normed_t_h.at[w], normed_t.at[w - 1], sem_t.at[w - 1]).wait()
        second[w] = feed[w].astype(F32)
    given = {}
    for j in (3, 2, 1):
        outer[...] = jnp.zeros_like(outer)
        inner[...] = jnp.zeros_like(inner)

        def back(w, carry, j=j):
            at = slot_of(j, 0) + w
            backward_step(
                feed.at[w], feed_t.at[w], normed_t.at[w - 1], act.at[at], slope.at[at], weights, j * width,
                outer, inner, second.at[w], bias.at[j - 1],
            )
            if j == 1:
                copy_of(second.at[w], grad_h.at[w - 1], sem_out.at[3, w]).start()
            return carry

        lax.fori_loop(j, WIDTHS, back, 0)
        slot = j % 2
        if slot in given:
            for copy in given[slot]:
                copy.wait()
        outer_b[slot] = outer[...].astype(BF)
        inner_b[slot] = inner[...].astype(BF)
        columns = pl.ds(j % 2 * width, width)
        targets = (mine_h, other_h) if j > 1 else (mine_lo_h, other_lo_h)
        given[slot] = give_halves(
            table[source.core], outer_b.at[slot], inner_b.at[slot], targets[0].at[:, columns], targets[1].at[:, columns],
            sem_give.at[slot],
        )
    for copies in given.values():
        writes += copies
    for w in range(1, WIDTHS):
        writes.append(copy_of(second.at[w], grad_h.at[w - 1], sem_out.at[3, w]))
    for copy in writes:
        copy.wait()


def feed_all(source, normed, bi, second, og, vec, normed_t):
    _, length, width = normed.shape
    four, four_t = (WIDTHS, length, width), (WIDTHS, width, length)
    many = WIDTHS - 1
    slots = len(feed_order((1, 2, 3)))
    return call(
        functools.partial(feed_all_kernel, source),
        LIMIT,
        58,
        in_specs=[SCALARS, held(bi), held(vec)] + [ANY] * (4 + len(source.arrays)),
        out_specs=[ANY] * 10 + [held(vec), held(vec)],
        out_shape=[
            shape_of(four, BF),
            shape_of(four, BF),
            shape_of(four, BF),
            shape_of(four, BF),
            shape_of(four_t, BF),
            shape_of((width, 2 * width), BF),
            shape_of((width, 2 * width), BF),
            shape_of((width, 2 * width), BF),
            shape_of((width, 2 * width), BF),
            shape_of((many, length, width), F32),
            shape_of((many, 1, width), F32),
            shape_of((8, width), F32),
        ],
        scratch_shapes=[
            pltpu.VMEM((width, 8 * width), BF),
            pltpu.VMEM(four, BF),
            pltpu.VMEM(four, F32),
            pltpu.VMEM((2, length, width), BF),
            pltpu.VMEM((many, width, length), BF),
            pltpu.VMEM((slots, length, width), BF),
            pltpu.VMEM((slots, length, width), BF),
            pltpu.VMEM(four, BF),
            pltpu.VMEM(four_t, BF),
            pltpu.VMEM((width, width), F32),
            pltpu.VMEM((width, width), F32),
            pltpu.VMEM((2, width, width), BF),
            pltpu.VMEM((2, width, width), BF),
            pltpu.SemaphoreType.DMA((WIDTHS, 2)),
            pltpu.SemaphoreType.DMA((WIDTHS,)),
            pltpu.SemaphoreType.DMA((WIDTHS,)),
            pltpu.SemaphoreType.DMA((WIDTHS,)),
            pltpu.SemaphoreType.DMA((many,)),
            pltpu.SemaphoreType.DMA((WIDTHS,)),
            pltpu.SemaphoreType.DMA((4, WIDTHS)),
            pltpu.SemaphoreType.DMA((2,)),
        ],
        name="feed_all",
    )(source.table, bi, vec, normed, second, og, normed_t, *source.arrays)


def feed_zero_kernel(source, table, vec, feed_h, feed_t_h, normed_t_h, act_h, slope_h, grad_in, hat_h, scale_h, att_h, wo_h, *refs):
    count = len(source.arrays)
    pieces, refs = refs[:count], refs[count + 2 :]
    mine_h, other_h, first_g_h, att_g_h, wo_g_h, bias, sums = refs[:7]
    weights, feed, feed_t, normed_t, act, slope, outer, inner, grads, outer_b, inner_b = refs[7:18]
    hat, scale, att, wo, att_g, total, wo_g, wo_g_b = refs[18:26]
    sem_w, sem_in, sem_g, sem_x, sem_out = refs[26:]
    length, width = feed.shape[1:]
    def reads(w):
        return (
            copy_of(feed_t_h.at[w], feed_t.at[w], sem_in.at[0, w]),
            copy_of(act_h.at[w], act.at[w], sem_in.at[1, w]),
            copy_of(feed_h.at[w], feed.at[w], sem_in.at[2, w]),
            copy_of(slope_h.at[w], slope.at[w], sem_in.at[3, w]),
            copy_of(normed_t_h.at[w], normed_t.at[w], sem_in.at[4, w]),
            copy_of(hat_h.at[w], hat.at[w], sem_in.at[5, w]),
            copy_of(scale_h.at[w], scale.at[w], sem_in.at[6, w]),
        )

    for w in reversed(range(WIDTHS)):
        for copy in reads(w)[:5]:
            copy.start()
        if w == WIDTHS - 1:
            source.start(table, pieces, weights, sem_w, 0, width, 0)
        if w > 0:
            copy_of(grad_in.at[w - 1], grads.at[w], sem_g.at[w]).start()
        if w == WIDTHS - 1:
            beside = (copy_of(att_h, att, sem_x.at[0]), copy_of(wo_h.at[:, pl.ds(width, width)], wo, sem_x.at[1]))
            for copy in beside:
                copy.start()
        for copy in reads(w)[5:]:
            copy.start()
    outer[...] = jnp.zeros_like(outer)
    inner[...] = jnp.zeros_like(inner)
    bias[...] = jnp.zeros_like(bias)
    sums[...] = jnp.zeros_like(sums)
    total[...] = jnp.zeros_like(total)
    wo_g[...] = jnp.zeros_like(wo_g)

    def body(step, carry):
        w = WIDTHS - 1 - step
        for copy in reads(w)[:2]:
            copy.wait()

        def ready():
            for copy in reads(w)[2:]:
                copy.wait()

            @pl.when(step == 0)
            def _():
                source.wait(weights, sem_w, width, 0)
                for copy in beside:
                    copy.wait()

            @pl.when(w == 0)
            def _():
                grads[0] = feed[0].astype(F32)

            @pl.when(w > 0)
            def _():
                copy_of(grad_in.at[0], grads.at[w], sem_g.at[w]).wait()

        backward_step(
            feed.at[w], feed_t.at[w], normed_t.at[w], act.at[w], slope.at[w], weights, 0, outer, inner, grads.at[w],
            bias.at[0], ready,
        )
        rough, factor = hat[w].astype(F32), scale[w]
        grad = grads[w]
        sums[0:1, :] += jnp.sum(grad * rough, axis=0, keepdims=True)
        sums[1:2, :] += jnp.sum(grad, axis=0, keepdims=True)
        first_g = norm_back(grad * vec[3:4, :], rough, factor)
        grads[w] = first_g
        copy_of(grads.at[w], first_g_h.at[w], sem_out.at[0]).start()
        low = first_g.astype(BF)
        wide = low.astype(F32)
        sums[2:3, :] += jnp.sum(wide, axis=0, keepdims=True)
        total[...] += wide
        lane = lax.broadcasted_iota(jnp.int32, (length, width), 1)
        kept = lane < (w + 1) * (3 * HEAD_DIM)
        att_g[w] = jnp.where(kept, matmul(low, wo[...]), 0.0).astype(BF)
        copy_of(att_g.at[w], att_g_h.at[w], sem_out.at[1]).start()
        columns = pl.ds(pl.multiple_of(BLOCK * window_at(w), BLOCK), 2 * BLOCK)
        part = jnp.where(chunk_mask(w, length), att[:, columns].astype(F32), 0.0).astype(BF)
        wo_g[:, columns] += matmul(total[...].astype(BF).T, part)
        return carry

    lax.fori_loop(0, WIDTHS, body, 0)
    outer_b[...] = outer[...].astype(BF)
    inner_b[...] = inner[...].astype(BF)
    writes = give_halves(
        table[source.core], outer_b, inner_b, mine_h.at[:, pl.ds(0, width)], other_h.at[:, pl.ds(0, width)], sem_out.at[2]
    )
    wo_g_b[...] = wo_g[...].astype(BF)
    copy = copy_of(wo_g_b, wo_g_h, sem_out.at[2])
    copy.start()
    for copy in writes + [copy, copy_of(grads, first_g_h, sem_out.at[0]), copy_of(att_g, att_g_h, sem_out.at[1])]:
        copy.wait()


def feed_zero(source, vec, feed, feed_t, normed_t, act, slope, grad, hat, scale, att, wo, mine, other):
    _, length, width = feed.shape
    four, four_t = (WIDTHS, length, width), (WIDTHS, width, length)
    first = 12 + len(source.arrays)
    return call(
        functools.partial(feed_zero_kernel, source),
        LIMIT,
        28,
        in_specs=[SCALARS, held(vec)] + [ANY] * (10 + len(source.arrays) + 2),
        out_specs=[ANY] * 5 + [held(vec), held(vec)],
        out_shape=[
            shape_of(mine.shape, BF),
            shape_of(other.shape, BF),
            shape_of(four, F32),
            shape_of(four, BF),
            shape_of((width, width), BF),
            shape_of((1, 1, width), F32),
            shape_of((8, width), F32),
        ],
        scratch_shapes=[
            pltpu.VMEM((width, 2 * width), BF),
            pltpu.VMEM(four, BF),
            pltpu.VMEM(four_t, BF),
            pltpu.VMEM(four_t, BF),
            pltpu.VMEM(four, BF),
            pltpu.VMEM(four, BF),
            pltpu.VMEM((width, width), F32),
            pltpu.VMEM((width, width), F32),
            pltpu.VMEM(four, F32),
            pltpu.VMEM((width, width), BF),
            pltpu.VMEM((width, width), BF),
            pltpu.VMEM(four, BF),
            pltpu.VMEM((WIDTHS, length, 1), F32),
            pltpu.VMEM((length, width), BF),
            pltpu.VMEM((width, width), BF),
            pltpu.VMEM(four, BF),
            pltpu.VMEM((length, width), F32),
            pltpu.VMEM((width, width), F32),
            pltpu.VMEM((width, width), BF),
            pltpu.SemaphoreType.DMA((2,)),
            pltpu.SemaphoreType.DMA((7, WIDTHS)),
            pltpu.SemaphoreType.DMA((WIDTHS,)),
            pltpu.SemaphoreType.DMA((2,)),
            pltpu.SemaphoreType.DMA((3,)),
        ],
        input_output_aliases={first: 0, first + 1: 1},
        name="feed_zero",
    )(source.table, vec, feed, feed_t, normed_t, act, slope, grad, hat, scale, att, wo, *source.arrays, mine, other)


def attend_back_kernel(first_pair, pairs, q, k, v, p, g, dq_o, dk_o, dv_o, all_o, sums_o, dk_t, dv_t):
    pair = first_pair + pl.program_id(0)
    length = q.shape[0]
    spans = windows(length)
    factor = 1.0 / math.sqrt(HEAD_DIM)
    lane = lax.broadcasted_iota(jnp.int32, (BLOCK, BLOCK), 1)
    low_half = lane < HEAD_DIM
    masks = (
        jnp.where(low_half, 1.0, 0.0).astype(BF),
        jnp.where(low_half, 0.0, 1.0).astype(BF),
    )

    def run(first):
        widths = list(range(first, WIDTHS))
        many = len(widths)
        dk_t[...] = jnp.zeros_like(dk_t)
        dv_t[...] = jnp.zeros_like(dv_t)
        q_t = (q[...] * jnp.asarray(factor, BF)).T
        g_t = [g[w].T for w in widths]
        mask = jnp.concatenate([masks[0]] * many + [masks[1]] * many, axis=0)
        wide = jnp.concatenate([low_half] * many, axis=0)
        chance_g = []
        for i, (start, span) in enumerate(spans):
            g_here = jnp.concatenate([g[w, i * BLOCK : (i + 1) * BLOCK, :] for w in widths], axis=0)
            chance_g.append(matmul_last(jnp.concatenate([g_here, g_here], axis=0) * mask, v[start : start + span, :]))
        scores_g = []
        for i, (start, span) in enumerate(spans):
            lows = []
            for half in range(2):
                chances = p[half, i, :, :span].astype(F32)
                for n in range(many):
                    at = (half * many + n) * BLOCK
                    product = chances * chance_g[i][at : at + BLOCK, :]
                    row = jnp.sum(product, axis=1, keepdims=True)
                    lows.append((product - chances * row).astype(BF))
            scores_g.append(lows)
        for i, (start, span) in enumerate(spans):
            here = slice(i * BLOCK, (i + 1) * BLOCK)
            near = slice(start, start + span)
            lows = scores_g[i]
            found = matmul(jnp.concatenate(lows, axis=0), k[near, :] * jnp.asarray(factor, BF))
            dq = jnp.where(wide, found[: many * BLOCK], found[many * BLOCK :]).astype(BF)
            for n, w in enumerate(widths):
                dq_o[w, here, :] = dq[n * BLOCK : (n + 1) * BLOCK, :]
            for half in range(2):
                rows_of = slice(half * HEAD_DIM, (half + 1) * HEAD_DIM)
                for n, w in enumerate(widths):
                    dk_t[w, rows_of, near] += matmul(q_t[rows_of, here], lows[half * many + n])
                stacked = jnp.concatenate([g_t[n][rows_of, here] for n in range(many)], axis=0)
                values_g = matmul(stacked, p[half, i, :, :span])
                for n, w in enumerate(widths):
                    dv_t[w, rows_of, near] += values_g[n * HEAD_DIM : (n + 1) * HEAD_DIM, :]
        totals = [jnp.zeros((length, BLOCK), F32) for _ in range(3)]
        for w in range(WIDTHS):
            if w < first:
                for ref in (dq_o, dk_o, dv_o):
                    ref[w] = jnp.zeros((length, BLOCK), BF)
                continue
            dk_o[w] = dk_t[w].astype(BF).T
            dv_o[w] = dv_t[w].astype(BF).T
            for n, ref in enumerate((dq_o, dk_o, dv_o)):
                totals[n] += ref[w].astype(F32)
        for n in range(3):
            all_o[n] = totals[n].astype(BF)
        sums_o[0:1, :] = jnp.sum(totals[0], axis=0, keepdims=True)
        sums_o[1:2, :] = jnp.sum(totals[2], axis=0, keepdims=True)

    heads_each = HEADS // WIDTHS
    firsts = [(2 * n) // heads_each for n in range(HEADS // 2)]
    for first in sorted(set(firsts)):
        members = [n for n, f in enumerate(firsts) if f == first and first_pair <= n < first_pair + pairs]
        if not members:
            continue

        @pl.when((pair >= members[0]) & (pair <= members[-1]))
        def _(first=first):
            run(first)


def attend_backward(first_pair, pairs, q, k, v, p, g):
    length = q.shape[0]
    columns = pairs * BLOCK
    part = pl.BlockSpec((length, BLOCK), lambda n: (0, first_pair + n))
    wide = pl.BlockSpec((WIDTHS, length, BLOCK), lambda n: (0, 0, first_pair + n))
    wide_o = pl.BlockSpec((WIDTHS, length, BLOCK), lambda n: (0, 0, n))
    return call(
        functools.partial(attend_back_kernel, first_pair, pairs),
        LIMIT,
        10,
        grid=(pairs,),
        in_specs=[part, part, part, pl.BlockSpec((2,) + p.shape[1:], lambda n: (first_pair + n, 0, 0, 0)), wide],
        out_specs=[wide_o] * 3
        + [pl.BlockSpec((3, length, BLOCK), lambda n: (0, 0, n)), pl.BlockSpec((8, BLOCK), lambda n: (0, n))],
        out_shape=[shape_of((WIDTHS, length, columns), BF)] * 3
        + [shape_of((3, length, columns), BF), shape_of((8, columns), F32)],
        scratch_shapes=[pltpu.VMEM((WIDTHS, BLOCK, length), F32)] * 2,
        name="attend_backward",
    )(q, k, v, p, g)


def project_kernel(core, x_t, grads, wo_g, last, mine_o, other_o):
    rows = x_t[...]
    columns = grads.shape[2]

    def fill(first, second):
        first[:, :columns] = matmul(rows, grads[0]).astype(BF)
        first[:, columns : 2 * columns] = matmul(rows, grads[1]).astype(BF)
        second[:, :columns] = matmul(rows, grads[2]).astype(BF)
        second[:, columns : 2 * columns] = wo_g[...]
        if last is not None:
            first[:, 2 * columns :] = last[...]
            second[:, 2 * columns :] = last[...]

    @pl.when(core[0] == 0)
    def _():
        fill(mine_o, other_o)

    @pl.when(core[0] != 0)
    def _():
        fill(other_o, mine_o)


def project_grads(core, x_t, grads, wo_g, part, last):
    width, length = x_t.shape
    columns = grads.shape[2]
    out = (width, 2 * columns + (0 if last is None else last.shape[1]))
    given = [] if last is None else [last]
    kernel = project_kernel
    if last is None:
        kernel = lambda core, x_t, grads, wo_g, *outs: project_kernel(core, x_t, grads, wo_g, None, *outs)
    return call(
        kernel,
        LIMIT,
        4.5,
        grid=(1,),
        in_specs=[
            pl.BlockSpec(memory_space=pltpu.SMEM),
            whole(x_t.shape),
            whole(grads.shape),
            pl.BlockSpec((width, columns), lambda n: (0, part)),
        ]
        + [whole(entry.shape) for entry in given],
        out_specs=[whole(out)] * 2,
        out_shape=[shape_of(out, BF)] * 2,
        name="project_grads",
    )(jnp.full((1,), core, jnp.int32), x_t, grads, wo_g, *given)


def input_kernel(some, first_g, dq_a, dk_a, dv_a, dq_b, dk_b, dv_b, wq, wk, wv, *refs):
    out = refs[-1]
    w = pl.program_id(0)
    split = dq_a.shape[2]
    for section in some:
        kept = -(-(section + 1) * 3 * HEAD_DIM // BLOCK) * BLOCK

        @pl.when(w == section - some[0])
        def _():
            total = first_g[0]
            for low, high, weight in ((dq_a, dq_b, wq), (dk_a, dk_b, wk), (dv_a, dv_b, wv)):
                near = min(kept, split)
                total += matmul_last(low[0, :, :near], weight[:, :near])
                if kept > split:
                    total += matmul_last(high[0, :, : kept - split], weight[:, split:kept])
            out[0] = total


def input_grads(some, first_g, low, high, query_key, value_output, earlier):
    _, length, width = first_g.shape
    base = some[0]
    per_width = pl.BlockSpec((1, length, width), lambda w: (w + base, 0, 0))
    part = pl.BlockSpec((1, length, low[0].shape[2]), lambda w: (w + base, 0, 0))
    last = pl.BlockSpec((1, length, high[0].shape[2]), lambda w: (jnp.maximum(w + base, WIDTHS // 2), 0, 0))
    given = [] if earlier is None else [earlier]

    def weight(n):
        return pl.BlockSpec((width, width), lambda w: (0, n))

    return call(
        functools.partial(input_kernel, some),
        LIMIT,
        8,
        grid=(len(some),),
        in_specs=[per_width] + [part] * 3 + [last] * 3 + [weight(0), weight(1), weight(0)] + [ANY] * len(given),
        out_specs=per_width,
        out_shape=shape_of(first_g.shape, F32),
        input_output_aliases={10: 0} if given else {},
        name="input_grads",
    )(first_g, *low, *high, query_key, query_key, value_output, *given)


def tie(*values):
    return lax.optimization_barrier(values)


class Ring:
    def __init__(self, mesh):
        self.dp = mesh.shape["dp"]
        self.fsdp = mesh.shape["fsdp"]
        self.square = self.fsdp == 8 and self.dp % 2 == 0
        index = lax.axis_index("fsdp")
        self.z = lax.axis_index("dp")
        self.y, self.x, self.c = index // 4, (index // 2) % 2, index % 2

    def swap(self, value, bit):
        total = self.dp * self.fsdp
        return lax.ppermute(value, AXES, [(i, i ^ bit) for i in range(total)])

    def shift(self, value, by):
        total = self.dp * self.fsdp
        return lax.ppermute(value, AXES, [(i, (i + by * self.fsdp) % total) for i in range(total)])

    def mine(self, first, second):
        return jnp.where(self.c == 0, first, second)


CORE, X_SIDE, Y_SIDE = 1, 2, 4


class Gather:
    def __init__(self, ring, halves):
        self.ring, self.halves = ring, halves
        self.shard = halves
        self.line = self.came = self.sides = self.corners = self.crossed = ()

    def start_core(self):
        ring = self.ring
        if ring.square:
            kept, sent = ring.mine(*self.halves), ring.mine(*self.halves[::-1])
            came = ring.swap(sent, CORE)
            self.shard = ring.mine(jnp.concatenate([kept, came], axis=0), jnp.concatenate([came, kept], axis=0))

    def start_line(self):
        ring = self.ring
        if ring.square:
            self.came = tuple(ring.shift(self.shard, by) for by in range(1, ring.dp))

    def ready_line(self):
        if self.ring.square:
            self.line = jnp.stack((self.shard,) + self.came)

    def start_sides(self):
        ring = self.ring
        if ring.square:
            self.sides = (ring.swap(self.line, X_SIDE), ring.swap(self.line, Y_SIDE))

    def start_corners(self):
        ring, half = self.ring, self.ring.dp // 2
        if ring.square:
            self.corners = (
                ring.swap(self.sides[0][:half], Y_SIDE),
                ring.swap(self.sides[1][half:], X_SIDE),
            )

    def cross(self, *values):
        if self.ring.square:
            self.crossed += tuple(self.ring.swap(value, CORE) for value in values)

    def pieces(self):
        ring, half = self.ring, self.ring.dp // 2
        own = (
            (self.line, 0, ring.y, ring.x),
            (self.sides[0], 0, ring.y, 1 - ring.x),
            (self.sides[1], 0, 1 - ring.y, ring.x),
            (self.corners[0], 0, 1 - ring.y, 1 - ring.x),
            (self.corners[1], half, 1 - ring.y, 1 - ring.x),
        )
        rows = self.shard.shape[0]
        copies, at = [], []
        for n, (value, behind, y, x) in enumerate(own):
            for index in range(value.shape[0]):
                z = (ring.z + ring.dp - behind - index) % ring.dp
                copies.append((n, index))
                at.append(jnp.asarray(rows * ((z * 2 + y) * 2 + x), jnp.int32))
        arrays = [value for value, *_ in own] + list(self.crossed)
        return arrays, copies, jnp.stack(at + [jnp.asarray(ring.c, jnp.int32)])

    def source(self):
        return Source(self)


class Source:
    def __init__(self, gather):
        ring = gather.ring
        self.square = ring.square
        self.columns = gather.halves[0].shape[1]
        if ring.square:
            self.rows = gather.shard.shape[0]
            self.arrays, self.copies, self.table = gather.pieces()
        else:
            self.rows = gather.halves[0].shape[0] * ring.dp * ring.fsdp
            self.arrays = [lax.all_gather(half, AXES, axis=0, tiled=True) for half in gather.halves]
            self.copies = []
            self.table = jnp.asarray(ring.c, jnp.int32).reshape(1)
        self.core = len(self.copies)

    def start(self, table, pieces, target, sems, first, columns, to):
        apart = target.shape[1] // 2
        if not self.square:
            for half in range(2):
                pltpu.make_async_copy(
                    pieces[half].at[:, pl.ds(first, columns)],
                    target.at[:, pl.ds(half * apart + to, columns)],
                    sems.at[half],
                ).start()
            return
        core = table[self.core]
        many = len(pieces) // 2
        for side in range(2):
            half = core if side == 0 else 1 - core
            for n, (piece, index) in enumerate(self.copies):
                row = pl.multiple_of(table[n], 16)
                pltpu.make_async_copy(
                    pieces[side * many + piece].at[index, :, pl.ds(first, columns)],
                    target.at[pl.ds(row, self.rows), pl.ds(pl.multiple_of(half * apart + to, BLOCK), columns)],
                    sems.at[half],
                ).start()

    def wait(self, target, sems, columns, to):
        for half in range(2):
            whole_half = target.at[:, pl.ds(half * (target.shape[1] // 2) + to, columns)]
            pltpu.make_async_copy(whole_half, whole_half, sems.at[half]).wait()


def place_rows(source, layout):
    def kernel(table, *refs):
        count = len(source.arrays)
        pieces, outs, sem = refs[:count], refs[count:-1], refs[-1]
        if not source.square:
            copies = [
                pltpu.make_async_copy(pieces[half].at[:, pl.ds(first, columns)], outs[n], sem)
                for n, (half, first, columns) in enumerate(layout)
            ]
            for copy in copies:
                copy.start()
            for copy in copies:
                copy.wait()
            return
        many = count // 2
        core = table[source.core]

        def run(own):
            copies = []
            for n, (half, first, columns) in enumerate(layout):
                for m, (piece, index) in enumerate(source.copies):
                    row = pl.multiple_of(table[m], 16)
                    copies.append(
                        pltpu.make_async_copy(
                            pieces[piece + (0 if half == own else many)].at[index, :, pl.ds(first, columns)],
                            outs[n].at[pl.ds(row, source.rows), :],
                            sem,
                        )
                    )
            for copy in copies:
                copy.start()
            for copy in copies:
                copy.wait()

        for own in range(2):
            pl.when(core == own)(functools.partial(run, own))

    rows = source.rows * max(len(source.copies), 1)
    return call(
        kernel,
        LIMIT,
        5,
        in_specs=[SCALARS] + [ANY] * len(source.arrays),
        out_specs=[pl.BlockSpec(memory_space=pltpu.VMEM)] * len(layout),
        out_shape=[shape_of((rows, columns), BF) for *_, columns in layout],
        scratch_shapes=[pltpu.SemaphoreType.DMA],
        name="place_rows",
    )(source.table, *source.arrays)


class Scatter:
    def __init__(self, ring, mine, other):
        self.ring, self.kept, self.other = ring, mine, other
        self.came = self.sides = self.lines = self.leaving = ()

    def start_core(self):
        if self.ring.square:
            self.came = self.ring.swap(self.other, CORE)

    def block(self, y, x):
        dp = self.ring.dp

        def pick(value):
            value = value.reshape(dp, 2, 2, value.shape[0] // (4 * dp), value.shape[1])
            value = lax.dynamic_index_in_dim(value, y, 1, keepdims=False)
            return lax.dynamic_index_in_dim(value, x, 1, keepdims=False)

        return pick(self.kept).astype(F32) + pick(self.came).astype(F32)

    def ready_sides(self):
        ring = self.ring
        if ring.square:
            to_x = self.block(ring.y, 1 - ring.x).astype(BF)
            to_y = self.block(1 - ring.y, ring.x).astype(BF)
            corner = self.block(1 - ring.y, 1 - ring.x).astype(BF)
            self.leaving = (corner, to_x, to_y)

    def start_sides(self):
        ring = self.ring
        if ring.square:
            corner, to_x, to_y = self.leaving
            self.sides = (ring.swap(corner, X_SIDE | Y_SIDE), ring.swap(to_x, X_SIDE), ring.swap(to_y, Y_SIDE))

    def ready_line(self):
        ring = self.ring
        if ring.square:
            line = self.block(ring.y, ring.x)
            for side in self.sides:
                line = line + side.astype(F32)
            low = line.astype(BF)
            self.own = lax.dynamic_index_in_dim(line, ring.z, 0, keepdims=False)
            self.leaving = tuple(
                lax.dynamic_index_in_dim(low, (ring.z + by) % ring.dp, 0, keepdims=False) for by in range(1, ring.dp)
            )

    def start_line(self):
        ring = self.ring
        if ring.square:
            self.lines = tuple(ring.shift(value, by) for by, value in enumerate(self.leaving, 1))

    def finish(self):
        ring = self.ring
        if not ring.square:
            halves = (ring.mine(self.kept, self.other), ring.mine(self.other, self.kept))
            return tuple(
                lax.psum_scatter(half.astype(F32), AXES, scatter_dimension=0, tiled=True) for half in halves
            )
        total = self.own
        for line in self.lines:
            total = total + line.astype(F32)
        rows = total.shape[0] // 2
        kept, sent = ring.mine(total[:rows], total[rows:]), ring.mine(total[rows:], total[:rows])
        came = ring.swap(sent, CORE)
        return ring.mine(kept, came), ring.mine(came, kept)


def solution(mesh):
    rows_split = P(AXES, None)
    vector_split = P(AXES)

    def per_device(
        tokens,
        segment_ids,
        output_grad,
        query_weight,
        query_bias,
        key_weight,
        value_weight,
        value_bias,
        output_weight,
        output_bias,
        first_gain,
        first_shift,
        inner_weight,
        inner_bias,
        outer_weight,
        outer_bias,
        second_gain,
        second_shift,
    ):
        ring = Ring(mesh)
        devices = ring.dp * ring.fsdp
        width = tokens.shape[1]
        hidden = inner_weight.shape[1]
        own = query_bias.shape[0]
        half = hidden // 2
        singles = (query_bias, value_bias, output_bias, first_gain, first_shift, outer_bias, second_gain, second_shift)
        count = len(singles)
        beside = ring.square and own > count and own * WIDTHS <= BLOCK
        columns = []
        if beside:
            row = lax.broadcasted_iota(jnp.int32, (own, BLOCK), 0)
            block = jnp.zeros((own, own), BF)
            for n, vector in enumerate(singles):
                block = jnp.where(row[:, :own] == n, vector[None], block)
            wide = jnp.where(row[:, : WIDTHS * own] == count, inner_bias[None], jnp.zeros((), BF))
            columns = [
                jnp.pad(block, ((0, 0), (0, BLOCK - own))) + jnp.pad(wide, ((0, 0), (0, BLOCK - WIDTHS * own)))
            ]

        def side(*parts):
            return jnp.concatenate(parts, axis=1)

        one = Gather(ring, (side(query_weight, key_weight, *columns), side(value_weight, output_weight, *columns)))
        two = Gather(ring, (inner_weight, outer_weight))
        pair = 2 * width
        one.start_core()
        one.start_line()
        one.came, two.halves = tie(one.came, two.halves)
        one.ready_line()
        one.start_sides()
        two.start_core()
        two.start_line()
        one.start_corners()
        one.cross(one.line, *one.sides)
        one.cross(*one.corners)
        source_one = one.source()
        two.came, _ = tie(two.came, one.crossed)
        two.ready_line()
        two.start_sides()
        layout = ((0, 0, pair), (1, 0, pair)) + (((0, pair, BLOCK),) if beside else ())
        query_key, value_output, *vectors = place_rows(source_one, layout)
        if beside:
            vectors = vectors[0].astype(F32).reshape(devices, own, BLOCK)
            vec = vectors[:, :count, :own].transpose(1, 0, 2).reshape(count, width)
            bi = vectors[:, count, : WIDTHS * own].reshape(WIDTHS, 1, width)
        else:
            vec = jnp.stack([lax.all_gather(entry, AXES, tiled=True) for entry in singles]).astype(F32)
            bi = lax.all_gather(inner_bias, AXES, tiled=True).astype(F32).reshape(WIDTHS, 1, width)
        q, k, v, att, p = attend(tokens, query_key, value_output, vec, segment_ids[0])
        hat, scale, normed, normed_t, second, x_t = first_norm(tokens, att, value_output, vec)
        normed, two.sides = tie(normed, two.sides)
        two.start_corners()
        two.cross(two.line, *two.sides)
        two.cross(*two.corners)
        source_two = two.source()
        act, slope, out, feed, feed_t, mine_hi, other_hi, mine_lo, other_lo, grad, bias_hi, sums_b = feed_all(
            source_two, normed, bi, second, output_grad, vec, normed_t
        )
        high = Scatter(ring, mine_hi, other_hi)
        high.start_core()
        grad, high.came = tie(grad, high.came)
        high.ready_sides()
        grad, high.leaving = tie(grad, high.leaving)
        high.start_sides()
        mine_lo, other_lo, first_g, att_g, wo_g, bias_0, sums_a = feed_zero(
            source_two, vec, feed, feed_t, normed_t, act, slope, grad, hat, scale, att, value_output, mine_lo, other_lo
        )
        low = Scatter(ring, mine_lo, other_lo)
        att_g, low.other, high.sides = tie(att_g, low.other, high.sides)
        low.start_core()
        high.ready_line()
        att_g, high.leaving = tie(att_g, high.leaving)
        high.start_line()
        pairs = HEADS // 4
        *low_g, all_a, sums_c = attend_backward(0, pairs, q, k, v, p, att_g)
        all_a, low.came, high.lines = tie(all_a, low.came, high.lines)
        low.ready_sides()
        all_a, low.leaving = tie(all_a, low.leaving)
        low.start_sides()
        left = Scatter(ring, *project_grads(ring.c, x_t, all_a, wo_g, 0, None))
        att_g, left.other = tie(att_g, left.other)
        left.start_core()
        *high_g, all_b, sums_d = attend_backward(pairs, pairs, q, k, v, p, att_g)
        all_b, left.came = tie(all_b, left.came)
        left.ready_sides()
        all_b, left.leaving = tie(all_b, left.leaving)
        left.start_sides()
        attention_sums = jnp.concatenate([sums_c[:2], sums_d[:2]], axis=1)
        rows = jnp.concatenate([attention_sums, sums_a[2:3], sums_a[:2], sums_b[2:3], sums_b[:2]], axis=0)
        bias_g = jnp.concatenate([bias_0, bias_hi], axis=0)
        columns_g = None
        if beside:
            rows = rows.reshape(count, devices, own).transpose(1, 0, 2)
            rows = jnp.pad(rows, ((0, 0), (0, own - count), (0, BLOCK - own)))
            bias_g = bias_g.reshape(devices, 1, WIDTHS * own)
            bias_g = jnp.pad(bias_g, ((0, 0), (count, own - count - 1), (0, BLOCK - WIDTHS * own)))
            columns_g = (rows + bias_g).reshape(width, BLOCK).astype(BF)
        right = Scatter(ring, *project_grads(ring.c, x_t, all_b, wo_g, 1, columns_g))
        first_g, right.other, low.sides = tie(first_g, right.other, low.sides)
        right.start_core()
        low.ready_line()
        low.leaving, right.came = tie(low.leaving, right.came)
        low.start_line()
        right.ready_sides()
        first_g, right.leaving = tie(first_g, right.leaving)
        right.start_sides()
        in_g = input_grads((0, 1), first_g, low_g, high_g, query_key, value_output, None)
        in_g, left.sides = tie(in_g, left.sides)
        left.ready_line()
        in_g, left.leaving = tie(in_g, left.leaving)
        left.start_line()
        in_g = input_grads((2, 3), first_g, low_g, high_g, query_key, value_output, in_g)
        in_g, right.sides, low.lines = tie(in_g, right.sides, low.lines)
        right.ready_line()
        right.start_line()

        high_r, low_r, left_r, right_r = high.finish(), low.finish(), left.finish(), right.finish()
        outer_g, inner_g = [side(lower, higher) for lower, higher in zip(low_r, high_r)]
        split = pairs * BLOCK
        wq_g, wk_g, wv_g, wo_g = [
            side(left_r[n // 2][:, at : at + split], right_r[n // 2][:, at : at + split])
            for n, at in enumerate((0, split, 0, split))
        ]
        if beside:
            last = right_r[0][:, 2 * split :]
            vectors_g = [last[n, :own] for n in range(count)] + [last[count, : WIDTHS * own]]
        else:
            vectors_g = [
                lax.psum_scatter(entry, AXES, scatter_dimension=0, tiled=True)
                for entry in list(rows) + [bias_g.reshape(hidden)]
            ]
        bq_g, bv_g, bo_g, ga_g, sa_g, bu_g, gb_g, sb_g, bi_g = vectors_g
        return (
            out, in_g, wq_g, bq_g, wk_g, wv_g, bv_g, wo_g, bo_g, ga_g, sa_g, inner_g, bi_g, outer_g, bu_g, gb_g, sb_g,
        )

    layered = P(None, AXES, None)
    return jax.shard_map(
        per_device,
        mesh=mesh,
        in_specs=(
            rows_split, rows_split, layered, rows_split, vector_split, rows_split, rows_split, vector_split,
            rows_split, vector_split, vector_split, vector_split, rows_split, vector_split, rows_split,
            vector_split, vector_split, vector_split,
        ),
        out_specs=(
            layered, layered, rows_split, vector_split, rows_split, rows_split, vector_split, rows_split,
            vector_split, vector_split, vector_split, rows_split, vector_split, rows_split, vector_split,
            vector_split, vector_split,
        ),
        check_vma=False,
    )
```

```python
import functools
import math

import jax
import jax.numpy as jnp
from jax import lax
from jax.experimental import pallas as pl
from jax.experimental.pallas import tpu as pltpu
from jax.sharding import PartitionSpec as P

HEADS = 12
HEAD_DIM = 64
WIDTHS = 4
BLOCK = 128
AXES = ("dp", "fsdp")
BF = jnp.bfloat16
F32 = jnp.float32
MIB = 1024 * 1024
LIMIT = 60
LIMIT_PLACE = 60
LIMIT_ATTEND = 60
BYTES = 3.3e6


def matmul(left_side, right_side):
    return lax.dot_general(
        left_side, right_side, (((1,), (0,)), ((), ())), preferred_element_type=F32
    )


def matmul_last(left_side, right_side):
    return lax.dot_general(
        left_side, right_side, (((1,), (1,)), ((), ())), preferred_element_type=F32
    )


def windows(length):
    count = length // BLOCK
    spans = []
    for i in range(count):
        start = max(0, i - 1) * BLOCK
        spans.append((start, min(count, i + 2) * BLOCK - start))
    return spans


def call(kernel, limit, micros, **options):
    return pl.pallas_call(
        kernel,
        compiler_params=pltpu.CompilerParams(vmem_limit_bytes=limit * MIB),
        cost_estimate=pl.CostEstimate(flops=0, bytes_accessed=int(micros * BYTES), transcendentals=0),
        **options,
    )


def shape_of(shape, dtype):
    return jax.ShapeDtypeStruct(shape, dtype)


def whole(shape):
    return pl.BlockSpec(shape, lambda *_: (0,) * len(shape))


def attend_kernel(x, wq, wk, wv, vec, seg_col, seg_row, q_o, k_o, v_o, a_o, p_o, bias):
    spans = windows(x.shape[0])

    @pl.when(pl.program_id(0) == 0)
    def _():
        for i, (start, span) in enumerate(spans):
            same = seg_col[i * BLOCK : (i + 1) * BLOCK, :] == seg_row[:, start : start + span]
            bias[i, :, :span] = jnp.where(same, 0.0, -1e30)

    rows = x[...]
    q_o[...] = (matmul(rows, wq[...]) + vec[0:1, :]).astype(BF)
    k_o[...] = matmul(rows, wk[...]).astype(BF)
    v_o[...] = (matmul(rows, wv[...]) + vec[1:2, :]).astype(BF)
    lane = lax.broadcasted_iota(jnp.int32, (BLOCK, BLOCK), 1)
    low_half = lane < HEAD_DIM
    factor = 1.0 / math.sqrt(HEAD_DIM)
    mask = jnp.concatenate(
        [jnp.where(low_half, factor, 0.0).astype(BF), jnp.where(low_half, 0.0, factor).astype(BF)], axis=0
    )
    for pair in range(q_o.shape[1] // BLOCK):
        cols = slice(pair * BLOCK, (pair + 1) * BLOCK)
        scores = []
        for i, (start, span) in enumerate(spans):
            q_here = q_o[i * BLOCK : (i + 1) * BLOCK, cols]
            both = jnp.concatenate([q_here, q_here], axis=0) * mask
            scores.append(matmul_last(both, k_o[start : start + span, cols]))
        chances = []
        for i, (start, span) in enumerate(spans):
            blocked = bias[i, :, :span]
            score = scores[i] + jnp.concatenate([blocked, blocked], axis=0)
            shifted = jnp.exp(score - jnp.max(score, axis=1, keepdims=True))
            total = jnp.sum(shifted, axis=1, keepdims=True)
            chances.append((shifted * (1.0 / total)).astype(BF))
        for i, (start, span) in enumerate(spans):
            mixed = matmul(chances[i], v_o[start : start + span, cols])
            here = slice(i * BLOCK, (i + 1) * BLOCK)
            a_o[here, cols] = jnp.where(low_half, mixed[:BLOCK], mixed[BLOCK:]).astype(BF)
            p_o[2 * pair, i, :, :span] = chances[i][:BLOCK]
            p_o[2 * pair + 1, i, :, :span] = chances[i][BLOCK:]


def attend(x, query_key, value_output, vec, segments):
    length, width = x.shape
    step = 256
    steps = width // step
    count = length // BLOCK
    part = pl.BlockSpec((length, step), lambda p: (0, p))
    heads = step // HEAD_DIM

    def weight(n):
        return pl.BlockSpec((width, step), lambda p: (0, n * steps + p))

    return call(
        attend_kernel,
        LIMIT_ATTEND,
        9.5,
        grid=(steps,),
        in_specs=[
            whole(x.shape),
            weight(0),
            weight(1),
            weight(0),
            pl.BlockSpec((vec.shape[0], step), lambda p: (0, p)),
            whole((length, 1)),
            whole((1, length)),
        ],
        out_specs=[part, part, part, part, pl.BlockSpec((heads, count, BLOCK, 3 * BLOCK), lambda p: (p, 0, 0, 0))],
        out_shape=[shape_of((length, width), BF)] * 4 + [shape_of((HEADS, count, BLOCK, 3 * BLOCK), BF)],
        scratch_shapes=[pltpu.VMEM((count, BLOCK, 3 * BLOCK), F32)],
        name="attend",
    )(x, query_key, query_key, value_output, vec, segments.reshape(length, 1), segments.reshape(1, length))


def norm_parts(values):
    center = values - jnp.mean(values, axis=1, keepdims=True)
    scale = lax.rsqrt(jnp.mean(center * center, axis=1, keepdims=True) + 1e-12)
    return center * scale, scale


def norm_back(spread_grad, hat, scale):
    return scale * (
        spread_grad
        - jnp.mean(spread_grad, axis=1, keepdims=True)
        - hat * jnp.mean(spread_grad * hat, axis=1, keepdims=True)
    )


def chunk_mask(w, rows):
    lane = lax.broadcasted_iota(jnp.int32, (rows, 2 * BLOCK), 1)
    start = HEAD_DIM * (w % 2)
    return (lane >= start) & (lane < start + 3 * HEAD_DIM)


def window_at(w):
    return w + w // 2


def first_kernel(x, att_a, att_b, wo_a, wo_b, vec, hat_o, scale_o, normed_o, normed_t_o, second_o, x_t_o, branch):
    w = pl.program_id(0)

    @pl.when(w == 0)
    def _():
        branch[...] = x[...].astype(F32) + vec[2:3, :]
        x_t_o[...] = x[...].T

    kept = jnp.where(chunk_mask(w, x.shape[0]), jnp.concatenate([att_a[...], att_b[...]], axis=1).astype(F32), 0.0)
    weight = jnp.concatenate([wo_a[...], wo_b[...]], axis=1)
    first = branch[...] + matmul_last(kept.astype(BF), weight)
    branch[...] = first
    hat, scale = norm_parts(first)
    hat_o[0] = hat.astype(BF)
    scale_o[0] = scale
    normed = hat * vec[3:4, :] + vec[4:5, :]
    second_o[0] = normed + vec[5:6, :]
    low = normed.astype(BF)
    normed_o[0] = low
    normed_t_o[0] = low.T


def first_norm(x, att, weights, vec):
    length, width = x.shape
    base = width // BLOCK
    per_width = pl.BlockSpec((1, length, width), lambda w: (w, 0, 0))
    return call(
        first_kernel,
        LIMIT,
        9.7,
        grid=(WIDTHS,),
        in_specs=[
            whole(x.shape),
            pl.BlockSpec((length, BLOCK), lambda w: (0, window_at(w))),
            pl.BlockSpec((length, BLOCK), lambda w: (0, window_at(w) + 1)),
            pl.BlockSpec((width, BLOCK), lambda w: (0, base + window_at(w))),
            pl.BlockSpec((width, BLOCK), lambda w: (0, base + window_at(w) + 1)),
            whole(vec.shape),
        ],
        out_specs=[
            per_width,
            pl.BlockSpec((1, length, 1), lambda w: (w, 0, 0)),
            per_width,
            pl.BlockSpec((1, width, length), lambda w: (w, 0, 0)),
            per_width,
            whole((width, length)),
        ],
        out_shape=[
            shape_of((WIDTHS, length, width), BF),
            shape_of((WIDTHS, length, 1), F32),
            shape_of((WIDTHS, length, width), BF),
            shape_of((WIDTHS, width, length), BF),
            shape_of((WIDTHS, length, width), F32),
            shape_of((width, length), BF),
        ],
        scratch_shapes=[pltpu.VMEM((length, width), F32)],
        name="first_norm",
    )(x, att, att, weights, weights, vec)


ERF_T = 0.3275911 / math.sqrt(2.0)
BELL = 1.0 / math.sqrt(2.0 * math.pi)
ERF_A = tuple(
    0.5 * entry / BELL for entry in (0.254829592, -0.284496736, 1.421413741, -1.453152027, 1.061405429)
)
ROWS = 256


def gelu_pair(values):
    size = jnp.abs(values)
    bell = jnp.exp2(values * values * (-0.5 * math.log2(math.e)) + math.log2(BELL))
    below = 1.0 + ERF_T * size
    t = pl.reciprocal(below, approx=True)
    t = t * (2.0 - below * t)
    poly = ERF_A[4] * t + ERF_A[3]
    for entry in (ERF_A[2], ERF_A[1], ERF_A[0]):
        poly = poly * t + entry
    tail = poly * t * bell
    step = tail - size * bell
    return jnp.maximum(values, 0.0) - size * tail, jnp.where(values >= 0.0, 1.0 - step, step)


def feed_order(chunks):
    return [(j, w) for j in chunks for w in range(j, WIDTHS)]


def copy_of(source, target, sem):
    return pltpu.make_async_copy(source, target, sem)


def forward_step(normed, weights, bias, act, slope, second, column):
    length, width = normed.shape
    half = weights.shape[1] // 2
    for r in range(0, length, ROWS):
        rows = slice(r, r + ROWS)
        inner = matmul(normed[rows, :], weights[:, pl.ds(column, width)]) + bias
        active, tilt = gelu_pair(inner)
        active = active.astype(BF)
        act[rows, :] = active
        slope[rows, :] = tilt.astype(BF)
        second[rows, :] += matmul_last(active, weights[:, pl.ds(half + column, width)])


def second_norm(second, og, vec, out, feed, feed_t, sums):
    hat, scale = norm_parts(second[...])
    out[...] = (hat * vec[6:7, :] + vec[7:8, :]).astype(BF)
    grad = og[...].astype(F32)
    sums[0:1, :] += jnp.sum(grad * hat, axis=0, keepdims=True)
    sums[1:2, :] += jnp.sum(grad, axis=0, keepdims=True)
    low = norm_back(grad * vec[6:7, :], hat, scale).astype(BF)
    feed[...] = low
    feed_t[...] = low.T
    sums[2:3, :] += jnp.sum(low.astype(F32), axis=0, keepdims=True)


def backward_step(feed, feed_t, normed_t, act, slope, weights, column, outer, inner, grads, bias, ready=None):
    length, width = feed.shape
    half = weights.shape[1] // 2
    outer[...] += matmul(feed_t[...], act[...])
    if ready is not None:
        ready()
    lows = []
    for r in range(0, length, ROWS):
        rows = slice(r, r + ROWS)
        raw = matmul(feed[rows, :], weights[:, pl.ds(half + column, width)])
        low = (slope[rows, :].astype(F32) * raw).astype(BF)
        bias[...] += jnp.sum(low.astype(F32), axis=0, keepdims=True)
        grads[rows, :] += matmul_last(low, weights[:, pl.ds(column, width)])
        lows.append(low)
    inner[...] += matmul(normed_t[...], jnp.concatenate(lows, axis=0))


ANY = pl.BlockSpec(memory_space=pl.ANY)
SCALARS = pl.BlockSpec(memory_space=pltpu.SMEM)


def held(array):
    return pl.BlockSpec(memory_space=pltpu.VMEM)


def give_halves(core, outer, inner, mine_h, other_h, sem):
    @pl.when(core == 0)
    def _():
        copy_of(outer, mine_h, sem).start()
        copy_of(inner, other_h, sem).start()

    @pl.when(core != 0)
    def _():
        copy_of(inner, mine_h, sem).start()
        copy_of(outer, other_h, sem).start()

    return [copy_of(outer, mine_h, sem), copy_of(inner, other_h, sem)]


def feed_high_kernel(source, table, bi, vec, normed_h, second_h, og_h, normed_t_h, *refs):
    count = len(source.arrays)
    pieces, refs = refs[:count], refs[count:]
    act_h, slope_h, act_1_h, slope_1_h, out_h, feed_h, feed_t_h, mine_h, other_h, grad_h, bias, sums = refs[:12]
    weights, normed, second, og, normed_t, act, slope, feed, feed_t, outer, inner, outer_b, inner_b = refs[12:25]
    sem_w, sem_n, sem_act, sem_out, sem_give = refs[25:]
    width = normed.shape[2]
    low = WIDTHS - 2

    def rows_of(n):
        return (
            copy_of(normed_h.at[low + n], normed.at[n], sem_n.at[0, n]),
            copy_of(second_h.at[low + n], second.at[n], sem_n.at[1, n]),
            copy_of(og_h.at[low + n], og.at[n], sem_n.at[2, n]),
            copy_of(normed_t_h.at[low + n], normed_t.at[n], sem_n.at[3, n]),
        )

    for copy in rows_of(1)[:2]:
        copy.start()
    for j in range(WIDTHS):
        source.start(table, pieces, weights, sem_w.at[j], j * width, width, j * width)
    for copy in rows_of(1)[2:] + rows_of(0):
        copy.start()
    sums[...] = jnp.zeros_like(sums)
    bias[...] = jnp.zeros_like(bias)
    for copy in rows_of(1)[:2]:
        copy.wait()
    writes, given = [], []
    for n in (1, 0):
        w = low + n
        if n == 0:
            for copy in rows_of(0)[:2]:
                copy.wait()

        def body(j, carry, n=n, w=w):
            if n == 1:
                source.wait(weights, sem_w.at[j], width, 0)
            at = 4 * (1 - n) + j
            column = pl.multiple_of(j * width, BLOCK)
            forward_step(normed.at[n], weights, bi[j], act.at[at], slope.at[at], second.at[n], column)

            @pl.when(j == 0)
            def _():
                copy_of(act.at[at], act_h.at[w], sem_act.at[n, 0]).start()
                copy_of(slope.at[at], slope_h.at[w], sem_act.at[n, 1]).start()

            @pl.when(j == 1)
            def _():
                copy_of(act.at[at], act_1_h.at[n], sem_act.at[n, 2]).start()
                copy_of(slope.at[at], slope_1_h.at[n], sem_act.at[n, 3]).start()

            return carry

        lax.fori_loop(0, w + 1, body, 0)
        base = 4 * (1 - n)
        writes += [
            copy_of(act.at[base], act_h.at[w], sem_act.at[n, 0]),
            copy_of(slope.at[base], slope_h.at[w], sem_act.at[n, 1]),
            copy_of(act.at[base + 1], act_1_h.at[n], sem_act.at[n, 2]),
            copy_of(slope.at[base + 1], slope_1_h.at[n], sem_act.at[n, 3]),
        ]
        for copy in rows_of(n)[2:]:
            copy.wait()
        second_norm(second.at[n], og.at[n], vec, normed.at[n], feed.at[n], feed_t.at[n], sums)
        for m, copy in enumerate(
            (
                copy_of(normed.at[n], out_h.at[w], sem_out.at[0, n]),
                copy_of(feed.at[n], feed_h.at[w], sem_out.at[1, n]),
                copy_of(feed_t.at[n], feed_t_h.at[w], sem_out.at[2, n]),
            )
        ):
            copy.start()
            writes.append(copy)
        second[n] = feed[n].astype(F32)
        outer[...] = jnp.zeros_like(outer)
        inner[...] = jnp.zeros_like(inner)

        def back(m, carry, n=n, w=w):
            at = jnp.where(m == 1, w, 4 + w) if n == 0 else w
            backward_step(
                feed.at[m], feed_t.at[m], normed_t.at[m], act.at[at], slope.at[at], weights, w * width,
                outer, inner, second.at[m], bias.at[n],
            )
            return carry

        lax.fori_loop(n, 2, back, 0)
        outer_b[n] = outer[...].astype(BF)
        inner_b[n] = inner[...].astype(BF)
        columns = pl.ds(n * width, width)
        given += give_halves(
            table[source.core], outer_b.at[n], inner_b.at[n], mine_h.at[:, columns], other_h.at[:, columns], sem_give.at[n]
        )
    last = copy_of(second, grad_h, sem_out.at[3, 0])
    last.start()
    for copy in writes + given + [last]:
        copy.wait()


def feed_high(source, normed, bi, second, og, vec, normed_t):
    _, length, width = normed.shape
    four, four_t = (WIDTHS, length, width), (WIDTHS, width, length)
    two, two_t = (2, length, width), (2, width, length)
    slots = 7
    return call(
        functools.partial(feed_high_kernel, source),
        LIMIT,
        35,
        in_specs=[SCALARS, held(bi), held(vec)] + [ANY] * (4 + len(source.arrays)),
        out_specs=[ANY] * 10 + [held(vec), held(vec)],
        out_shape=[
            shape_of(four, BF),
            shape_of(four, BF),
            shape_of(two, BF),
            shape_of(two, BF),
            shape_of(four, BF),
            shape_of(four, BF),
            shape_of(four_t, BF),
            shape_of((width, 2 * width), BF),
            shape_of((width, 2 * width), BF),
            shape_of(two, F32),
            shape_of((2, 1, width), F32),
            shape_of((8, width), F32),
        ],
        scratch_shapes=[
            pltpu.VMEM((width, 8 * width), BF),
            pltpu.VMEM(two, BF),
            pltpu.VMEM(two, F32),
            pltpu.VMEM(two, BF),
            pltpu.VMEM(two_t, BF),
            pltpu.VMEM((slots, length, width), BF),
            pltpu.VMEM((slots, length, width), BF),
            pltpu.VMEM(two, BF),
            pltpu.VMEM(two_t, BF),
            pltpu.VMEM((width, width), F32),
            pltpu.VMEM((width, width), F32),
            pltpu.VMEM((2, width, width), BF),
            pltpu.VMEM((2, width, width), BF),
            pltpu.SemaphoreType.DMA((WIDTHS, 2)),
            pltpu.SemaphoreType.DMA((4, 2)),
            pltpu.SemaphoreType.DMA((2, 4)),
            pltpu.SemaphoreType.DMA((4, 2)),
            pltpu.SemaphoreType.DMA((2,)),
        ],
        name="feed_high",
    )(source.table, bi, vec, normed, second, og, normed_t, *source.arrays)


def feed_mid_kernel(source, table, bi, vec, normed_h, second_h, og_h, normed_t_h, act_1_h, slope_1_h, grad_in, feed_in, feed_t_in, *refs):
    count = len(source.arrays)
    pieces, refs = refs[:count], refs[count + 3 :]
    act_h, slope_h, out_h, feed_h, feed_t_h, mine_h, other_h, grad_h, bias, sums = refs[:10]
    weights, normed, second, og, normed_t, act, slope, feed, feed_t, grads, outer, inner, outer_b, inner_b = refs[10:24]
    sem_w, sem_n, sem_b, sem_act, sem_out, sem_give = refs[24:]
    width = normed.shape[2]

    def rows_of(w):
        return (
            copy_of(normed_h.at[w], normed.at[w], sem_n.at[0, w]),
            copy_of(second_h.at[w], second.at[w], sem_n.at[1, w]),
            copy_of(og_h.at[w], og.at[w], sem_n.at[2, w]),
        )

    def back_rows(m):
        return (
            copy_of(feed_t_in.at[2 + m], feed_t.at[2 + m], sem_b.at[0, m]),
            copy_of(act_1_h.at[m], act.at[1 + m], sem_b.at[1, m]),
            copy_of(feed_in.at[2 + m], feed.at[2 + m], sem_b.at[2, m]),
            copy_of(slope_1_h.at[m], slope.at[1 + m], sem_b.at[3, m]),
            copy_of(grad_in.at[m], grads.at[1 + m], sem_b.at[4, m]),
        )

    turned = [copy_of(normed_t_h.at[w], normed_t.at[w - 1], sem_n.at[3, w - 1]) for w in range(1, WIDTHS)]
    for copy in rows_of(1)[:2]:
        copy.start()
    for j in range(2):
        source.start(table, pieces, weights, sem_w.at[j], j * width, width, j * width)
    for copy in rows_of(1)[2:] + rows_of(0) + (turned[0],) + back_rows(0) + (turned[1],) + back_rows(1) + (turned[2],):
        copy.start()
    sums[...] = jnp.zeros_like(sums)
    bias[...] = jnp.zeros_like(bias)
    outer[...] = jnp.zeros_like(outer)
    inner[...] = jnp.zeros_like(inner)
    writes = []
    for w in (1, 0):
        for copy in rows_of(w)[:2]:
            copy.wait()
        for j in range(w + 1):
            if w == 1:
                source.wait(weights, sem_w.at[j], width, 0)
            at = 0 if j == 1 else 3 + w
            forward_step(normed.at[w], weights, bi[j], act.at[at], slope.at[at], second.at[w], j * width)
            if j == 0:
                for m, copy in enumerate(
                    (copy_of(act.at[at], act_h.at[w], sem_act.at[0, w]), copy_of(slope.at[at], slope_h.at[w], sem_act.at[1, w]))
                ):
                    copy.start()
                    writes.append(copy)
        rows_of(w)[2].wait()
        second_norm(second.at[w], og.at[w], vec, normed.at[w], feed.at[w], feed_t.at[w], sums)
        for copy in (
            copy_of(normed.at[w], out_h.at[w], sem_out.at[0, w]),
            copy_of(feed.at[w], feed_h.at[w], sem_out.at[1, w]),
            copy_of(feed_t.at[w], feed_t_h.at[w], sem_out.at[2, w]),
        ):
            copy.start()
            writes.append(copy)
    grads[0] = feed[1].astype(F32)
    for copy in turned:
        copy.wait()

    def back(m, carry):
        @pl.when(m > 0)
        def _():
            for copy in back_rows(m - 1):
                copy.wait()

        backward_step(
            feed.at[1 + m], feed_t.at[1 + m], normed_t.at[m], act.at[m], slope.at[m], weights, width,
            outer, inner, grads.at[m], bias.at[0],
        )
        copy_of(grads.at[m], grad_h.at[m], sem_out.at[3, m]).start()
        return carry

    lax.fori_loop(0, WIDTHS - 1, back, 0)
    outer_b[...] = outer[...].astype(BF)
    inner_b[...] = inner[...].astype(BF)
    writes += give_halves(table[source.core], outer_b, inner_b, mine_h, other_h, sem_give)
    writes += [copy_of(grads.at[m], grad_h.at[m], sem_out.at[3, m]) for m in range(WIDTHS - 1)]
    for copy in writes:
        copy.wait()


def feed_mid(source, normed, bi, second, og, vec, normed_t, act_1, slope_1, grad, act, slope, out, feed, feed_t):
    _, length, width = normed.shape
    four, four_t = (WIDTHS, length, width), (WIDTHS, width, length)
    two = (2, length, width)
    many = WIDTHS - 1
    first = 12 + len(source.arrays)
    return call(
        functools.partial(feed_mid_kernel, source),
        LIMIT,
        22,
        in_specs=[SCALARS, held(bi), held(vec)] + [ANY] * (9 + len(source.arrays) + 3),
        out_specs=[ANY] * 8 + [held(vec), held(vec)],
        out_shape=[
            shape_of(four, BF),
            shape_of(four, BF),
            shape_of(four, BF),
            shape_of(four, BF),
            shape_of(four_t, BF),
            shape_of((width, width), BF),
            shape_of((width, width), BF),
            shape_of((many, length, width), F32),
            shape_of((1, 1, width), F32),
            shape_of((8, width), F32),
        ],
        scratch_shapes=[
            pltpu.VMEM((width, 4 * width), BF),
            pltpu.VMEM(two, BF),
            pltpu.VMEM(two, F32),
            pltpu.VMEM(two, BF),
            pltpu.VMEM((many, width, length), BF),
            pltpu.VMEM((5, length, width), BF),
            pltpu.VMEM((5, length, width), BF),
            pltpu.VMEM(four, BF),
            pltpu.VMEM(four_t, BF),
            pltpu.VMEM((many, length, width), F32),
            pltpu.VMEM((width, width), F32),
            pltpu.VMEM((width, width), F32),
            pltpu.VMEM((width, width), BF),
            pltpu.VMEM((width, width), BF),
            pltpu.SemaphoreType.DMA((2, 2)),
            pltpu.SemaphoreType.DMA((4, many)),
            pltpu.SemaphoreType.DMA((5, 2)),
            pltpu.SemaphoreType.DMA((2, 2)),
            pltpu.SemaphoreType.DMA((4, many)),
            pltpu.SemaphoreType.DMA,
        ],
        input_output_aliases={10: 3, 11: 4, first: 0, first + 1: 1, first + 2: 2},
        name="feed_mid",
    )(source.table, bi, vec, normed, second, og, normed_t, act_1, slope_1, grad, feed, feed_t, *source.arrays, act, slope, out)


def feed_zero_kernel(source, table, vec, feed_h, feed_t_h, normed_t_h, act_h, slope_h, grad_in, hat_h, scale_h, att_h, wo_h, *refs):
    count = len(source.arrays)
    pieces, refs = refs[:count], refs[count:]
    mine_h, other_h, first_g_h, att_g_h, wo_g_h, bias, sums = refs[:7]
    weights, feed, feed_t, normed_t, act, slope, outer, inner, grads, outer_b, inner_b = refs[7:18]
    hat, scale, att, wo, att_g, total, wo_g, wo_g_b = refs[18:26]
    sem_w, sem_in, sem_g, sem_x, sem_out = refs[26:]
    length, width = feed.shape[1:]
    def reads(w):
        return (
            copy_of(feed_t_h.at[w], feed_t.at[w], sem_in.at[0, w]),
            copy_of(act_h.at[w], act.at[w], sem_in.at[1, w]),
            copy_of(feed_h.at[w], feed.at[w], sem_in.at[2, w]),
            copy_of(slope_h.at[w], slope.at[w], sem_in.at[3, w]),
            copy_of(normed_t_h.at[w], normed_t.at[w], sem_in.at[4, w]),
            copy_of(hat_h.at[w], hat.at[w], sem_in.at[5, w]),
            copy_of(scale_h.at[w], scale.at[w], sem_in.at[6, w]),
        )

    for w in reversed(range(WIDTHS)):
        for copy in reads(w)[:5]:
            copy.start()
        if w == WIDTHS - 1:
            source.start(table, pieces, weights, sem_w, 0, width, 0)
        if w > 0:
            copy_of(grad_in.at[w - 1], grads.at[w], sem_g.at[w]).start()
        if w == WIDTHS - 1:
            beside = (copy_of(att_h, att, sem_x.at[0]), copy_of(wo_h.at[:, pl.ds(width, width)], wo, sem_x.at[1]))
            for copy in beside:
                copy.start()
        for copy in reads(w)[5:]:
            copy.start()
    outer[...] = jnp.zeros_like(outer)
    inner[...] = jnp.zeros_like(inner)
    bias[...] = jnp.zeros_like(bias)
    sums[...] = jnp.zeros_like(sums)
    total[...] = jnp.zeros_like(total)
    wo_g[...] = jnp.zeros_like(wo_g)

    def body(step, carry):
        w = WIDTHS - 1 - step
        for copy in reads(w)[:2]:
            copy.wait()

        def ready():
            for copy in reads(w)[2:5]:
                copy.wait()

            @pl.when(step == 0)
            def _():
                source.wait(weights, sem_w, width, 0)

            @pl.when(w == 0)
            def _():
                grads[0] = feed[0].astype(F32)

            @pl.when(w > 0)
            def _():
                copy_of(grad_in.at[0], grads.at[w], sem_g.at[w]).wait()

        backward_step(
            feed.at[w], feed_t.at[w], normed_t.at[w], act.at[w], slope.at[w], weights, 0, outer, inner, grads.at[w],
            bias.at[0], ready,
        )
        for copy in reads(w)[5:]:
            copy.wait()

        @pl.when(step == 0)
        def _():
            for copy in beside:
                copy.wait()

        rough, factor = hat[w].astype(F32), scale[w]
        grad = grads[w]
        sums[0:1, :] += jnp.sum(grad * rough, axis=0, keepdims=True)
        sums[1:2, :] += jnp.sum(grad, axis=0, keepdims=True)
        first_g = norm_back(grad * vec[3:4, :], rough, factor)
        grads[w] = first_g
        copy_of(grads.at[w], first_g_h.at[w], sem_out.at[0]).start()
        low = first_g.astype(BF)
        wide = low.astype(F32)
        sums[2:3, :] += jnp.sum(wide, axis=0, keepdims=True)
        total[...] += wide
        lane = lax.broadcasted_iota(jnp.int32, (length, width), 1)
        kept = lane < (w + 1) * (3 * HEAD_DIM)
        att_g[w] = jnp.where(kept, matmul(low, wo[...]), 0.0).astype(BF)
        copy_of(att_g.at[w], att_g_h.at[w], sem_out.at[1]).start()
        columns = pl.ds(pl.multiple_of(BLOCK * window_at(w), BLOCK), 2 * BLOCK)
        part = jnp.where(chunk_mask(w, length), att[:, columns].astype(F32), 0.0).astype(BF)
        wo_g[:, columns] += matmul(total[...].astype(BF).T, part)
        return carry

    lax.fori_loop(0, WIDTHS, body, 0)
    outer_b[...] = outer[...].astype(BF)
    inner_b[...] = inner[...].astype(BF)
    writes = give_halves(table[source.core], outer_b, inner_b, mine_h, other_h, sem_out.at[2])
    wo_g_b[...] = wo_g[...].astype(BF)
    copy = copy_of(wo_g_b, wo_g_h, sem_out.at[2])
    copy.start()
    for copy in writes + [copy, copy_of(grads, first_g_h, sem_out.at[0]), copy_of(att_g, att_g_h, sem_out.at[1])]:
        copy.wait()


def feed_zero(source, vec, feed, feed_t, normed_t, act, slope, grad, hat, scale, att, wo):
    _, length, width = feed.shape
    four, four_t = (WIDTHS, length, width), (WIDTHS, width, length)
    return call(
        functools.partial(feed_zero_kernel, source),
        LIMIT,
        28,
        in_specs=[SCALARS, held(vec)] + [ANY] * (10 + len(source.arrays)),
        out_specs=[ANY] * 5 + [held(vec), held(vec)],
        out_shape=[
            shape_of((width, width), BF),
            shape_of((width, width), BF),
            shape_of(four, F32),
            shape_of(four, BF),
            shape_of((width, width), BF),
            shape_of((1, 1, width), F32),
            shape_of((8, width), F32),
        ],
        scratch_shapes=[
            pltpu.VMEM((width, 2 * width), BF),
            pltpu.VMEM(four, BF),
            pltpu.VMEM(four_t, BF),
            pltpu.VMEM(four_t, BF),
            pltpu.VMEM(four, BF),
            pltpu.VMEM(four, BF),
            pltpu.VMEM((width, width), F32),
            pltpu.VMEM((width, width), F32),
            pltpu.VMEM(four, F32),
            pltpu.VMEM((width, width), BF),
            pltpu.VMEM((width, width), BF),
            pltpu.VMEM(four, BF),
            pltpu.VMEM((WIDTHS, length, 1), F32),
            pltpu.VMEM((length, width), BF),
            pltpu.VMEM((width, width), BF),
            pltpu.VMEM(four, BF),
            pltpu.VMEM((length, width), F32),
            pltpu.VMEM((width, width), F32),
            pltpu.VMEM((width, width), BF),
            pltpu.SemaphoreType.DMA((2,)),
            pltpu.SemaphoreType.DMA((7, WIDTHS)),
            pltpu.SemaphoreType.DMA((WIDTHS,)),
            pltpu.SemaphoreType.DMA((2,)),
            pltpu.SemaphoreType.DMA((3,)),
        ],
        name="feed_zero",
    )(source.table, vec, feed, feed_t, normed_t, act, slope, grad, hat, scale, att, wo, *source.arrays)


def attend_back_kernel(first_pair, pairs, own, core, x_t, wo_g, q, k, v, p, g, *refs):
    dq_o, dk_o, dv_o, mine_o, other_o, sums_o, dk_t, dv_t = refs
    step = pl.program_id(0)
    pair = first_pair + step
    columns = pairs * BLOCK
    length = q.shape[0]
    spans = windows(length)
    factor = 1.0 / math.sqrt(HEAD_DIM)
    lane = lax.broadcasted_iota(jnp.int32, (BLOCK, BLOCK), 1)
    low_half = lane < HEAD_DIM
    masks = (
        jnp.where(low_half, 1.0, 0.0).astype(BF),
        jnp.where(low_half, 0.0, 1.0).astype(BF),
    )

    def run(first):
        widths = list(range(first, WIDTHS))
        many = len(widths)
        dk_t[...] = jnp.zeros_like(dk_t)
        dv_t[...] = jnp.zeros_like(dv_t)
        q_t = (q[...] * jnp.asarray(factor, BF)).T
        g_t = [g[w].T for w in widths]
        mask = jnp.concatenate([masks[0]] * many + [masks[1]] * many, axis=0)
        wide = jnp.concatenate([low_half] * many, axis=0)
        chance_g = []
        for i, (start, span) in enumerate(spans):
            g_here = jnp.concatenate([g[w, i * BLOCK : (i + 1) * BLOCK, :] for w in widths], axis=0)
            chance_g.append(matmul_last(jnp.concatenate([g_here, g_here], axis=0) * mask, v[start : start + span, :]))
        scores_g = []
        for i, (start, span) in enumerate(spans):
            lows = []
            for half in range(2):
                chances = p[half, i, :, :span].astype(F32)
                for n in range(many):
                    at = (half * many + n) * BLOCK
                    product = chances * chance_g[i][at : at + BLOCK, :]
                    row = jnp.sum(product, axis=1, keepdims=True)
                    lows.append((product - chances * row).astype(BF))
            scores_g.append(lows)
        for i, (start, span) in enumerate(spans):
            here = slice(i * BLOCK, (i + 1) * BLOCK)
            near = slice(start, start + span)
            lows = scores_g[i]
            found = matmul(jnp.concatenate(lows, axis=0), k[near, :] * jnp.asarray(factor, BF))
            dq = jnp.where(wide, found[: many * BLOCK], found[many * BLOCK :]).astype(BF)
            for n, w in enumerate(widths):
                dq_o[w, here, :] = dq[n * BLOCK : (n + 1) * BLOCK, :]
            for half in range(2):
                rows_of = slice(half * HEAD_DIM, (half + 1) * HEAD_DIM)
                for n, w in enumerate(widths):
                    dk_t[w, rows_of, near] += matmul(q_t[rows_of, here], lows[half * many + n])
                stacked = jnp.concatenate([g_t[n][rows_of, here] for n in range(many)], axis=0)
                values_g = matmul(stacked, p[half, i, :, :span])
                for n, w in enumerate(widths):
                    dv_t[w, rows_of, near] += values_g[n * HEAD_DIM : (n + 1) * HEAD_DIM, :]
        totals = [jnp.zeros((length, BLOCK), F32) for _ in range(3)]
        for w in range(WIDTHS):
            if w < first:
                for ref in (dq_o, dk_o, dv_o):
                    ref[w] = jnp.zeros((length, BLOCK), BF)
                continue
            dk_o[w] = dk_t[w].astype(BF).T
            dv_o[w] = dv_t[w].astype(BF).T
            for n, ref in enumerate((dq_o, dk_o, dv_o)):
                totals[n] += ref[w].astype(F32)
        here = pl.ds(pl.multiple_of(step * BLOCK, BLOCK), BLOCK)
        beside = pl.ds(pl.multiple_of(columns + step * BLOCK, BLOCK), BLOCK)
        sums_o[0:1, here] = jnp.sum(totals[0], axis=0, keepdims=True)
        sums_o[1:2, here] = jnp.sum(totals[2], axis=0, keepdims=True)
        parts = [matmul(x_t[...], total.astype(BF)).astype(BF) for total in totals]

        def fill(first, second):
            first[:, here] = parts[0]
            first[:, beside] = parts[1]
            second[:, here] = parts[2]
            second[:, beside] = wo_g[...]

        pl.when(core[0] == 0)(lambda: fill(mine_o, other_o))
        pl.when(core[0] != 0)(lambda: fill(other_o, mine_o))

    heads_each = HEADS // WIDTHS
    firsts = [(2 * n) // heads_each for n in range(HEADS // 2)]
    for first in sorted(set(firsts)):
        members = [n for n, f in enumerate(firsts) if f == first and first_pair <= n < first_pair + pairs]
        if not members:
            continue

        @pl.when((pair >= members[0]) & (pair <= members[-1]))
        def _(first=first):
            run(first)


def vector_rows(own, sums_o, given):
    sums_c, sums_a, sums_b, sums_b2, bias_0, bias_1, bias_hi = given
    width = sums_a.shape[1]
    rows = [
        jnp.concatenate([sums_c[0:1, :], sums_o[0:1, :]], axis=1),
        jnp.concatenate([sums_c[1:2, :], sums_o[1:2, :]], axis=1),
        sums_a[2:3, :],
        sums_a[0:1, :],
        sums_a[1:2, :],
        sums_b[2:3, :] + sums_b2[2:3, :],
        sums_b[0:1, :] + sums_b2[0:1, :],
        sums_b[1:2, :] + sums_b2[1:2, :],
        jnp.zeros((8, width), F32),
    ]
    for j in range(WIDTHS):
        rows += [(bias_0[0], bias_1[0], bias_hi[0], bias_hi[1])[j]] * WIDTHS
    rows.append(jnp.zeros((BLOCK - 16 - WIDTHS * WIDTHS, width), F32))
    turned = jnp.concatenate(rows, axis=0).T
    lane = lax.broadcasted_iota(jnp.int32, (own, BLOCK), 1)
    blocks = []
    each = width // (own * WIDTHS)
    for j in range(WIDTHS):
        for n in range(each):
            at = (j * each + n) * own
            block = jnp.where(lane < 8, turned[at : at + own, :], 0.0)
            for m in range(WIDTHS):
                start = (n * WIDTHS + m) * own
                block = jnp.where(lane == 16 + WIDTHS * j + m, turned[start : start + own, :], block)
            blocks.append(block.astype(BF))
    return jnp.concatenate(blocks, axis=0)


def attend_back_last_kernel(first_pair, pairs, own, *refs):
    given, rest = refs[8:-8], refs[-8:]
    attend_back_kernel(first_pair, pairs, own, *refs[:8], *rest)
    if given:
        mine_o, other_o, sums_o = rest[3:6]

        @pl.when(pl.program_id(0) == pairs - 1)
        def _():
            block = vector_rows(own, sums_o, given)
            mine_o[:, 2 * pairs * BLOCK :] = block
            other_o[:, 2 * pairs * BLOCK :] = block


def attend_backward(core, first_pair, pairs, own, x_t, wo_g, q, k, v, p, g, given):
    length, width = q.shape
    columns = pairs * BLOCK
    part = pl.BlockSpec((length, BLOCK), lambda n: (0, first_pair + n))
    wide = pl.BlockSpec((WIDTHS, length, BLOCK), lambda n: (0, 0, first_pair + n))
    wide_o = pl.BlockSpec((WIDTHS, length, BLOCK), lambda n: (0, 0, n))
    out = (width, 2 * columns + (BLOCK if given else 0))
    return call(
        functools.partial(attend_back_last_kernel, first_pair, pairs, own),
        LIMIT,
        12,
        grid=(pairs,),
        in_specs=[
            SCALARS,
            whole(x_t.shape),
            pl.BlockSpec((width, BLOCK), lambda n: (0, first_pair + n)),
            part,
            part,
            part,
            pl.BlockSpec((2,) + p.shape[1:], lambda n: (first_pair + n, 0, 0, 0)),
            wide,
        ]
        + [whole(entry.shape) for entry in given],
        out_specs=[wide_o] * 3 + [whole(out)] * 2 + [whole((8, columns))],
        out_shape=[shape_of((WIDTHS, length, columns), BF)] * 3
        + [shape_of(out, BF)] * 2
        + [shape_of((8, columns), F32)],
        scratch_shapes=[pltpu.VMEM((WIDTHS, BLOCK, length), F32)] * 2,
        name="attend_backward",
    )(jnp.full((1,), core, jnp.int32), x_t, wo_g, q, k, v, p, g, *given)


def input_kernel(some, first_g, dq_a, dk_a, dv_a, dq_b, dk_b, dv_b, wq, wk, wv, *refs):
    out = refs[-1]
    w = pl.program_id(0)
    split = dq_a.shape[2]
    for section in some:
        kept = -(-(section + 1) * 3 * HEAD_DIM // BLOCK) * BLOCK

        @pl.when(w == section - some[0])
        def _():
            total = first_g[0]
            for low, high, weight in ((dq_a, dq_b, wq), (dk_a, dk_b, wk), (dv_a, dv_b, wv)):
                near = min(kept, split)
                total += matmul_last(low[0, :, :near], weight[:, :near])
                if kept > split:
                    total += matmul_last(high[0, :, : kept - split], weight[:, split:kept])
            out[0] = total


def input_grads(some, first_g, low, high, query_key, value_output, earlier):
    _, length, width = first_g.shape
    base = some[0]
    per_width = pl.BlockSpec((1, length, width), lambda w: (w + base, 0, 0))
    part = pl.BlockSpec((1, length, low[0].shape[2]), lambda w: (w + base, 0, 0))
    last = pl.BlockSpec((1, length, high[0].shape[2]), lambda w: (jnp.maximum(w + base, WIDTHS // 2), 0, 0))
    given = [] if earlier is None else [earlier]

    def weight(n):
        return pl.BlockSpec((width, width), lambda w: (0, n))

    return call(
        functools.partial(input_kernel, some),
        LIMIT,
        8,
        grid=(len(some),),
        in_specs=[per_width] + [part] * 3 + [last] * 3 + [weight(0), weight(1), weight(0)] + [ANY] * len(given),
        out_specs=per_width,
        out_shape=shape_of(first_g.shape, F32),
        input_output_aliases={10: 0} if given else {},
        name="input_grads",
    )(first_g, *low, *high, query_key, query_key, value_output, *given)


def tie(*values):
    return lax.optimization_barrier(values)


class Ring:
    def __init__(self, mesh):
        self.dp = mesh.shape["dp"]
        self.fsdp = mesh.shape["fsdp"]
        self.square = self.fsdp == 8 and self.dp == 4
        index = lax.axis_index("fsdp")
        self.z = lax.axis_index("dp")
        self.y, self.x, self.c = index // 4, (index // 2) % 2, index % 2

    def swap(self, value, bit):
        total = self.dp * self.fsdp
        return lax.ppermute(value, AXES, [(i, i ^ bit) for i in range(total)])

    def shift(self, value, by):
        total = self.dp * self.fsdp
        return lax.ppermute(value, AXES, [(i, (i + by * self.fsdp) % total) for i in range(total)])

    def along(self, value, bit):
        total = self.dp * self.fsdp
        return lax.ppermute(value, AXES, [(i, i ^ (bit * self.fsdp)) for i in range(total)])

    def mine(self, first, second):
        return jnp.where(self.c == 0, first, second)


CORE, X_SIDE, Y_SIDE = 1, 2, 4


class Gather:
    def __init__(self, ring, halves):
        self.ring, self.halves = ring, halves
        self.shard = halves
        self.line = self.came = self.sides = self.corners = self.crossed = ()

    def start_core(self):
        ring = self.ring
        if ring.square:
            kept, sent = ring.mine(*self.halves), ring.mine(*self.halves[::-1])
            came = ring.swap(sent, CORE)
            self.shard = ring.mine(jnp.concatenate([kept, came], axis=0), jnp.concatenate([came, kept], axis=0))

    def start_line(self, first=0, columns=None):
        ring = self.ring
        if ring.square:
            part = self.shard[:, first : self.shard.shape[1] if columns is None else first + columns]
            self.came += (tuple(ring.shift(part, by) for by in range(1, ring.dp)),)

    def ready_line(self):
        if self.ring.square:
            came = [jnp.concatenate(parts, axis=1) for parts in zip(*self.came)]
            self.line = jnp.stack([self.shard] + came)

    def start_sides(self):
        ring = self.ring
        if ring.square:
            self.sides = (ring.swap(self.line, X_SIDE), ring.swap(self.line, Y_SIDE))

    def start_corners(self):
        ring, half = self.ring, self.ring.dp // 2
        if ring.square:
            self.corners = (
                ring.swap(self.sides[0][:half], Y_SIDE),
                ring.swap(self.sides[1][half:], X_SIDE),
            )

    def cross(self, *values):
        if self.ring.square:
            self.crossed += tuple(self.ring.swap(value, CORE) for value in values)

    def pieces(self):
        ring, half = self.ring, self.ring.dp // 2
        own = (
            (self.line, 0, ring.y, ring.x),
            (self.sides[0], 0, ring.y, 1 - ring.x),
            (self.sides[1], 0, 1 - ring.y, ring.x),
            (self.corners[0], 0, 1 - ring.y, 1 - ring.x),
            (self.corners[1], half, 1 - ring.y, 1 - ring.x),
        )
        rows = self.shard.shape[0]
        copies, at = [], []
        for n, (value, behind, y, x) in enumerate(own):
            for index in range(value.shape[0]):
                z = (ring.z + ring.dp - behind - index) % ring.dp
                copies.append((n, index))
                at.append(jnp.asarray(rows * ((z * 2 + y) * 2 + x), jnp.int32))
        arrays = [value for value, *_ in own] + list(self.crossed)
        return arrays, copies, jnp.stack(at + [jnp.asarray(ring.c, jnp.int32)])

    def source(self):
        return Source(self)


class PlaneFirst(Gather):
    def start_plane(self):
        ring = self.ring
        if ring.square:
            row = jnp.stack([self.shard, ring.swap(self.shard, X_SIDE)])
            self.sides = (row, ring.swap(row, Y_SIDE))

    def ready_line(self):
        if self.ring.square:
            self.line = jnp.concatenate(self.sides)

    def start_line(self):
        ring = self.ring
        if ring.square:
            self.came = tuple(ring.shift(self.line, by) for by in range(1, ring.dp))

    def pieces(self):
        ring = self.ring
        rows = self.shard.shape[0]
        copies, at = [], []
        for behind in range(ring.dp):
            z = (ring.z + ring.dp - behind) % ring.dp
            for index, (y, x) in enumerate(
                ((ring.y, ring.x), (ring.y, 1 - ring.x), (1 - ring.y, ring.x), (1 - ring.y, 1 - ring.x))
            ):
                copies.append((behind, index))
                at.append(jnp.asarray(rows * ((z * 2 + y) * 2 + x), jnp.int32))
        arrays = [self.line, *self.came, *self.crossed]
        return arrays, copies, jnp.stack(at + [jnp.asarray(ring.c, jnp.int32)])


class Source:
    def __init__(self, gather):
        ring = gather.ring
        self.square = ring.square
        self.columns = gather.halves[0].shape[1]
        if ring.square:
            self.rows = gather.shard.shape[0]
            self.arrays, self.copies, self.table = gather.pieces()
        else:
            self.rows = gather.halves[0].shape[0] * ring.dp * ring.fsdp
            self.arrays = [lax.all_gather(half, AXES, axis=0, tiled=True) for half in gather.halves]
            self.copies = []
            self.table = jnp.asarray(ring.c, jnp.int32).reshape(1)
        self.core = len(self.copies)

    def start(self, table, pieces, target, sems, first, columns, to):
        apart = target.shape[1] // 2
        if not self.square:
            for half in range(2):
                pltpu.make_async_copy(
                    pieces[half].at[:, pl.ds(first, columns)],
                    target.at[:, pl.ds(half * apart + to, columns)],
                    sems.at[half],
                ).start()
            return
        core = table[self.core]
        many = len(pieces) // 2
        for side in range(2):
            half = core if side == 0 else 1 - core
            for n, (piece, index) in enumerate(self.copies):
                row = pl.multiple_of(table[n], 16)
                pltpu.make_async_copy(
                    pieces[side * many + piece].at[index, :, pl.ds(first, columns)],
                    target.at[pl.ds(row, self.rows), pl.ds(pl.multiple_of(half * apart + to, BLOCK), columns)],
                    sems.at[half],
                ).start()

    def wait(self, target, sems, columns, to):
        for half in range(2):
            whole_half = target.at[:, pl.ds(half * (target.shape[1] // 2) + to, columns)]
            pltpu.make_async_copy(whole_half, whole_half, sems.at[half]).wait()


def place_rows(source, layout, beside):
    count = len(source.arrays)
    rows = source.rows * max(len(source.copies), 1)

    def kernel(table, *refs):
        pieces, outs = refs[:count], refs[count : count + len(layout)]
        sem = refs[-1]
        if not source.square:
            copies = [
                pltpu.make_async_copy(pieces[half].at[:, pl.ds(first, columns)], outs[n], sem.at[0])
                for n, (half, first, columns) in enumerate(layout)
            ]
            for copy in copies:
                copy.start()
            for copy in copies:
                copy.wait()
            return
        many = count // 2
        core = table[source.core]
        parts = [(half, first, columns, outs[n], 0) for n, (half, first, columns) in enumerate(layout)]
        if beside is not None:
            vec, bi, block = refs[count + len(layout) : -1]
            parts.insert(0, (0, beside, BLOCK, block, 1))

        def run(own):
            copies = []
            for half, first, columns, out, which in parts:
                for m, (piece, index) in enumerate(source.copies):
                    row = pl.multiple_of(table[m], 16)
                    copies.append(
                        (
                            which,
                            pltpu.make_async_copy(
                                pieces[piece + (0 if half == own else many)].at[index, :, pl.ds(first, columns)],
                                out.at[pl.ds(row, source.rows), :],
                                sem.at[which],
                            ),
                        )
                    )
            for _, copy in copies:
                copy.start()
            for which, copy in copies:
                if which == 1:
                    copy.wait()
            if beside is not None:
                vector_columns(block, vec, bi)
            for which, copy in copies:
                if which == 0:
                    copy.wait()

        for own in range(2):
            pl.when(core == own)(functools.partial(run, own))

    more = ([], [], [])
    if beside is not None:
        more = (
            [pl.BlockSpec(memory_space=pltpu.VMEM)] * 2,
            [shape_of((8, rows), F32), shape_of((WIDTHS, rows), F32)],
            [pltpu.VMEM((rows, BLOCK), BF)],
        )
    return call(
        kernel,
        LIMIT_PLACE,
        5,
        in_specs=[SCALARS] + [ANY] * count,
        out_specs=[pl.BlockSpec(memory_space=pltpu.VMEM)] * len(layout) + more[0],
        out_shape=[shape_of((rows, columns), BF) for *_, columns in layout] + more[1],
        scratch_shapes=more[2] + [pltpu.SemaphoreType.DMA((2,))],
        name="place_rows",
    )(source.table, *source.arrays)


def vector_columns(block, vec, bi):
    full = block[...].astype(F32)
    width = full.shape[0]
    vec[...] = full.T[:8, :]
    each = 8
    own = width // (each * WIDTHS)
    lane = lax.broadcasted_iota(jnp.int32, (own, BLOCK), 1)
    pieces = []
    for n in range(each):
        for m in range(WIDTHS):
            piece = jnp.zeros((own, BLOCK), F32)
            for j in range(WIDTHS):
                start = (j * each + n) * own
                piece = jnp.where(lane == 16 + WIDTHS * j + m, full[start : start + own, :], piece)
            pieces.append(piece)
    turned = jnp.concatenate(pieces, axis=0).T
    for j in range(WIDTHS):
        at = 16 + WIDTHS * j
        bi[j : j + 1, :] = jnp.sum(turned[at : at + WIDTHS, :], axis=0, keepdims=True)


class Scatter:
    def __init__(self, ring, mine, other):
        self.ring, self.kept, self.other = ring, mine, other
        self.came = self.sides = self.leaving = self.far = self.near = self.own = ()

    def start_core(self):
        if self.ring.square:
            self.came = self.ring.swap(self.other, CORE)

    def block(self, y, x):
        dp = self.ring.dp

        def pick(value):
            value = value.reshape(dp, 2, 2, value.shape[0] // (4 * dp), value.shape[1])
            value = lax.dynamic_index_in_dim(value, y, 1, keepdims=False)
            return lax.dynamic_index_in_dim(value, x, 1, keepdims=False)

        return pick(self.kept).astype(F32) + pick(self.came).astype(F32)

    def ready_sides(self):
        ring = self.ring
        if ring.square:
            to_x = self.block(ring.y, 1 - ring.x).astype(BF)
            to_y = self.block(1 - ring.y, ring.x).astype(BF)
            corner = self.block(1 - ring.y, 1 - ring.x).astype(BF)
            self.leaving = (corner, to_x, to_y)

    def start_sides(self):
        ring = self.ring
        if ring.square:
            corner, to_x, to_y = self.leaving
            self.sides = (ring.swap(corner, X_SIDE | Y_SIDE), ring.swap(to_x, X_SIDE), ring.swap(to_y, Y_SIDE))

    def ready_far(self):
        ring = self.ring
        if ring.square:
            line = self.block(ring.y, ring.x)
            for side in self.sides:
                line = line + side.astype(F32)
            line = line.reshape(2, 2, *line.shape[1:])
            self.leaving = lax.dynamic_index_in_dim(line, 1 - ring.z // 2, 0, keepdims=False).astype(BF)
            self.own = lax.dynamic_index_in_dim(line, ring.z // 2, 0, keepdims=False)

    def start_far(self):
        if self.ring.square:
            self.far = self.ring.along(self.leaving, 2)

    def ready_near(self):
        ring = self.ring
        if ring.square:
            pair = self.own + self.far.astype(F32)
            self.leaving = lax.dynamic_index_in_dim(pair, 1 - ring.z % 2, 0, keepdims=False).astype(BF)
            self.own = lax.dynamic_index_in_dim(pair, ring.z % 2, 0, keepdims=False)

    def start_near(self):
        if self.ring.square:
            self.near = (self.ring.along(self.leaving, 1),)

    def ready_last(self):
        ring = self.ring
        if ring.square:
            line = self.block(ring.y, ring.x)
            for side in self.sides:
                line = line + side.astype(F32)
            low = line.astype(BF)
            self.own = lax.dynamic_index_in_dim(line, ring.z, 0, keepdims=False)
            self.leaving = tuple(
                lax.dynamic_index_in_dim(low, (ring.z + by) % ring.dp, 0, keepdims=False) for by in range(1, ring.dp)
            )

    def start_last(self):
        ring = self.ring
        if ring.square:
            self.near = tuple(ring.shift(value, by) for by, value in enumerate(self.leaving, 1))


def finish(ring, groups):
    if not ring.square:
        halves = (
            jnp.concatenate([ring.mine(group.kept, group.other) for group in groups], axis=1),
            jnp.concatenate([ring.mine(group.other, group.kept) for group in groups], axis=1),
        )
        return tuple(lax.psum_scatter(half.astype(F32), AXES, scatter_dimension=0, tiled=True) for half in halves)
    total = jnp.concatenate(
        [functools.reduce(lambda sum_, part: sum_ + part.astype(F32), group.near, group.own) for group in groups], axis=1
    )
    rows = total.shape[0] // 2
    kept, sent = ring.mine(total[:rows], total[rows:]), ring.mine(total[rows:], total[:rows])
    came = ring.swap(sent, CORE)
    return ring.mine(kept, came), ring.mine(came, kept)


def solution(mesh):
    rows_split = P(AXES, None)
    vector_split = P(AXES)

    def per_device(
        tokens,
        segment_ids,
        output_grad,
        query_weight,
        query_bias,
        key_weight,
        value_weight,
        value_bias,
        output_weight,
        output_bias,
        first_gain,
        first_shift,
        inner_weight,
        inner_bias,
        outer_weight,
        outer_bias,
        second_gain,
        second_shift,
    ):
        ring = Ring(mesh)
        devices = ring.dp * ring.fsdp
        width = tokens.shape[1]
        hidden = inner_weight.shape[1]
        own = query_bias.shape[0]
        half = hidden // 2
        singles = (query_bias, value_bias, output_bias, first_gain, first_shift, outer_bias, second_gain, second_shift)
        count = len(singles)
        beside = ring.square and own % 8 == 0
        columns = []
        if beside:
            row = lax.broadcasted_iota(jnp.int32, (BLOCK, own), 0)
            block = jnp.zeros((BLOCK, own), BF)
            for n, vector in enumerate(singles):
                block = jnp.where(row == n, vector[None], block)
            chunk = (ring.z * ring.fsdp + lax.axis_index("fsdp")) // (devices // WIDTHS)
            for n in range(WIDTHS):
                quarter = inner_bias[n * own : (n + 1) * own]
                block = jnp.where(row == 16 + WIDTHS * chunk + n, quarter[None], block)
            columns = [block.T]

        def side(*parts):
            return jnp.concatenate(parts, axis=1)

        one = Gather(ring, (side(query_weight, key_weight, *columns), side(value_weight, output_weight, *columns)))
        two = Gather(ring, (inner_weight, outer_weight))
        pair = 2 * width
        one.start_core()
        one.shard, two.halves = tie(one.shard, two.halves)
        one.start_line()
        two.start_core()
        one.came, two.shard = tie(one.came, two.shard)
        one.ready_line()
        one.start_sides()
        two.start_line(0, half)
        one.line, one.sides, two.came = tie(one.line, one.sides, two.came)
        one.start_corners()
        two.start_line(half, half)
        one.line, one.sides, one.corners, two.came = tie(one.line, one.sides, one.corners, two.came)
        one.cross(one.line, *one.sides, *one.corners)
        two.ready_line()
        two.start_sides()
        source_one = one.source()
        query_key, value_output, *vectors = place_rows(source_one, ((0, 0, pair), (1, 0, pair)), pair if beside else None)
        if beside:
            vec, bi = vectors
            bi = bi.reshape(WIDTHS, 1, width)
        else:
            vec = jnp.stack([lax.all_gather(entry, AXES, tiled=True) for entry in singles]).astype(F32)
            bi = lax.all_gather(inner_bias, AXES, tiled=True).astype(F32).reshape(WIDTHS, 1, width)
        q, k, v, att, p = attend(tokens, query_key, value_output, vec, segment_ids[0])
        att, two.line, two.sides = tie(att, two.line, two.sides)
        two.start_corners()
        two.cross(two.line, *two.sides)
        hat, scale, normed, normed_t, second, x_t = first_norm(tokens, att, value_output, vec)
        normed, two.corners, two.crossed = tie(normed, two.corners, two.crossed)
        two.cross(*two.corners)
        source_two = two.source()

        act, slope, act_1, slope_1, out, feed, feed_t, mine, other, grad, bias_hi, sums_b = feed_high(
            source_two, normed, bi, second, output_grad, vec, normed_t
        )
        high = Scatter(ring, mine, other)
        high.start_core()
        grad, high.came = tie(grad, high.came)
        high.ready_sides()
        grad, high.leaving = tie(grad, high.leaving)
        high.start_sides()
        act, slope, out, feed, feed_t, mine, other, grad, bias_1, sums_b2 = feed_mid(
            source_two, normed, bi, second, output_grad, vec, normed_t, act_1, slope_1, grad, act, slope, out, feed, feed_t
        )
        grad, other, high.sides = tie(grad, other, high.sides)

        mid = Scatter(ring, mine, other)
        mid.start_core()
        high.ready_far()
        mid.ready_sides()
        grad, mid.leaving, high.leaving = tie(grad, mid.leaving, high.leaving)
        mid.start_sides()
        high.start_far()
        mine, other, first_g, att_g, wo_g, bias_0, sums_a = feed_zero(
            source_two, vec, feed, feed_t, normed_t, act, slope, grad, hat, scale, att, value_output
        )
        att_g, other, mid.sides, high.far = tie(att_g, other, mid.sides, high.far)

        low = Scatter(ring, mine, other)
        low.start_core()
        high.ready_near()
        mid.ready_far()
        low.ready_sides()
        att_g, low.leaving, mid.leaving, high.leaving = tie(att_g, low.leaving, mid.leaving, high.leaving)
        low.start_sides()
        mid.start_far()
        high.start_near()
        pairs = HEADS // 4
        *low_g, mine, other, sums_c = attend_backward(ring.c, 0, pairs, own, x_t, wo_g, q, k, v, p, att_g, ())
        att_g, other, low.sides, mid.far, high.near = tie(att_g, other, low.sides, mid.far, high.near)

        left = Scatter(ring, mine, other)
        left.start_core()
        mid.ready_near()
        low.ready_far()
        left.ready_sides()
        att_g, left.leaving, low.leaving, mid.leaving = tie(att_g, left.leaving, low.leaving, mid.leaving)
        left.start_sides()
        low.start_far()
        mid.start_near()
        given = (sums_c, sums_a, sums_b, sums_b2, bias_0, bias_1, bias_hi) if beside else ()
        *high_g, mine, other, sums_d = attend_backward(
            ring.c, pairs, pairs, own, x_t, wo_g, q, k, v, p, att_g, given
        )
        first_g, other, left.sides, low.far, mid.near = tie(first_g, other, left.sides, low.far, mid.near)

        right = Scatter(ring, mine, other)
        right.start_core()
        low.ready_near()
        left.ready_far()
        right.ready_sides()
        first_g, right.leaving, left.leaving, low.leaving = tie(first_g, right.leaving, left.leaving, low.leaving)
        right.start_sides()
        left.start_far()
        low.start_near()
        in_g = input_grads(tuple(range(WIDTHS)), first_g, low_g, high_g, query_key, value_output, None)
        in_g, right.sides, left.far, low.near = tie(in_g, right.sides, left.far, low.near)

        left.ready_near()
        right.ready_last()
        right.leaving, left.leaving = tie(right.leaving, left.leaving)
        right.start_last()
        left.start_near()
        outer_g, inner_g = finish(ring, (low, mid, high))
        right.near, left.near, outer_g = tie(right.near, left.near, outer_g)
        first_half, second_half = finish(ring, (left, right))
        split = pairs * BLOCK
        parts = [
            side(entry[:, at : at + split], entry[:, at + 2 * split : at + 3 * split])
            for entry in (first_half, second_half)
            for at in (0, split)
        ]
        wq_g, wk_g, wv_g, wo_g = parts
        if beside:
            last = first_half[:, 4 * split :]
            bias_g = last[:, 16 : 16 + WIDTHS * WIDTHS].reshape(own, WIDTHS, WIDTHS).sum(axis=1)
            vectors_g = [last[:, n] for n in range(count)] + [bias_g.T.reshape(own * WIDTHS)]
        else:
            attention_sums = jnp.concatenate([sums_c[:2], sums_d[:2]], axis=1)
            sums_b = sums_b + sums_b2
            rows = [*attention_sums, sums_a[2], sums_a[0], sums_a[1], sums_b[2], sums_b[0], sums_b[1]]
            rows.append(jnp.concatenate([bias_0, bias_1, bias_hi], axis=0).reshape(hidden))
            vectors_g = [lax.psum_scatter(entry, AXES, scatter_dimension=0, tiled=True) for entry in rows]
        bq_g, bv_g, bo_g, ga_g, sa_g, bu_g, gb_g, sb_g, bi_g = vectors_g
        return (
            out, in_g, wq_g, bq_g, wk_g, wv_g, bv_g, wo_g, bo_g, ga_g, sa_g, inner_g, bi_g, outer_g, bu_g, gb_g, sb_g,
        )

    layered = P(None, AXES, None)
    return jax.shard_map(
        per_device,
        mesh=mesh,
        in_specs=(
            rows_split, rows_split, layered, rows_split, vector_split, rows_split, rows_split, vector_split,
            rows_split, vector_split, vector_split, vector_split, rows_split, vector_split, rows_split,
            vector_split, vector_split, vector_split,
        ),
        out_specs=(
            layered, layered, rows_split, vector_split, rows_split, rows_split, vector_split, rows_split,
            vector_split, vector_split, vector_split, rows_split, vector_split, rows_split, vector_split,
            vector_split, vector_split,
        ),
        check_vma=False,
    )
```

```python
import functools
import math

import jax
import jax.numpy as jnp
from jax import lax
from jax.experimental import pallas as pl
from jax.experimental.pallas import tpu as pltpu
from jax.sharding import PartitionSpec as P

HEADS = 12
HEAD_DIM = 64
WIDTHS = 4
BLOCK = 128
AXES = ("dp", "fsdp")
BF = jnp.bfloat16
F32 = jnp.float32
MIB = 1024 * 1024
LIMIT = 60
LIMIT_PLACE = 60
LIMIT_ATTEND = 60
BYTES = 3.3e6


def matmul(left_side, right_side):
    return lax.dot_general(
        left_side, right_side, (((1,), (0,)), ((), ())), preferred_element_type=F32
    )


def matmul_last(left_side, right_side):
    return lax.dot_general(
        left_side, right_side, (((1,), (1,)), ((), ())), preferred_element_type=F32
    )


def windows(length):
    count = length // BLOCK
    spans = []
    for i in range(count):
        start = max(0, i - 1) * BLOCK
        spans.append((start, min(count, i + 2) * BLOCK - start))
    return spans


def call(kernel, limit, micros, **options):
    return pl.pallas_call(
        kernel,
        compiler_params=pltpu.CompilerParams(vmem_limit_bytes=limit * MIB),
        cost_estimate=pl.CostEstimate(flops=0, bytes_accessed=int(micros * BYTES), transcendentals=0),
        **options,
    )


def shape_of(shape, dtype):
    return jax.ShapeDtypeStruct(shape, dtype)


def whole(shape):
    return pl.BlockSpec(shape, lambda *_: (0,) * len(shape))


def attend_kernel(x, wq, wk, wv, vec, seg_col, seg_row, q_o, k_o, v_o, a_o, p_o, bias):
    spans = windows(x.shape[0])

    @pl.when(pl.program_id(0) == 0)
    def _():
        for i, (start, span) in enumerate(spans):
            same = seg_col[i * BLOCK : (i + 1) * BLOCK, :] == seg_row[:, start : start + span]
            bias[i, :, :span] = jnp.where(same, 0.0, -1e30)

    rows = x[...]
    q_o[...] = (matmul(rows, wq[...]) + vec[0:1, :]).astype(BF)
    k_o[...] = matmul(rows, wk[...]).astype(BF)
    v_o[...] = (matmul(rows, wv[...]) + vec[1:2, :]).astype(BF)
    lane = lax.broadcasted_iota(jnp.int32, (BLOCK, BLOCK), 1)
    low_half = lane < HEAD_DIM
    factor = 1.0 / math.sqrt(HEAD_DIM)
    mask = jnp.concatenate(
        [jnp.where(low_half, factor, 0.0).astype(BF), jnp.where(low_half, 0.0, factor).astype(BF)], axis=0
    )
    for pair in range(q_o.shape[1] // BLOCK):
        cols = slice(pair * BLOCK, (pair + 1) * BLOCK)
        scores = []
        for i, (start, span) in enumerate(spans):
            q_here = q_o[i * BLOCK : (i + 1) * BLOCK, cols]
            both = jnp.concatenate([q_here, q_here], axis=0) * mask
            scores.append(matmul_last(both, k_o[start : start + span, cols]))
        chances = []
        for i, (start, span) in enumerate(spans):
            blocked = bias[i, :, :span]
            score = scores[i] + jnp.concatenate([blocked, blocked], axis=0)
            shifted = jnp.exp(score - jnp.max(score, axis=1, keepdims=True))
            total = jnp.sum(shifted, axis=1, keepdims=True)
            chances.append((shifted * (1.0 / total)).astype(BF))
        for i, (start, span) in enumerate(spans):
            mixed = matmul(chances[i], v_o[start : start + span, cols])
            here = slice(i * BLOCK, (i + 1) * BLOCK)
            a_o[here, cols] = jnp.where(low_half, mixed[:BLOCK], mixed[BLOCK:]).astype(BF)
            p_o[2 * pair, i, :, :span] = chances[i][:BLOCK]
            p_o[2 * pair + 1, i, :, :span] = chances[i][BLOCK:]


def attend(x, query_key, value_output, vec, segments):
    length, width = x.shape
    step = 256
    steps = width // step
    count = length // BLOCK
    part = pl.BlockSpec((length, step), lambda p: (0, p))
    heads = step // HEAD_DIM

    def weight(n):
        return pl.BlockSpec((width, step), lambda p: (0, n * steps + p))

    return call(
        attend_kernel,
        LIMIT_ATTEND,
        9.5,
        grid=(steps,),
        in_specs=[
            whole(x.shape),
            weight(0),
            weight(1),
            weight(0),
            pl.BlockSpec((vec.shape[0], step), lambda p: (0, p)),
            whole((length, 1)),
            whole((1, length)),
        ],
        out_specs=[part, part, part, part, pl.BlockSpec((heads, count, BLOCK, 3 * BLOCK), lambda p: (p, 0, 0, 0))],
        out_shape=[shape_of((length, width), BF)] * 4 + [shape_of((HEADS, count, BLOCK, 3 * BLOCK), BF)],
        scratch_shapes=[pltpu.VMEM((count, BLOCK, 3 * BLOCK), F32)],
        name="attend",
    )(x, query_key, query_key, value_output, vec, segments.reshape(length, 1), segments.reshape(1, length))


def norm_parts(values):
    center = values - jnp.mean(values, axis=1, keepdims=True)
    scale = lax.rsqrt(jnp.mean(center * center, axis=1, keepdims=True) + 1e-12)
    return center * scale, scale


def norm_back(spread_grad, hat, scale):
    return scale * (
        spread_grad
        - jnp.mean(spread_grad, axis=1, keepdims=True)
        - hat * jnp.mean(spread_grad * hat, axis=1, keepdims=True)
    )


def chunk_mask(w, rows):
    lane = lax.broadcasted_iota(jnp.int32, (rows, 2 * BLOCK), 1)
    start = HEAD_DIM * (w % 2)
    return (lane >= start) & (lane < start + 3 * HEAD_DIM)


def window_at(w):
    return w + w // 2


def first_kernel(x, att_a, att_b, wo_a, wo_b, vec, hat_o, scale_o, normed_o, normed_t_o, second_o, x_t_o, branch):
    w = pl.program_id(0)

    @pl.when(w == 0)
    def _():
        branch[...] = x[...].astype(F32) + vec[2:3, :]
        x_t_o[...] = x[...].T

    kept = jnp.where(chunk_mask(w, x.shape[0]), jnp.concatenate([att_a[...], att_b[...]], axis=1).astype(F32), 0.0)
    weight = jnp.concatenate([wo_a[...], wo_b[...]], axis=1)
    first = branch[...] + matmul_last(kept.astype(BF), weight)
    branch[...] = first
    hat, scale = norm_parts(first)
    hat_o[0] = hat.astype(BF)
    scale_o[0] = scale
    normed = hat * vec[3:4, :] + vec[4:5, :]
    second_o[0] = normed + vec[5:6, :]
    low = normed.astype(BF)
    normed_o[0] = low
    normed_t_o[0] = low.T


def first_norm(x, att, weights, vec):
    length, width = x.shape
    base = width // BLOCK
    per_width = pl.BlockSpec((1, length, width), lambda w: (w, 0, 0))
    return call(
        first_kernel,
        LIMIT,
        9.7,
        grid=(WIDTHS,),
        in_specs=[
            whole(x.shape),
            pl.BlockSpec((length, BLOCK), lambda w: (0, window_at(w))),
            pl.BlockSpec((length, BLOCK), lambda w: (0, window_at(w) + 1)),
            pl.BlockSpec((width, BLOCK), lambda w: (0, base + window_at(w))),
            pl.BlockSpec((width, BLOCK), lambda w: (0, base + window_at(w) + 1)),
            whole(vec.shape),
        ],
        out_specs=[
            per_width,
            pl.BlockSpec((1, length, 1), lambda w: (w, 0, 0)),
            per_width,
            pl.BlockSpec((1, width, length), lambda w: (w, 0, 0)),
            per_width,
            whole((width, length)),
        ],
        out_shape=[
            shape_of((WIDTHS, length, width), BF),
            shape_of((WIDTHS, length, 1), F32),
            shape_of((WIDTHS, length, width), BF),
            shape_of((WIDTHS, width, length), BF),
            shape_of((WIDTHS, length, width), F32),
            shape_of((width, length), BF),
        ],
        scratch_shapes=[pltpu.VMEM((length, width), F32)],
        name="first_norm",
    )(x, att, att, weights, weights, vec)


ERF_T = 0.3275911 / math.sqrt(2.0)
BELL = 1.0 / math.sqrt(2.0 * math.pi)
ERF_A = tuple(
    0.5 * entry / BELL for entry in (0.254829592, -0.284496736, 1.421413741, -1.453152027, 1.061405429)
)
ROWS = 256


def gelu_pair(values):
    size = jnp.abs(values)
    bell = jnp.exp2(values * values * (-0.5 * math.log2(math.e)) + math.log2(BELL))
    below = 1.0 + ERF_T * size
    t = pl.reciprocal(below, approx=True)
    t = t * (2.0 - below * t)
    poly = ERF_A[4] * t + ERF_A[3]
    for entry in (ERF_A[2], ERF_A[1], ERF_A[0]):
        poly = poly * t + entry
    tail = poly * t * bell
    step = tail - size * bell
    return jnp.maximum(values, 0.0) - size * tail, jnp.where(values >= 0.0, 1.0 - step, step)


def feed_order(chunks):
    return [(j, w) for j in chunks for w in range(j, WIDTHS)]


def copy_of(source, target, sem):
    return pltpu.make_async_copy(source, target, sem)


def forward_step(normed, weights, bias, act, slope, second, column):
    length, width = normed.shape
    half = weights.shape[1] // 2
    for r in range(0, length, ROWS):
        rows = slice(r, r + ROWS)
        inner = matmul(normed[rows, :], weights[:, pl.ds(column, width)]) + bias
        active, tilt = gelu_pair(inner)
        active = active.astype(BF)
        act[rows, :] = active
        slope[rows, :] = tilt.astype(BF)
        second[rows, :] += matmul_last(active, weights[:, pl.ds(half + column, width)])


def second_norm(second, og, vec, out, feed, feed_t, sums):
    hat, scale = norm_parts(second[...])
    out[...] = (hat * vec[6:7, :] + vec[7:8, :]).astype(BF)
    grad = og[...].astype(F32)
    sums[0:1, :] += jnp.sum(grad * hat, axis=0, keepdims=True)
    sums[1:2, :] += jnp.sum(grad, axis=0, keepdims=True)
    low = norm_back(grad * vec[6:7, :], hat, scale).astype(BF)
    feed[...] = low
    feed_t[...] = low.T
    sums[2:3, :] += jnp.sum(low.astype(F32), axis=0, keepdims=True)


def backward_step(feed, feed_t, normed_t, act, slope, weights, column, outer, inner, grads, bias, fresh, ready=None):
    length, width = feed.shape
    half = weights.shape[1] // 2
    part = matmul(feed_t[...], act[...])
    outer[...] = part if fresh else outer[...] + part
    if ready is not None:
        ready()
    lows = []
    for r in range(0, length, ROWS):
        rows = slice(r, r + ROWS)
        raw = matmul(feed[rows, :], weights[:, pl.ds(half + column, width)])
        low = (slope[rows, :].astype(F32) * raw).astype(BF)
        bias[...] += jnp.sum(low.astype(F32), axis=0, keepdims=True)
        grads[rows, :] += matmul_last(low, weights[:, pl.ds(column, width)])
        lows.append(low)
    part = matmul(normed_t[...], jnp.concatenate(lows, axis=0))
    inner[...] = part if fresh else inner[...] + part


ANY = pl.BlockSpec(memory_space=pl.ANY)
SCALARS = pl.BlockSpec(memory_space=pltpu.SMEM)


def held(array):
    return pl.BlockSpec(memory_space=pltpu.VMEM)


def give_halves(core, outer, inner, mine_h, other_h, sem):
    @pl.when(core == 0)
    def _():
        copy_of(outer, mine_h, sem).start()
        copy_of(inner, other_h, sem).start()

    @pl.when(core != 0)
    def _():
        copy_of(inner, mine_h, sem).start()
        copy_of(outer, other_h, sem).start()

    return [copy_of(outer, mine_h, sem), copy_of(inner, other_h, sem)]


def feed_high_kernel(source, table, bi, vec, normed_h, second_h, og_h, normed_t_h, *refs):
    count = len(source.arrays)
    pieces, refs = refs[:count], refs[count:]
    act_h, slope_h, act_1_h, slope_1_h, out_h, feed_h, feed_t_h, mine_h, other_h, grad_h, bias, sums = refs[:12]
    weights, normed, second, og, normed_t, act, slope, feed, feed_t, outer, inner, outer_b, inner_b = refs[12:25]
    sem_w, sem_n, sem_act, sem_out, sem_give = refs[25:]
    width = normed.shape[2]
    low = WIDTHS - 2

    def rows_of(n):
        return (
            copy_of(normed_h.at[low + n], normed.at[n], sem_n.at[0, n]),
            copy_of(second_h.at[low + n], second.at[n], sem_n.at[1, n]),
            copy_of(og_h.at[low + n], og.at[n], sem_n.at[2, n]),
            copy_of(normed_t_h.at[low + n], normed_t.at[n], sem_n.at[3, n]),
        )

    for copy in rows_of(1)[:2]:
        copy.start()
    for j in range(WIDTHS):
        source.start(table, pieces, weights, sem_w.at[j], j * width, width, j * width)
    for copy in rows_of(1)[2:] + rows_of(0):
        copy.start()
    sums[...] = jnp.zeros_like(sums)
    bias[...] = jnp.zeros_like(bias)
    for copy in rows_of(1)[:2]:
        copy.wait()
    writes, given = [], []
    for n in (1, 0):
        w = low + n
        for j in range(w + 1):
            if n == 1 and j < 2:
                source.wait(weights, sem_w.at[j], width, j * width)
            if n == 1 and j == 2:
                for later in (2, 3):
                    source.wait(weights, sem_w.at[later], width, later * width)
                for copy in rows_of(1)[2:] + rows_of(0):
                    copy.wait()
            at = 4 * (1 - n) + j
            forward_step(normed.at[n], weights, bi[j], act.at[at], slope.at[at], second.at[n], j * width)
        base = 4 * (1 - n)
        writes += [
            copy_of(act.at[base], act_h.at[w], sem_act.at[n, 0]),
            copy_of(slope.at[base], slope_h.at[w], sem_act.at[n, 1]),
            copy_of(act.at[base + 1], act_1_h.at[n], sem_act.at[n, 2]),
            copy_of(slope.at[base + 1], slope_1_h.at[n], sem_act.at[n, 3]),
        ]
        for copy in writes[-4:]:
            copy.start()
        second_norm(second.at[n], og.at[n], vec, normed.at[n], feed.at[n], feed_t.at[n], sums)
        for m, copy in enumerate(
            (
                copy_of(normed.at[n], out_h.at[w], sem_out.at[0, n]),
                copy_of(feed.at[n], feed_h.at[w], sem_out.at[1, n]),
                copy_of(feed_t.at[n], feed_t_h.at[w], sem_out.at[2, n]),
            )
        ):
            copy.start()
            writes.append(copy)
        second[n] = feed[n].astype(F32)

        def back(m, carry, n=n, w=w):
            at = (w if m == 1 else 4 + w) if n == 0 else w
            backward_step(
                feed.at[m], feed_t.at[m], normed_t.at[m], act.at[at], slope.at[at], weights, w * width,
                outer, inner, second.at[m], bias.at[n], m == n,
            )
            return carry

        for m in range(n, 2):
            back(m, 0)
        outer_b[n] = outer[...].astype(BF)
        inner_b[n] = inner[...].astype(BF)
        columns = pl.ds(n * width, width)
        given += give_halves(
            table[source.core], outer_b.at[n], inner_b.at[n], mine_h.at[:, columns], other_h.at[:, columns], sem_give.at[n]
        )
    last = copy_of(second, grad_h, sem_out.at[3, 0])
    last.start()
    for copy in writes + given + [last]:
        copy.wait()


def feed_high(source, normed, bi, second, og, vec, normed_t):
    _, length, width = normed.shape
    four, four_t = (WIDTHS, length, width), (WIDTHS, width, length)
    two, two_t = (2, length, width), (2, width, length)
    slots = 7
    return call(
        functools.partial(feed_high_kernel, source),
        LIMIT,
        35,
        in_specs=[SCALARS, held(bi), held(vec)] + [ANY] * (4 + len(source.arrays)),
        out_specs=[ANY] * 10 + [held(vec), held(vec)],
        out_shape=[
            shape_of(four, BF),
            shape_of(four, BF),
            shape_of(two, BF),
            shape_of(two, BF),
            shape_of(four, BF),
            shape_of(four, BF),
            shape_of(four_t, BF),
            shape_of((width, 2 * width), BF),
            shape_of((width, 2 * width), BF),
            shape_of(two, F32),
            shape_of((2, 1, width), F32),
            shape_of((8, width), F32),
        ],
        scratch_shapes=[
            pltpu.VMEM((width, 8 * width), BF),
            pltpu.VMEM(two, BF),
            pltpu.VMEM(two, F32),
            pltpu.VMEM(two, BF),
            pltpu.VMEM(two_t, BF),
            pltpu.VMEM((slots, length, width), BF),
            pltpu.VMEM((slots, length, width), BF),
            pltpu.VMEM(two, BF),
            pltpu.VMEM(two_t, BF),
            pltpu.VMEM((width, width), F32),
            pltpu.VMEM((width, width), F32),
            pltpu.VMEM((2, width, width), BF),
            pltpu.VMEM((2, width, width), BF),
            pltpu.SemaphoreType.DMA((WIDTHS, 2)),
            pltpu.SemaphoreType.DMA((4, 2)),
            pltpu.SemaphoreType.DMA((2, 4)),
            pltpu.SemaphoreType.DMA((4, 2)),
            pltpu.SemaphoreType.DMA((2,)),
        ],
        name="feed_high",
    )(source.table, bi, vec, normed, second, og, normed_t, *source.arrays)


def feed_mid_kernel(source, table, bi, vec, normed_h, second_h, og_h, normed_t_h, act_1_h, slope_1_h, grad_in, feed_in, feed_t_in, *refs):
    count = len(source.arrays)
    pieces, refs = refs[:count], refs[count + 3 :]
    act_h, slope_h, out_h, feed_h, feed_t_h, mine_h, other_h, grad_h, bias, sums = refs[:10]
    weights, normed, second, og, normed_t, act, slope, feed, feed_t, grads, outer, inner, outer_b, inner_b = refs[10:24]
    sem_w, sem_n, sem_b, sem_act, sem_out, sem_give = refs[24:]
    width = normed.shape[2]

    def rows_of(w):
        return (
            copy_of(normed_h.at[w], normed.at[w], sem_n.at[0, w]),
            copy_of(second_h.at[w], second.at[w], sem_n.at[1, w]),
            copy_of(og_h.at[w], og.at[w], sem_n.at[2, w]),
        )

    def back_rows(m):
        return (
            copy_of(feed_t_in.at[2 + m], feed_t.at[2 + m], sem_b.at[0, m]),
            copy_of(act_1_h.at[m], act.at[1 + m], sem_b.at[1, m]),
            copy_of(feed_in.at[2 + m], feed.at[2 + m], sem_b.at[2, m]),
            copy_of(slope_1_h.at[m], slope.at[1 + m], sem_b.at[3, m]),
            copy_of(grad_in.at[m], grads.at[1 + m], sem_b.at[4, m]),
        )

    turned = [copy_of(normed_t_h.at[w], normed_t.at[w - 1], sem_n.at[3, w - 1]) for w in range(1, WIDTHS)]
    for copy in rows_of(1)[:2]:
        copy.start()
    for j in range(2):
        source.start(table, pieces, weights, sem_w.at[j], j * width, width, j * width)
    for copy in rows_of(1)[2:] + rows_of(0) + (turned[0],) + back_rows(0) + (turned[1],) + back_rows(1) + (turned[2],):
        copy.start()
    sums[...] = jnp.zeros_like(sums)
    bias[...] = jnp.zeros_like(bias)
    for copy in rows_of(1)[:2]:
        copy.wait()
    for w in (1, 0):
        for j in range(w + 1):
            if w == 1 and j == 0:
                source.wait(weights, sem_w.at[0], width, 0)
            if w == 1 and j == 1:
                source.wait(weights, sem_w.at[1], width, width)
                for copy in rows_of(1)[2:] + rows_of(0):
                    copy.wait()
            at = 0 if j == 1 else 3 + w
            forward_step(normed.at[w], weights, bi[j], act.at[at], slope.at[at], second.at[w], j * width)
        second_norm(second.at[w], og.at[w], vec, normed.at[w], feed.at[w], feed_t.at[w], sums)
    writes = []
    for w in (1, 0):
        writes += [
            copy_of(act.at[3 + w], act_h.at[w], sem_act.at[0, w]),
            copy_of(slope.at[3 + w], slope_h.at[w], sem_act.at[1, w]),
            copy_of(normed.at[w], out_h.at[w], sem_out.at[0, w]),
            copy_of(feed.at[w], feed_h.at[w], sem_out.at[1, w]),
            copy_of(feed_t.at[w], feed_t_h.at[w], sem_out.at[2, w]),
        ]
    for copy in writes:
        copy.start()
    for copy in turned + [copy for m in range(2) for copy in back_rows(m)]:
        copy.wait()
    grads[0] = feed[1].astype(F32)
    for m in range(WIDTHS - 1):
        backward_step(
            feed.at[1 + m], feed_t.at[1 + m], normed_t.at[m], act.at[m], slope.at[m], weights, width,
            outer, inner, grads.at[m], bias.at[0], m == 0,
        )
        copy_of(grads.at[m], grad_h.at[m], sem_out.at[3, m]).start()
    outer_b[...] = outer[...].astype(BF)
    inner_b[...] = inner[...].astype(BF)
    writes += give_halves(table[source.core], outer_b, inner_b, mine_h, other_h, sem_give)
    writes += [copy_of(grads.at[m], grad_h.at[m], sem_out.at[3, m]) for m in range(WIDTHS - 1)]
    for copy in writes:
        copy.wait()


def feed_mid(source, normed, bi, second, og, vec, normed_t, act_1, slope_1, grad, act, slope, out, feed, feed_t):
    _, length, width = normed.shape
    four, four_t = (WIDTHS, length, width), (WIDTHS, width, length)
    two = (2, length, width)
    many = WIDTHS - 1
    first = 12 + len(source.arrays)
    return call(
        functools.partial(feed_mid_kernel, source),
        LIMIT,
        22,
        in_specs=[SCALARS, held(bi), held(vec)] + [ANY] * (9 + len(source.arrays) + 3),
        out_specs=[ANY] * 8 + [held(vec), held(vec)],
        out_shape=[
            shape_of(four, BF),
            shape_of(four, BF),
            shape_of(four, BF),
            shape_of(four, BF),
            shape_of(four_t, BF),
            shape_of((width, width), BF),
            shape_of((width, width), BF),
            shape_of((many, length, width), F32),
            shape_of((1, 1, width), F32),
            shape_of((8, width), F32),
        ],
        scratch_shapes=[
            pltpu.VMEM((width, 4 * width), BF),
            pltpu.VMEM(two, BF),
            pltpu.VMEM(two, F32),
            pltpu.VMEM(two, BF),
            pltpu.VMEM((many, width, length), BF),
            pltpu.VMEM((5, length, width), BF),
            pltpu.VMEM((5, length, width), BF),
            pltpu.VMEM(four, BF),
            pltpu.VMEM(four_t, BF),
            pltpu.VMEM((many, length, width), F32),
            pltpu.VMEM((width, width), F32),
            pltpu.VMEM((width, width), F32),
            pltpu.VMEM((width, width), BF),
            pltpu.VMEM((width, width), BF),
            pltpu.SemaphoreType.DMA((2, 2)),
            pltpu.SemaphoreType.DMA((4, many)),
            pltpu.SemaphoreType.DMA((5, 2)),
            pltpu.SemaphoreType.DMA((2, 2)),
            pltpu.SemaphoreType.DMA((4, many)),
            pltpu.SemaphoreType.DMA,
        ],
        input_output_aliases={10: 3, 11: 4, first: 0, first + 1: 1, first + 2: 2},
        name="feed_mid",
    )(source.table, bi, vec, normed, second, og, normed_t, act_1, slope_1, grad, feed, feed_t, *source.arrays, act, slope, out)


def feed_zero_kernel(source, table, vec, feed_h, feed_t_h, normed_t_h, act_h, slope_h, grad_in, hat_h, scale_h, att_h, wo_h, *refs):
    count = len(source.arrays)
    pieces, refs = refs[:count], refs[count:]
    mine_h, other_h, first_g_h, att_g_h, wo_g_h, bias, sums = refs[:7]
    weights, feed, feed_t, normed_t, act, slope, outer, inner, grads, outer_b, inner_b = refs[7:18]
    hat, scale, att, wo, att_g, total, wo_g, wo_g_b = refs[18:26]
    sem_w, sem_in, sem_g, sem_x, sem_out = refs[26:]
    length, width = feed.shape[1:]
    def reads(w):
        return (
            copy_of(feed_t_h.at[w], feed_t.at[w], sem_in.at[0, w]),
            copy_of(act_h.at[w], act.at[w], sem_in.at[1, w]),
            copy_of(feed_h.at[w], feed.at[w], sem_in.at[2, w]),
            copy_of(slope_h.at[w], slope.at[w], sem_in.at[3, w]),
            copy_of(normed_t_h.at[w], normed_t.at[w], sem_in.at[4, w]),
            copy_of(hat_h.at[w], hat.at[w], sem_in.at[5, w]),
            copy_of(scale_h.at[w], scale.at[w], sem_in.at[6, w]),
        )

    for w in reversed(range(WIDTHS)):
        for copy in reads(w)[:5]:
            copy.start()
        if w == WIDTHS - 1:
            source.start(table, pieces, weights, sem_w, 0, width, 0)
        if w > 0:
            copy_of(grad_in.at[w - 1], grads.at[w], sem_g.at[w]).start()
        if w == WIDTHS - 1:
            beside = (copy_of(att_h, att, sem_x.at[0]), copy_of(wo_h.at[:, pl.ds(width, width)], wo, sem_x.at[1]))
            for copy in beside:
                copy.start()
        for copy in reads(w)[5:]:
            copy.start()
    bias[...] = jnp.zeros_like(bias)
    sums[...] = jnp.zeros_like(sums)
    total[...] = jnp.zeros_like(total)
    wo_g[...] = jnp.zeros_like(wo_g)

    for w in reversed(range(WIDTHS)):
        if w == WIDTHS - 1:
            for copy in reads(w)[:2]:
                copy.wait()

        def ready(w=w):
            for copy in reads(w)[2:] + (reads(w - 1)[:2] if w else ()) + (beside if w == WIDTHS - 1 else ()):
                copy.wait()
            if w == WIDTHS - 1:
                source.wait(weights, sem_w, width, 0)
            if w == 0:
                grads[0] = feed[0].astype(F32)
            else:
                copy_of(grad_in.at[w - 1], grads.at[w], sem_g.at[w]).wait()

        backward_step(
            feed.at[w], feed_t.at[w], normed_t.at[w], act.at[w], slope.at[w], weights, 0, outer, inner, grads.at[w],
            bias.at[0], w == WIDTHS - 1, ready,
        )
        rough, factor = hat[w].astype(F32), scale[w]
        grad = grads[w]
        sums[0:1, :] += jnp.sum(grad * rough, axis=0, keepdims=True)
        sums[1:2, :] += jnp.sum(grad, axis=0, keepdims=True)
        first_g = norm_back(grad * vec[3:4, :], rough, factor)
        grads[w] = first_g
        copy_of(grads.at[w], first_g_h.at[w], sem_out.at[0]).start()
        low = first_g.astype(BF)
        wide = low.astype(F32)
        sums[2:3, :] += jnp.sum(wide, axis=0, keepdims=True)
        total[...] += wide
        kept = (w + 1) * 3 * HEAD_DIM
        columns = -(-kept // BLOCK) * BLOCK
        found = matmul(low, wo[:, :columns])
        if columns > kept:
            lane = lax.broadcasted_iota(jnp.int32, (length, columns), 1)
            found = jnp.where(lane < kept, found, 0.0)
        att_g[w, :, :columns] = found.astype(BF)
        if columns < width:
            att_g[w, :, columns:] = jnp.zeros((length, width - columns), BF)
        copy_of(att_g.at[w], att_g_h.at[w], sem_out.at[1]).start()
        start = BLOCK * window_at(w)
        part = jnp.where(chunk_mask(w, length), att[:, start : start + 2 * BLOCK].astype(F32), 0.0).astype(BF)
        wo_g[:, start : start + 2 * BLOCK] += matmul(total[...].astype(BF).T, part)
    outer_b[...] = outer[...].astype(BF)
    inner_b[...] = inner[...].astype(BF)
    writes = give_halves(table[source.core], outer_b, inner_b, mine_h, other_h, sem_out.at[2])
    wo_g_b[...] = wo_g[...].astype(BF)
    copy = copy_of(wo_g_b, wo_g_h, sem_out.at[2])
    copy.start()
    for copy in writes + [copy, copy_of(grads, first_g_h, sem_out.at[0]), copy_of(att_g, att_g_h, sem_out.at[1])]:
        copy.wait()


def feed_zero(source, vec, feed, feed_t, normed_t, act, slope, grad, hat, scale, att, wo):
    _, length, width = feed.shape
    four, four_t = (WIDTHS, length, width), (WIDTHS, width, length)
    return call(
        functools.partial(feed_zero_kernel, source),
        LIMIT,
        28,
        in_specs=[SCALARS, held(vec)] + [ANY] * (10 + len(source.arrays)),
        out_specs=[ANY] * 5 + [held(vec), held(vec)],
        out_shape=[
            shape_of((width, width), BF),
            shape_of((width, width), BF),
            shape_of(four, F32),
            shape_of(four, BF),
            shape_of((width, width), BF),
            shape_of((1, 1, width), F32),
            shape_of((8, width), F32),
        ],
        scratch_shapes=[
            pltpu.VMEM((width, 2 * width), BF),
            pltpu.VMEM(four, BF),
            pltpu.VMEM(four_t, BF),
            pltpu.VMEM(four_t, BF),
            pltpu.VMEM(four, BF),
            pltpu.VMEM(four, BF),
            pltpu.VMEM((width, width), F32),
            pltpu.VMEM((width, width), F32),
            pltpu.VMEM(four, F32),
            pltpu.VMEM((width, width), BF),
            pltpu.VMEM((width, width), BF),
            pltpu.VMEM(four, BF),
            pltpu.VMEM((WIDTHS, length, 1), F32),
            pltpu.VMEM((length, width), BF),
            pltpu.VMEM((width, width), BF),
            pltpu.VMEM(four, BF),
            pltpu.VMEM((length, width), F32),
            pltpu.VMEM((width, width), F32),
            pltpu.VMEM((width, width), BF),
            pltpu.SemaphoreType.DMA((2,)),
            pltpu.SemaphoreType.DMA((7, WIDTHS)),
            pltpu.SemaphoreType.DMA((WIDTHS,)),
            pltpu.SemaphoreType.DMA((2,)),
            pltpu.SemaphoreType.DMA((3,)),
        ],
        name="feed_zero",
    )(source.table, vec, feed, feed_t, normed_t, act, slope, grad, hat, scale, att, wo, *source.arrays)


def attend_back_kernel(first_pair, pairs, own, core, x_t, wo_g, q, k, v, p, g, *refs):
    dq_o, dk_o, dv_o, mine_o, other_o, sums_o, dk_t, dv_t = refs
    step = pl.program_id(0)
    pair = first_pair + step
    columns = pairs * BLOCK
    length = q.shape[0]
    spans = windows(length)
    factor = 1.0 / math.sqrt(HEAD_DIM)
    lane = lax.broadcasted_iota(jnp.int32, (BLOCK, BLOCK), 1)
    low_half = lane < HEAD_DIM
    masks = (
        jnp.where(low_half, 1.0, 0.0).astype(BF),
        jnp.where(low_half, 0.0, 1.0).astype(BF),
    )

    def run(first):
        widths = list(range(first, WIDTHS))
        many = len(widths)
        dk_t[...] = jnp.zeros_like(dk_t)
        dv_t[...] = jnp.zeros_like(dv_t)
        q_t = (q[...] * jnp.asarray(factor, BF)).T
        g_t = [g[w].T for w in widths]
        mask = jnp.concatenate([masks[0]] * many + [masks[1]] * many, axis=0)
        wide = jnp.concatenate([low_half] * many, axis=0)
        chance_g = []
        for i, (start, span) in enumerate(spans):
            g_here = jnp.concatenate([g[w, i * BLOCK : (i + 1) * BLOCK, :] for w in widths], axis=0)
            chance_g.append(matmul_last(jnp.concatenate([g_here, g_here], axis=0) * mask, v[start : start + span, :]))
        scores_g = []
        for i, (start, span) in enumerate(spans):
            lows = []
            for half in range(2):
                chances = p[half, i, :, :span].astype(F32)
                for n in range(many):
                    at = (half * many + n) * BLOCK
                    product = chances * chance_g[i][at : at + BLOCK, :]
                    row = jnp.sum(product, axis=1, keepdims=True)
                    lows.append((product - chances * row).astype(BF))
            scores_g.append(lows)
        for i, (start, span) in enumerate(spans):
            here = slice(i * BLOCK, (i + 1) * BLOCK)
            near = slice(start, start + span)
            lows = scores_g[i]
            found = matmul(jnp.concatenate(lows, axis=0), k[near, :] * jnp.asarray(factor, BF))
            dq = jnp.where(wide, found[: many * BLOCK], found[many * BLOCK :]).astype(BF)
            for n, w in enumerate(widths):
                dq_o[w, here, :] = dq[n * BLOCK : (n + 1) * BLOCK, :]
            for half in range(2):
                rows_of = slice(half * HEAD_DIM, (half + 1) * HEAD_DIM)
                for n, w in enumerate(widths):
                    dk_t[w, rows_of, near] += matmul(q_t[rows_of, here], lows[half * many + n])
                stacked = jnp.concatenate([g_t[n][rows_of, here] for n in range(many)], axis=0)
                values_g = matmul(stacked, p[half, i, :, :span])
                for n, w in enumerate(widths):
                    dv_t[w, rows_of, near] += values_g[n * HEAD_DIM : (n + 1) * HEAD_DIM, :]
        totals = [jnp.zeros((length, BLOCK), F32) for _ in range(3)]
        for w in range(WIDTHS):
            if w < first:
                for ref in (dq_o, dk_o, dv_o):
                    ref[w] = jnp.zeros((length, BLOCK), BF)
                continue
            dk_o[w] = dk_t[w].astype(BF).T
            dv_o[w] = dv_t[w].astype(BF).T
            for n, ref in enumerate((dq_o, dk_o, dv_o)):
                totals[n] += ref[w].astype(F32)
        here = pl.ds(pl.multiple_of(step * BLOCK, BLOCK), BLOCK)
        beside = pl.ds(pl.multiple_of(columns + step * BLOCK, BLOCK), BLOCK)
        sums_o[0:1, here] = jnp.sum(totals[0], axis=0, keepdims=True)
        sums_o[1:2, here] = jnp.sum(totals[2], axis=0, keepdims=True)
        parts = [matmul(x_t[...], total.astype(BF)).astype(BF) for total in totals]

        def fill(first, second):
            first[:, here] = parts[0]
            first[:, beside] = parts[1]
            second[:, here] = parts[2]
            second[:, beside] = wo_g[...]

        pl.when(core[0] == 0)(lambda: fill(mine_o, other_o))
        pl.when(core[0] != 0)(lambda: fill(other_o, mine_o))

    heads_each = HEADS // WIDTHS
    firsts = [(2 * n) // heads_each for n in range(HEADS // 2)]
    for first in sorted(set(firsts)):
        members = [n for n, f in enumerate(firsts) if f == first and first_pair <= n < first_pair + pairs]
        if not members:
            continue

        @pl.when((pair >= members[0]) & (pair <= members[-1]))
        def _(first=first):
            run(first)


def vector_rows(own, sums_o, given):
    sums_c, sums_a, sums_b, sums_b2, bias_0, bias_1, bias_hi = given
    width = sums_a.shape[1]
    rows = [
        jnp.concatenate([sums_c[0:1, :], sums_o[0:1, :]], axis=1),
        jnp.concatenate([sums_c[1:2, :], sums_o[1:2, :]], axis=1),
        sums_a[2:3, :],
        sums_a[0:1, :],
        sums_a[1:2, :],
        sums_b[2:3, :] + sums_b2[2:3, :],
        sums_b[0:1, :] + sums_b2[0:1, :],
        sums_b[1:2, :] + sums_b2[1:2, :],
        jnp.zeros((8, width), F32),
    ]
    for j in range(WIDTHS):
        rows += [(bias_0[0], bias_1[0], bias_hi[0], bias_hi[1])[j]] * WIDTHS
    rows.append(jnp.zeros((BLOCK - 16 - WIDTHS * WIDTHS, width), F32))
    turned = jnp.concatenate(rows, axis=0).T
    lane = lax.broadcasted_iota(jnp.int32, (own, BLOCK), 1)
    blocks = []
    each = width // (own * WIDTHS)
    for j in range(WIDTHS):
        for n in range(each):
            at = (j * each + n) * own
            block = jnp.where(lane < 8, turned[at : at + own, :], 0.0)
            for m in range(WIDTHS):
                start = (n * WIDTHS + m) * own
                block = jnp.where(lane == 16 + WIDTHS * j + m, turned[start : start + own, :], block)
            blocks.append(block.astype(BF))
    return jnp.concatenate(blocks, axis=0)


def attend_back_last_kernel(first_pair, pairs, own, *refs):
    given, rest = refs[8:-8], refs[-8:]
    attend_back_kernel(first_pair, pairs, own, *refs[:8], *rest)
    if given:
        mine_o, other_o, sums_o = rest[3:6]

        @pl.when(pl.program_id(0) == pairs - 1)
        def _():
            block = vector_rows(own, sums_o, given)
            mine_o[:, 2 * pairs * BLOCK :] = block
            other_o[:, 2 * pairs * BLOCK :] = block


def attend_backward(core, first_pair, pairs, own, x_t, wo_g, q, k, v, p, g, given):
    length, width = q.shape
    columns = pairs * BLOCK
    part = pl.BlockSpec((length, BLOCK), lambda n: (0, first_pair + n))
    wide = pl.BlockSpec((WIDTHS, length, BLOCK), lambda n: (0, 0, first_pair + n))
    wide_o = pl.BlockSpec((WIDTHS, length, BLOCK), lambda n: (0, 0, n))
    out = (width, 2 * columns + (BLOCK if given else 0))
    return call(
        functools.partial(attend_back_last_kernel, first_pair, pairs, own),
        LIMIT,
        12,
        grid=(pairs,),
        in_specs=[
            SCALARS,
            whole(x_t.shape),
            pl.BlockSpec((width, BLOCK), lambda n: (0, first_pair + n)),
            part,
            part,
            part,
            pl.BlockSpec((2,) + p.shape[1:], lambda n: (first_pair + n, 0, 0, 0)),
            wide,
        ]
        + [whole(entry.shape) for entry in given],
        out_specs=[wide_o] * 3 + [whole(out)] * 2 + [whole((8, columns))],
        out_shape=[shape_of((WIDTHS, length, columns), BF)] * 3
        + [shape_of(out, BF)] * 2
        + [shape_of((8, columns), F32)],
        scratch_shapes=[pltpu.VMEM((WIDTHS, BLOCK, length), F32)] * 2,
        name="attend_backward",
    )(jnp.full((1,), core, jnp.int32), x_t, wo_g, q, k, v, p, g, *given)


def input_kernel(some, first_g, dq_a, dk_a, dv_a, dq_b, dk_b, dv_b, wq, wk, wv, *refs):
    out = refs[-1]
    w = pl.program_id(0)
    split = dq_a.shape[2]
    for section in some:
        kept = -(-(section + 1) * 3 * HEAD_DIM // BLOCK) * BLOCK

        @pl.when(w == section - some[0])
        def _():
            total = first_g[0]
            for low, high, weight in ((dq_a, dq_b, wq), (dk_a, dk_b, wk), (dv_a, dv_b, wv)):
                near = min(kept, split)
                total += matmul_last(low[0, :, :near], weight[:, :near])
                if kept > split:
                    total += matmul_last(high[0, :, : kept - split], weight[:, split:kept])
            out[0] = total


def input_grads(some, first_g, low, high, query_key, value_output, earlier):
    _, length, width = first_g.shape
    base = some[0]
    per_width = pl.BlockSpec((1, length, width), lambda w: (w + base, 0, 0))
    part = pl.BlockSpec((1, length, low[0].shape[2]), lambda w: (w + base, 0, 0))
    last = pl.BlockSpec((1, length, high[0].shape[2]), lambda w: (jnp.maximum(w + base, WIDTHS // 2), 0, 0))
    given = [] if earlier is None else [earlier]

    def weight(n):
        return pl.BlockSpec((width, width), lambda w: (0, n))

    return call(
        functools.partial(input_kernel, some),
        LIMIT,
        8,
        grid=(len(some),),
        in_specs=[per_width] + [part] * 3 + [last] * 3 + [weight(0), weight(1), weight(0)] + [ANY] * len(given),
        out_specs=per_width,
        out_shape=shape_of(first_g.shape, F32),
        input_output_aliases={10: 0} if given else {},
        name="input_grads",
    )(first_g, *low, *high, query_key, query_key, value_output, *given)


def tie(*values):
    return lax.optimization_barrier(values)


class Ring:
    def __init__(self, mesh):
        self.dp = mesh.shape["dp"]
        self.fsdp = mesh.shape["fsdp"]
        self.square = self.fsdp == 8 and self.dp == 4
        index = lax.axis_index("fsdp")
        self.z = lax.axis_index("dp")
        self.y, self.x, self.c = index // 4, (index // 2) % 2, index % 2

    def swap(self, value, bit):
        total = self.dp * self.fsdp
        return lax.ppermute(value, AXES, [(i, i ^ bit) for i in range(total)])

    def shift(self, value, by):
        total = self.dp * self.fsdp
        return lax.ppermute(value, AXES, [(i, (i + by * self.fsdp) % total) for i in range(total)])

    def along(self, value, bit):
        total = self.dp * self.fsdp
        return lax.ppermute(value, AXES, [(i, i ^ (bit * self.fsdp)) for i in range(total)])

    def mine(self, first, second):
        return jnp.where(self.c == 0, first, second)


CORE, X_SIDE, Y_SIDE = 1, 2, 4


class Gather:
    def __init__(self, ring, halves):
        self.ring, self.halves = ring, halves
        self.shard = halves
        self.line = self.came = self.sides = self.corners = self.crossed = ()

    def start_core(self):
        ring = self.ring
        if ring.square:
            kept, sent = ring.mine(*self.halves), ring.mine(*self.halves[::-1])
            came = ring.swap(sent, CORE)
            self.shard = ring.mine(jnp.concatenate([kept, came], axis=0), jnp.concatenate([came, kept], axis=0))

    def start_line(self, first=0, columns=None):
        ring = self.ring
        if ring.square:
            part = self.shard[:, first : self.shard.shape[1] if columns is None else first + columns]
            self.came += (tuple(ring.shift(part, by) for by in range(1, ring.dp)),)

    def ready_line(self):
        if self.ring.square:
            came = [jnp.concatenate(parts, axis=1) for parts in zip(*self.came)]
            self.line = jnp.stack([self.shard] + came)

    def start_sides(self):
        ring = self.ring
        if ring.square:
            self.sides = (ring.swap(self.line, X_SIDE), ring.swap(self.line, Y_SIDE))

    def start_corners(self):
        ring, half = self.ring, self.ring.dp // 2
        if ring.square:
            self.corners = (
                ring.swap(self.sides[0][:half], Y_SIDE),
                ring.swap(self.sides[1][half:], X_SIDE),
            )

    def cross(self, *values):
        if self.ring.square:
            self.crossed += tuple(self.ring.swap(value, CORE) for value in values)

    def pieces(self):
        ring, half = self.ring, self.ring.dp // 2
        own = (
            (self.line, 0, ring.y, ring.x),
            (self.sides[0], 0, ring.y, 1 - ring.x),
            (self.sides[1], 0, 1 - ring.y, ring.x),
            (self.corners[0], 0, 1 - ring.y, 1 - ring.x),
            (self.corners[1], half, 1 - ring.y, 1 - ring.x),
        )
        rows = self.shard.shape[0]
        copies, at = [], []
        for n, (value, behind, y, x) in enumerate(own):
            for index in range(value.shape[0]):
                z = (ring.z + ring.dp - behind - index) % ring.dp
                copies.append((n, index))
                at.append(jnp.asarray(rows * ((z * 2 + y) * 2 + x), jnp.int32))
        arrays = [value for value, *_ in own] + list(self.crossed)
        return arrays, copies, jnp.stack(at + [jnp.asarray(ring.c, jnp.int32)])

    def source(self):
        return Source(self)


class PlaneFirst(Gather):
    def start_plane(self):
        ring = self.ring
        if ring.square:
            row = jnp.stack([self.shard, ring.swap(self.shard, X_SIDE)])
            self.sides = (row, ring.swap(row, Y_SIDE))

    def ready_line(self):
        if self.ring.square:
            self.line = jnp.concatenate(self.sides)

    def start_line(self):
        ring = self.ring
        if ring.square:
            self.came = tuple(ring.shift(self.line, by) for by in range(1, ring.dp))

    def pieces(self):
        ring = self.ring
        rows = self.shard.shape[0]
        copies, at = [], []
        for behind in range(ring.dp):
            z = (ring.z + ring.dp - behind) % ring.dp
            for index, (y, x) in enumerate(
                ((ring.y, ring.x), (ring.y, 1 - ring.x), (1 - ring.y, ring.x), (1 - ring.y, 1 - ring.x))
            ):
                copies.append((behind, index))
                at.append(jnp.asarray(rows * ((z * 2 + y) * 2 + x), jnp.int32))
        arrays = [self.line, *self.came, *self.crossed]
        return arrays, copies, jnp.stack(at + [jnp.asarray(ring.c, jnp.int32)])


class Source:
    def __init__(self, gather):
        ring = gather.ring
        self.square = ring.square
        self.columns = gather.halves[0].shape[1]
        if ring.square:
            self.rows = gather.shard.shape[0]
            self.arrays, self.copies, self.table = gather.pieces()
        else:
            self.rows = gather.halves[0].shape[0] * ring.dp * ring.fsdp
            self.arrays = [lax.all_gather(half, AXES, axis=0, tiled=True) for half in gather.halves]
            self.copies = []
            self.table = jnp.asarray(ring.c, jnp.int32).reshape(1)
        self.core = len(self.copies)

    def start(self, table, pieces, target, sems, first, columns, to):
        apart = target.shape[1] // 2
        if not self.square:
            for half in range(2):
                pltpu.make_async_copy(
                    pieces[half].at[:, pl.ds(first, columns)],
                    target.at[:, pl.ds(half * apart + to, columns)],
                    sems.at[half],
                ).start()
            return
        core = table[self.core]
        many = len(pieces) // 2
        for side in range(2):
            half = core if side == 0 else 1 - core
            for n, (piece, index) in enumerate(self.copies):
                row = pl.multiple_of(table[n], 16)
                pltpu.make_async_copy(
                    pieces[side * many + piece].at[index, :, pl.ds(first, columns)],
                    target.at[pl.ds(row, self.rows), pl.ds(pl.multiple_of(half * apart + to, BLOCK), columns)],
                    sems.at[half],
                ).start()

    def wait(self, target, sems, columns, to):
        for half in range(2):
            whole_half = target.at[:, pl.ds(half * (target.shape[1] // 2) + to, columns)]
            pltpu.make_async_copy(whole_half, whole_half, sems.at[half]).wait()


def place_rows(source, layout, beside):
    count = len(source.arrays)
    rows = source.rows * max(len(source.copies), 1)

    def kernel(table, *refs):
        pieces, outs = refs[:count], refs[count : count + len(layout)]
        sem = refs[-1]
        if not source.square:
            copies = [
                pltpu.make_async_copy(pieces[half].at[:, pl.ds(first, columns)], outs[n], sem.at[0])
                for n, (half, first, columns) in enumerate(layout)
            ]
            for copy in copies:
                copy.start()
            for copy in copies:
                copy.wait()
            return
        many = count // 2
        core = table[source.core]
        parts = [(half, first, columns, outs[n], 0) for n, (half, first, columns) in enumerate(layout)]
        if beside is not None:
            vec, bi, block = refs[count + len(layout) : -1]
            parts.insert(0, (0, beside, BLOCK, block, 1))

        def run(own):
            copies = []
            for half, first, columns, out, which in parts:
                for m, (piece, index) in enumerate(source.copies):
                    row = pl.multiple_of(table[m], 16)
                    copies.append(
                        (
                            which,
                            pltpu.make_async_copy(
                                pieces[piece + (0 if half == own else many)].at[index, :, pl.ds(first, columns)],
                                out.at[pl.ds(row, source.rows), :],
                                sem.at[which],
                            ),
                        )
                    )
            for _, copy in copies:
                copy.start()
            for which, copy in copies:
                if which == 1:
                    copy.wait()
            if beside is not None:
                vector_columns(block, vec, bi)
            for which, copy in copies:
                if which == 0:
                    copy.wait()

        for own in range(2):
            pl.when(core == own)(functools.partial(run, own))

    more = ([], [], [])
    if beside is not None:
        more = (
            [pl.BlockSpec(memory_space=pltpu.VMEM)] * 2,
            [shape_of((8, rows), F32), shape_of((WIDTHS, rows), F32)],
            [pltpu.VMEM((rows, BLOCK), BF)],
        )
    return call(
        kernel,
        LIMIT_PLACE,
        5,
        in_specs=[SCALARS] + [ANY] * count,
        out_specs=[pl.BlockSpec(memory_space=pltpu.VMEM)] * len(layout) + more[0],
        out_shape=[shape_of((rows, columns), BF) for *_, columns in layout] + more[1],
        scratch_shapes=more[2] + [pltpu.SemaphoreType.DMA((2,))],
        name="place_rows",
    )(source.table, *source.arrays)


def vector_columns(block, vec, bi):
    full = block[...].astype(F32)
    width = full.shape[0]
    vec[...] = full.T[:8, :]
    each = 8
    own = width // (each * WIDTHS)
    lane = lax.broadcasted_iota(jnp.int32, (own, BLOCK), 1)
    pieces = []
    for n in range(each):
        for m in range(WIDTHS):
            piece = jnp.zeros((own, BLOCK), F32)
            for j in range(WIDTHS):
                start = (j * each + n) * own
                piece = jnp.where(lane == 16 + WIDTHS * j + m, full[start : start + own, :], piece)
            pieces.append(piece)
    turned = jnp.concatenate(pieces, axis=0).T
    for j in range(WIDTHS):
        at = 16 + WIDTHS * j
        bi[j : j + 1, :] = jnp.sum(turned[at : at + WIDTHS, :], axis=0, keepdims=True)


class Scatter:
    def __init__(self, ring, mine, other):
        self.ring, self.kept, self.other = ring, mine, other
        self.came = self.sides = self.leaving = self.far = self.near = self.own = ()

    def start_core(self):
        if self.ring.square:
            self.came = self.ring.swap(self.other, CORE)

    def block(self, y, x):
        dp = self.ring.dp

        def pick(value):
            value = value.reshape(dp, 2, 2, value.shape[0] // (4 * dp), value.shape[1])
            value = lax.dynamic_index_in_dim(value, y, 1, keepdims=False)
            return lax.dynamic_index_in_dim(value, x, 1, keepdims=False)

        return pick(self.kept).astype(F32) + pick(self.came).astype(F32)

    def ready_sides(self):
        ring = self.ring
        if ring.square:
            to_x = self.block(ring.y, 1 - ring.x).astype(BF)
            to_y = self.block(1 - ring.y, ring.x).astype(BF)
            corner = self.block(1 - ring.y, 1 - ring.x).astype(BF)
            self.leaving = (corner, to_x, to_y)

    def start_sides(self):
        ring = self.ring
        if ring.square:
            corner, to_x, to_y = self.leaving
            self.sides = (ring.swap(corner, X_SIDE | Y_SIDE), ring.swap(to_x, X_SIDE), ring.swap(to_y, Y_SIDE))

    def ready_far(self):
        ring = self.ring
        if ring.square:
            line = self.block(ring.y, ring.x)
            for side in self.sides:
                line = line + side.astype(F32)
            line = line.reshape(2, 2, *line.shape[1:])
            self.leaving = lax.dynamic_index_in_dim(line, 1 - ring.z // 2, 0, keepdims=False).astype(BF)
            self.own = lax.dynamic_index_in_dim(line, ring.z // 2, 0, keepdims=False)

    def start_far(self):
        if self.ring.square:
            self.far = self.ring.along(self.leaving, 2)

    def ready_near(self):
        ring = self.ring
        if ring.square:
            pair = self.own + self.far.astype(F32)
            self.leaving = lax.dynamic_index_in_dim(pair, 1 - ring.z % 2, 0, keepdims=False).astype(BF)
            self.own = lax.dynamic_index_in_dim(pair, ring.z % 2, 0, keepdims=False)

    def start_near(self):
        if self.ring.square:
            self.near = (self.ring.along(self.leaving, 1),)

    def ready_last(self):
        ring = self.ring
        if ring.square:
            line = self.block(ring.y, ring.x)
            for side in self.sides:
                line = line + side.astype(F32)
            low = line.astype(BF)
            self.own = lax.dynamic_index_in_dim(line, ring.z, 0, keepdims=False)
            self.leaving = tuple(
                lax.dynamic_index_in_dim(low, (ring.z + by) % ring.dp, 0, keepdims=False) for by in range(1, ring.dp)
            )

    def start_last(self):
        ring = self.ring
        if ring.square:
            self.near = tuple(ring.shift(value, by) for by, value in enumerate(self.leaving, 1))


def finish(ring, groups):
    if not ring.square:
        halves = (
            jnp.concatenate([ring.mine(group.kept, group.other) for group in groups], axis=1),
            jnp.concatenate([ring.mine(group.other, group.kept) for group in groups], axis=1),
        )
        return tuple(lax.psum_scatter(half.astype(F32), AXES, scatter_dimension=0, tiled=True) for half in halves)
    total = jnp.concatenate(
        [functools.reduce(lambda sum_, part: sum_ + part.astype(F32), group.near, group.own) for group in groups], axis=1
    )
    rows = total.shape[0] // 2
    kept, sent = ring.mine(total[:rows], total[rows:]), ring.mine(total[rows:], total[:rows])
    came = ring.swap(sent, CORE)
    return ring.mine(kept, came), ring.mine(came, kept)


def solution(mesh):
    rows_split = P(AXES, None)
    vector_split = P(AXES)

    def per_device(
        tokens,
        segment_ids,
        output_grad,
        query_weight,
        query_bias,
        key_weight,
        value_weight,
        value_bias,
        output_weight,
        output_bias,
        first_gain,
        first_shift,
        inner_weight,
        inner_bias,
        outer_weight,
        outer_bias,
        second_gain,
        second_shift,
    ):
        ring = Ring(mesh)
        devices = ring.dp * ring.fsdp
        width = tokens.shape[1]
        hidden = inner_weight.shape[1]
        own = query_bias.shape[0]
        half = hidden // 2
        singles = (query_bias, value_bias, output_bias, first_gain, first_shift, outer_bias, second_gain, second_shift)
        count = len(singles)
        beside = ring.square and own % 8 == 0
        columns = []
        if beside:
            row = lax.broadcasted_iota(jnp.int32, (BLOCK, own), 0)
            block = jnp.zeros((BLOCK, own), BF)
            for n, vector in enumerate(singles):
                block = jnp.where(row == n, vector[None], block)
            chunk = (ring.z * ring.fsdp + lax.axis_index("fsdp")) // (devices // WIDTHS)
            for n in range(WIDTHS):
                quarter = inner_bias[n * own : (n + 1) * own]
                block = jnp.where(row == 16 + WIDTHS * chunk + n, quarter[None], block)
            columns = [block.T]

        def side(*parts):
            return jnp.concatenate(parts, axis=1)

        one = Gather(ring, (side(query_weight, key_weight, *columns), side(value_weight, output_weight, *columns)))
        two = Gather(ring, (inner_weight, outer_weight))
        pair = 2 * width
        one.start_core()
        one.shard, two.halves = tie(one.shard, two.halves)
        one.start_line()
        two.start_core()
        one.came, two.shard = tie(one.came, two.shard)
        one.ready_line()
        one.start_sides()
        two.start_line(0, half)
        one.line, one.sides, two.came = tie(one.line, one.sides, two.came)
        one.start_corners()
        two.start_line(half, half)
        one.line, one.sides, one.corners, two.came = tie(one.line, one.sides, one.corners, two.came)
        one.cross(one.line, *one.sides, *one.corners)
        two.ready_line()
        two.start_sides()
        source_one = one.source()
        query_key, value_output, *vectors = place_rows(source_one, ((0, 0, pair), (1, 0, pair)), pair if beside else None)
        if beside:
            vec, bi = vectors
            bi = bi.reshape(WIDTHS, 1, width)
        else:
            vec = jnp.stack([lax.all_gather(entry, AXES, tiled=True) for entry in singles]).astype(F32)
            bi = lax.all_gather(inner_bias, AXES, tiled=True).astype(F32).reshape(WIDTHS, 1, width)
        q, k, v, att, p = attend(tokens, query_key, value_output, vec, segment_ids[0])
        att, two.line, two.sides = tie(att, two.line, two.sides)
        two.start_corners()
        two.cross(two.line, *two.sides)
        hat, scale, normed, normed_t, second, x_t = first_norm(tokens, att, value_output, vec)
        normed, two.corners, two.crossed = tie(normed, two.corners, two.crossed)
        two.cross(*two.corners)
        source_two = two.source()

        act, slope, act_1, slope_1, out, feed, feed_t, mine, other, grad, bias_hi, sums_b = feed_high(
            source_two, normed, bi, second, output_grad, vec, normed_t
        )
        high = Scatter(ring, mine, other)
        high.start_core()
        grad, high.came = tie(grad, high.came)
        high.ready_sides()
        grad, high.leaving = tie(grad, high.leaving)
        high.start_sides()
        act, slope, out, feed, feed_t, mine, other, grad, bias_1, sums_b2 = feed_mid(
            source_two, normed, bi, second, output_grad, vec, normed_t, act_1, slope_1, grad, act, slope, out, feed, feed_t
        )
        grad, other, high.sides = tie(grad, other, high.sides)

        mid = Scatter(ring, mine, other)
        mid.start_core()
        high.ready_far()
        mid.ready_sides()
        grad, mid.leaving, high.leaving = tie(grad, mid.leaving, high.leaving)
        mid.start_sides()
        high.start_far()
        mine, other, first_g, att_g, wo_g, bias_0, sums_a = feed_zero(
            source_two, vec, feed, feed_t, normed_t, act, slope, grad, hat, scale, att, value_output
        )
        att_g, other, mid.sides, high.far = tie(att_g, other, mid.sides, high.far)

        low = Scatter(ring, mine, other)
        low.start_core()
        high.ready_near()
        mid.ready_far()
        low.ready_sides()
        att_g, low.leaving, mid.leaving, high.leaving = tie(att_g, low.leaving, mid.leaving, high.leaving)
        low.start_sides()
        mid.start_far()
        high.start_near()
        pairs = HEADS // 4
        *low_g, mine, other, sums_c = attend_backward(ring.c, 0, pairs, own, x_t, wo_g, q, k, v, p, att_g, ())
        att_g, other, low.sides, mid.far, high.near = tie(att_g, other, low.sides, mid.far, high.near)

        left = Scatter(ring, mine, other)
        left.start_core()
        mid.ready_near()
        low.ready_far()
        left.ready_sides()
        att_g, left.leaving, low.leaving, mid.leaving = tie(att_g, left.leaving, low.leaving, mid.leaving)
        left.start_sides()
        low.start_far()
        mid.start_near()
        given = (sums_c, sums_a, sums_b, sums_b2, bias_0, bias_1, bias_hi) if beside else ()
        *high_g, mine, other, sums_d = attend_backward(
            ring.c, pairs, pairs, own, x_t, wo_g, q, k, v, p, att_g, given
        )
        first_g, other, left.sides, low.far, mid.near = tie(first_g, other, left.sides, low.far, mid.near)

        right = Scatter(ring, mine, other)
        right.start_core()
        low.ready_near()
        left.ready_far()
        right.ready_sides()
        first_g, right.leaving, left.leaving, low.leaving = tie(first_g, right.leaving, left.leaving, low.leaving)
        right.start_sides()
        left.start_far()
        low.start_near()
        in_g = input_grads(tuple(range(WIDTHS)), first_g, low_g, high_g, query_key, value_output, None)
        in_g, right.sides, left.far, low.near = tie(in_g, right.sides, left.far, low.near)

        left.ready_near()
        right.ready_last()
        right.leaving, left.leaving = tie(right.leaving, left.leaving)
        right.start_last()
        left.start_near()
        outer_g, inner_g = finish(ring, (low, mid, high))
        right.near, left.near, outer_g = tie(right.near, left.near, outer_g)
        first_half, second_half = finish(ring, (left, right))
        split = pairs * BLOCK
        parts = [
            side(entry[:, at : at + split], entry[:, at + 2 * split : at + 3 * split])
            for entry in (first_half, second_half)
            for at in (0, split)
        ]
        wq_g, wk_g, wv_g, wo_g = parts
        if beside:
            last = first_half[:, 4 * split :]
            bias_g = last[:, 16 : 16 + WIDTHS * WIDTHS].reshape(own, WIDTHS, WIDTHS).sum(axis=1)
            vectors_g = [last[:, n] for n in range(count)] + [bias_g.T.reshape(own * WIDTHS)]
        else:
            attention_sums = jnp.concatenate([sums_c[:2], sums_d[:2]], axis=1)
            sums_b = sums_b + sums_b2
            rows = [*attention_sums, sums_a[2], sums_a[0], sums_a[1], sums_b[2], sums_b[0], sums_b[1]]
            rows.append(jnp.concatenate([bias_0, bias_1, bias_hi], axis=0).reshape(hidden))
            vectors_g = [lax.psum_scatter(entry, AXES, scatter_dimension=0, tiled=True) for entry in rows]
        bq_g, bv_g, bo_g, ga_g, sa_g, bu_g, gb_g, sb_g, bi_g = vectors_g
        return (
            out, in_g, wq_g, bq_g, wk_g, wv_g, bv_g, wo_g, bo_g, ga_g, sa_g, inner_g, bi_g, outer_g, bu_g, gb_g, sb_g,
        )

    layered = P(None, AXES, None)
    return jax.shard_map(
        per_device,
        mesh=mesh,
        in_specs=(
            rows_split, rows_split, layered, rows_split, vector_split, rows_split, rows_split, vector_split,
            rows_split, vector_split, vector_split, vector_split, rows_split, vector_split, rows_split,
            vector_split, vector_split, vector_split,
        ),
        out_specs=(
            layered, layered, rows_split, vector_split, rows_split, rows_split, vector_split, rows_split,
            vector_split, vector_split, vector_split, rows_split, vector_split, rows_split, vector_split,
            vector_split, vector_split,
        ),
        check_vma=False,
    )
```

```python
import functools
import math

import jax
import jax.numpy as jnp
from jax import lax
from jax.experimental import pallas as pl
from jax.experimental.pallas import tpu as pltpu
from jax.sharding import PartitionSpec as P

HEADS = 12
HEAD_DIM = 64
WIDTHS = 4
BLOCK = 128
AXES = ("dp", "fsdp")
BF = jnp.bfloat16
F32 = jnp.float32
MIB = 1024 * 1024
LIMIT = 60
LIMIT_PLACE = 60
LIMIT_ATTEND = 60
BYTES = 3.3e6


def matmul(left_side, right_side):
    return lax.dot_general(
        left_side, right_side, (((1,), (0,)), ((), ())), preferred_element_type=F32
    )


def matmul_last(left_side, right_side):
    return lax.dot_general(
        left_side, right_side, (((1,), (1,)), ((), ())), preferred_element_type=F32
    )


def windows(length):
    count = length // BLOCK
    spans = []
    for i in range(count):
        start = max(0, i - 1) * BLOCK
        spans.append((start, min(count, i + 2) * BLOCK - start))
    return spans


def call(kernel, limit, micros, **options):
    return pl.pallas_call(
        kernel,
        compiler_params=pltpu.CompilerParams(vmem_limit_bytes=limit * MIB),
        cost_estimate=pl.CostEstimate(flops=0, bytes_accessed=int(micros * BYTES), transcendentals=0),
        **options,
    )


def shape_of(shape, dtype):
    return jax.ShapeDtypeStruct(shape, dtype)


def whole(shape):
    return pl.BlockSpec(shape, lambda *_: (0,) * len(shape))


def attend_kernel(x, wq, wk, wv, vec, seg_col, seg_row, q_o, k_o, v_o, a_o, p_o, bias):
    spans = windows(x.shape[0])

    @pl.when(pl.program_id(0) == 0)
    def _():
        for i, (start, span) in enumerate(spans):
            same = seg_col[i * BLOCK : (i + 1) * BLOCK, :] == seg_row[:, start : start + span]
            bias[i, :, :span] = jnp.where(same, 0.0, -1e30)

    rows = x[...]
    q_o[...] = (matmul(rows, wq[...]) + vec[0:1, :]).astype(BF)
    k_o[...] = matmul(rows, wk[...]).astype(BF)
    v_o[...] = (matmul(rows, wv[...]) + vec[1:2, :]).astype(BF)
    lane = lax.broadcasted_iota(jnp.int32, (BLOCK, BLOCK), 1)
    low_half = lane < HEAD_DIM
    factor = 1.0 / math.sqrt(HEAD_DIM)
    mask = jnp.concatenate(
        [jnp.where(low_half, factor, 0.0).astype(BF), jnp.where(low_half, 0.0, factor).astype(BF)], axis=0
    )
    for pair in range(q_o.shape[1] // BLOCK):
        cols = slice(pair * BLOCK, (pair + 1) * BLOCK)
        scores = []
        for i, (start, span) in enumerate(spans):
            q_here = q_o[i * BLOCK : (i + 1) * BLOCK, cols]
            both = jnp.concatenate([q_here, q_here], axis=0) * mask
            scores.append(matmul_last(both, k_o[start : start + span, cols]))
        chances = []
        for i, (start, span) in enumerate(spans):
            blocked = bias[i, :, :span]
            score = scores[i] + jnp.concatenate([blocked, blocked], axis=0)
            shifted = jnp.exp(score - jnp.max(score, axis=1, keepdims=True))
            total = jnp.sum(shifted, axis=1, keepdims=True)
            chances.append((shifted * (1.0 / total)).astype(BF))
        for i, (start, span) in enumerate(spans):
            mixed = matmul(chances[i], v_o[start : start + span, cols])
            here = slice(i * BLOCK, (i + 1) * BLOCK)
            a_o[here, cols] = jnp.where(low_half, mixed[:BLOCK], mixed[BLOCK:]).astype(BF)
            p_o[2 * pair, i, :, :span] = chances[i][:BLOCK]
            p_o[2 * pair + 1, i, :, :span] = chances[i][BLOCK:]


def attend(x, query_key, value_output, vec, segments, segments_row):
    length, width = x.shape
    step = 256
    steps = width // step
    count = length // BLOCK
    part = pl.BlockSpec((length, step), lambda p: (0, p))
    heads = step // HEAD_DIM

    def weight(n):
        return pl.BlockSpec((width, step), lambda p: (0, n * steps + p))

    return call(
        attend_kernel,
        LIMIT_ATTEND,
        9.5,
        grid=(steps,),
        in_specs=[
            whole(x.shape),
            weight(0),
            weight(1),
            weight(0),
            pl.BlockSpec((vec.shape[0], step), lambda p: (0, p)),
            whole((length, 1)),
            whole((1, length)),
        ],
        out_specs=[part, part, part, part, pl.BlockSpec((heads, count, BLOCK, 3 * BLOCK), lambda p: (p, 0, 0, 0))],
        out_shape=[shape_of((length, width), BF)] * 4 + [shape_of((HEADS, count, BLOCK, 3 * BLOCK), BF)],
        scratch_shapes=[pltpu.VMEM((count, BLOCK, 3 * BLOCK), F32)],
        name="attend",
    )(x, query_key, query_key, value_output, vec, segments, segments_row)


def norm_parts(values):
    center = values - jnp.mean(values, axis=1, keepdims=True)
    scale = lax.rsqrt(jnp.mean(center * center, axis=1, keepdims=True) + 1e-12)
    return center * scale, scale


def norm_back(spread_grad, hat, scale):
    return scale * (
        spread_grad
        - jnp.mean(spread_grad, axis=1, keepdims=True)
        - hat * jnp.mean(spread_grad * hat, axis=1, keepdims=True)
    )


def chunk_mask(w, rows):
    lane = lax.broadcasted_iota(jnp.int32, (rows, 2 * BLOCK), 1)
    start = HEAD_DIM * (w % 2)
    return (lane >= start) & (lane < start + 3 * HEAD_DIM)


def window_at(w):
    return w + w // 2


def first_kernel(x, att_a, att_b, wo_a, wo_b, vec, hat_o, scale_o, normed_o, normed_t_o, second_o, x_t_o, branch):
    w = pl.program_id(0)

    @pl.when(w == 0)
    def _():
        branch[...] = x[...].astype(F32) + vec[2:3, :]
        x_t_o[...] = x[...].T

    kept = jnp.where(chunk_mask(w, x.shape[0]), jnp.concatenate([att_a[...], att_b[...]], axis=1).astype(F32), 0.0)
    weight = jnp.concatenate([wo_a[...], wo_b[...]], axis=1)
    first = branch[...] + matmul_last(kept.astype(BF), weight)
    branch[...] = first
    hat, scale = norm_parts(first)
    hat_o[0] = hat.astype(BF)
    scale_o[0] = scale
    normed = hat * vec[3:4, :] + vec[4:5, :]
    second_o[0] = normed + vec[5:6, :]
    low = normed.astype(BF)
    normed_o[0] = low
    normed_t_o[0] = low.T


def first_norm(x, att, weights, vec):
    length, width = x.shape
    base = width // BLOCK
    per_width = pl.BlockSpec((1, length, width), lambda w: (w, 0, 0))
    return call(
        first_kernel,
        LIMIT,
        9.7,
        grid=(WIDTHS,),
        in_specs=[
            whole(x.shape),
            pl.BlockSpec((length, BLOCK), lambda w: (0, window_at(w))),
            pl.BlockSpec((length, BLOCK), lambda w: (0, window_at(w) + 1)),
            pl.BlockSpec((width, BLOCK), lambda w: (0, base + window_at(w))),
            pl.BlockSpec((width, BLOCK), lambda w: (0, base + window_at(w) + 1)),
            whole(vec.shape),
        ],
        out_specs=[
            per_width,
            pl.BlockSpec((1, length, 1), lambda w: (w, 0, 0)),
            per_width,
            pl.BlockSpec((1, width, length), lambda w: (w, 0, 0)),
            per_width,
            whole((width, length)),
        ],
        out_shape=[
            shape_of((WIDTHS, length, width), BF),
            shape_of((WIDTHS, length, 1), F32),
            shape_of((WIDTHS, length, width), BF),
            shape_of((WIDTHS, width, length), BF),
            shape_of((WIDTHS, length, width), F32),
            shape_of((width, length), BF),
        ],
        scratch_shapes=[pltpu.VMEM((length, width), F32)],
        name="first_norm",
    )(x, att, att, weights, weights, vec)


ERF_T = 0.3275911 / math.sqrt(2.0)
BELL = 1.0 / math.sqrt(2.0 * math.pi)
ERF_A = tuple(
    0.5 * entry / BELL for entry in (0.254829592, -0.284496736, 1.421413741, -1.453152027, 1.061405429)
)
ROWS = 256


def gelu_pair(values):
    size = jnp.abs(values)
    bell = jnp.exp2(values * values * (-0.5 * math.log2(math.e)) + math.log2(BELL))
    below = 1.0 + ERF_T * size
    t = pl.reciprocal(below, approx=True)
    t = t * (2.0 - below * t)
    poly = ERF_A[4] * t + ERF_A[3]
    for entry in (ERF_A[2], ERF_A[1], ERF_A[0]):
        poly = poly * t + entry
    tail = poly * t * bell
    step = tail - size * bell
    return jnp.maximum(values, 0.0) - size * tail, jnp.where(values >= 0.0, 1.0 - step, step)


def feed_order(chunks):
    return [(j, w) for j in chunks for w in range(j, WIDTHS)]


def copy_of(source, target, sem):
    return pltpu.make_async_copy(source, target, sem)


def forward_step(normed, weights, bias, act, slope, second, column, between=()):
    length, width = normed.shape
    half = weights.shape[1] // 2
    between = list(between)
    for r in range(0, length, ROWS):
        rows = slice(r, r + ROWS)
        inner = matmul(normed[rows, :], weights[:, pl.ds(column, width)]) + bias
        if between:
            between.pop(0)()
        active, tilt = gelu_pair(inner)
        active = active.astype(BF)
        act[rows, :] = active
        slope[rows, :] = tilt.astype(BF)
        second[rows, :] += matmul_last(active, weights[:, pl.ds(half + column, width)])
    for work in between:
        work()


def second_norm(second, og, vec, out, feed, feed_t, sums):
    hat, scale = norm_parts(second[...])
    out[...] = (hat * vec[6:7, :] + vec[7:8, :]).astype(BF)
    grad = og[...].astype(F32)
    sums[0:1, :] += jnp.sum(grad * hat, axis=0, keepdims=True)
    sums[1:2, :] += jnp.sum(grad, axis=0, keepdims=True)
    low = norm_back(grad * vec[6:7, :], hat, scale).astype(BF)
    feed[...] = low
    feed_t[...] = low.T
    sums[2:3, :] += jnp.sum(low.astype(F32), axis=0, keepdims=True)


def backward_parts(feed, feed_t, normed_t, act, slope, weights, column, outer, inner, grads, bias, fresh):
    length, width = feed.shape
    half = weights.shape[1] // 2
    lows = []

    def first():
        part = matmul(feed_t[...], act[...])
        outer[...] = part if fresh else outer[...] + part

    def middle(r):
        rows = slice(r, r + ROWS)
        raw = matmul(feed[rows, :], weights[:, pl.ds(half + column, width)])
        low = (slope[rows, :].astype(F32) * raw).astype(BF)
        bias[...] += jnp.sum(low.astype(F32), axis=0, keepdims=True)
        grads[rows, :] += matmul_last(low, weights[:, pl.ds(column, width)])
        lows.append(low)

    def last():
        part = matmul(normed_t[...], jnp.concatenate(lows, axis=0))
        inner[...] = part if fresh else inner[...] + part

    return [first] + [functools.partial(middle, r) for r in range(0, length, ROWS)] + [last]


def backward_step(feed, feed_t, normed_t, act, slope, weights, column, outer, inner, grads, bias, fresh, ready=None):
    first, *others = backward_parts(
        feed, feed_t, normed_t, act, slope, weights, column, outer, inner, grads, bias, fresh
    )
    first()
    if ready is not None:
        ready()
    for work in others:
        work()


ANY = pl.BlockSpec(memory_space=pl.ANY)
SCALARS = pl.BlockSpec(memory_space=pltpu.SMEM)


def held(array):
    return pl.BlockSpec(memory_space=pltpu.VMEM)


def give_halves(core, outer, inner, mine_h, other_h, sem):
    @pl.when(core == 0)
    def _():
        copy_of(outer, mine_h, sem).start()
        copy_of(inner, other_h, sem).start()

    @pl.when(core != 0)
    def _():
        copy_of(inner, mine_h, sem).start()
        copy_of(outer, other_h, sem).start()

    return [copy_of(outer, mine_h, sem), copy_of(inner, other_h, sem)]


def feed_high_kernel(sources, table, table_b, bi, vec, normed_h, second_h, og_h, normed_t_h, *refs):
    source, count, last = sources[0], len(sources[0].arrays), len(sources[1].arrays)
    pieces, pieces_b, refs = refs[:count], refs[count : count + last], refs[count + last :]
    act_h, slope_h, act_1_h, slope_1_h, out_h, feed_h, feed_t_h, mine_h, other_h, grad_h, bias, sums = refs[:12]
    weights, normed, second, og, normed_t, act, slope, feed, feed_t, outer, inner, outer_b, inner_b = refs[12:25]
    sem_w, sem_n, sem_act, sem_out, sem_give = refs[25:]
    width = normed.shape[2]
    low = WIDTHS - 2

    def rows_of(n):
        return (
            copy_of(normed_h.at[low + n], normed.at[n], sem_n.at[0, n]),
            copy_of(second_h.at[low + n], second.at[n], sem_n.at[1, n]),
            copy_of(og_h.at[low + n], og.at[n], sem_n.at[2, n]),
            copy_of(normed_t_h.at[low + n], normed_t.at[n], sem_n.at[3, n]),
        )

    for copy in rows_of(1)[:2]:
        copy.start()
    for j in range(WIDTHS):
        part = width if j < WIDTHS - 1 else width // 2
        source.start(table, pieces, weights, sem_w.at[j], j * width, part, j * width)
        if part < width:
            sources[1].start(table_b, pieces_b, weights, sem_w.at[j], 0, width - part, j * width + part)
    for copy in rows_of(1)[2:] + rows_of(0):
        copy.start()
    sums[...] = jnp.zeros_like(sums)
    bias[...] = jnp.zeros_like(bias)
    for copy in rows_of(1)[:2]:
        copy.wait()
    writes = []

    def norm(n):
        w, base = low + n, 4 * (1 - n)
        writes.extend(
            (
                copy_of(act.at[base], act_h.at[w], sem_act.at[n, 0]),
                copy_of(slope.at[base], slope_h.at[w], sem_act.at[n, 1]),
                copy_of(act.at[base + 1], act_1_h.at[n], sem_act.at[n, 2]),
                copy_of(slope.at[base + 1], slope_1_h.at[n], sem_act.at[n, 3]),
            )
        )
        second_norm(second.at[n], og.at[n], vec, normed.at[n], feed.at[n], feed_t.at[n], sums)
        writes.extend(
            (
                copy_of(normed.at[n], out_h.at[w], sem_out.at[0, n]),
                copy_of(feed.at[n], feed_h.at[w], sem_out.at[1, n]),
                copy_of(feed_t.at[n], feed_t_h.at[w], sem_out.at[2, n]),
            )
        )
        for copy in writes[-7:]:
            copy.start()
        second[n] = feed[n].astype(F32)

    def back(m, n, at):
        return backward_parts(
            feed.at[m], feed_t.at[m], normed_t.at[m], act.at[at], slope.at[at], weights, (low + n) * width,
            outer, inner, second.at[m], bias.at[n], m == n,
        )

    def give(n):
        outer_b[n] = outer[...].astype(BF)
        inner_b[n] = inner[...].astype(BF)
        columns = pl.ds(n * width, width)
        return give_halves(
            table[source.core], outer_b.at[n], inner_b.at[n], mine_h.at[:, columns], other_h.at[:, columns], sem_give.at[n]
        )

    for j in range(WIDTHS):
        if j < 2:
            source.wait(weights, sem_w.at[j], width, j * width)
        if j == 2:
            for later in (2, 3):
                source.wait(weights, sem_w.at[later], width, later * width)
            for copy in rows_of(1)[2:] + rows_of(0):
                copy.wait()
        forward_step(normed.at[1], weights, bi[j], act.at[j], slope.at[j], second.at[1], j * width)
    norm(1)
    beside = back(1, 1, 3)
    for j in range(WIDTHS - 1):
        take = 2 if j < 2 else 0
        forward_step(
            normed.at[0], weights, bi[j], act.at[4 + j], slope.at[4 + j], second.at[0], j * width, beside[:take]
        )
        beside = beside[take:]
    given = give(1)
    norm(0)
    for work in back(0, 0, 6) + back(1, 0, 2):
        work()
    given += give(0)
    end = copy_of(second, grad_h, sem_out.at[3, 0])
    end.start()
    for copy in writes + given + [end]:
        copy.wait()


def feed_high(sources, normed, bi, second, og, vec, normed_t):
    _, length, width = normed.shape
    four, four_t = (WIDTHS, length, width), (WIDTHS, width, length)
    two, two_t = (2, length, width), (2, width, length)
    slots = 7
    return call(
        functools.partial(feed_high_kernel, sources),
        LIMIT,
        35,
        in_specs=[SCALARS, SCALARS, held(bi), held(vec)]
        + [ANY] * (4 + len(sources[0].arrays) + len(sources[1].arrays)),
        out_specs=[ANY] * 10 + [held(vec), held(vec)],
        out_shape=[
            shape_of(four, BF),
            shape_of(four, BF),
            shape_of(two, BF),
            shape_of(two, BF),
            shape_of(four, BF),
            shape_of(four, BF),
            shape_of(four_t, BF),
            shape_of((width, 2 * width), BF),
            shape_of((width, 2 * width), BF),
            shape_of(two, F32),
            shape_of((2, 1, width), F32),
            shape_of((8, width), F32),
        ],
        scratch_shapes=[
            pltpu.VMEM((width, 8 * width), BF),
            pltpu.VMEM(two, BF),
            pltpu.VMEM(two, F32),
            pltpu.VMEM(two, BF),
            pltpu.VMEM(two_t, BF),
            pltpu.VMEM((slots, length, width), BF),
            pltpu.VMEM((slots, length, width), BF),
            pltpu.VMEM(two, BF),
            pltpu.VMEM(two_t, BF),
            pltpu.VMEM((width, width), F32),
            pltpu.VMEM((width, width), F32),
            pltpu.VMEM((2, width, width), BF),
            pltpu.VMEM((2, width, width), BF),
            pltpu.SemaphoreType.DMA((WIDTHS, 2)),
            pltpu.SemaphoreType.DMA((4, 2)),
            pltpu.SemaphoreType.DMA((2, 4)),
            pltpu.SemaphoreType.DMA((4, 2)),
            pltpu.SemaphoreType.DMA((2,)),
        ],
        name="feed_high",
    )(
        sources[0].table, sources[1].table, bi, vec, normed, second, og, normed_t, *sources[0].arrays, *sources[1].arrays
    )


def feed_mid_kernel(source, table, bi, vec, normed_h, second_h, og_h, normed_t_h, act_1_h, slope_1_h, grad_in, feed_in, feed_t_in, *refs):
    count = len(source.arrays)
    pieces, refs = refs[:count], refs[count + 3 :]
    act_h, slope_h, out_h, feed_h, feed_t_h, mine_h, other_h, grad_h, bias, sums = refs[:10]
    weights, normed, second, og, normed_t, act, slope, feed, feed_t, grads, outer, inner, outer_b, inner_b = refs[10:24]
    sem_w, sem_n, sem_b, sem_act, sem_out, sem_give = refs[24:]
    width = normed.shape[2]

    def rows_of(w):
        return (
            copy_of(normed_h.at[w], normed.at[w], sem_n.at[0, w]),
            copy_of(second_h.at[w], second.at[w], sem_n.at[1, w]),
            copy_of(og_h.at[w], og.at[w], sem_n.at[2, w]),
        )

    def back_rows(m):
        return (
            copy_of(feed_t_in.at[2 + m], feed_t.at[2 + m], sem_b.at[0, m]),
            copy_of(act_1_h.at[m], act.at[1 + m], sem_b.at[1, m]),
            copy_of(feed_in.at[2 + m], feed.at[2 + m], sem_b.at[2, m]),
            copy_of(slope_1_h.at[m], slope.at[1 + m], sem_b.at[3, m]),
            copy_of(grad_in.at[m], grads.at[1 + m], sem_b.at[4, m]),
        )

    turned = [copy_of(normed_t_h.at[w], normed_t.at[w - 1], sem_n.at[3, w - 1]) for w in range(1, WIDTHS)]
    for copy in rows_of(1)[:2]:
        copy.start()
    for j in range(2):
        source.start(table, pieces, weights, sem_w.at[j], j * width, width, j * width)
    for copy in rows_of(1)[2:] + rows_of(0) + (turned[0],) + back_rows(0) + (turned[1],) + back_rows(1) + (turned[2],):
        copy.start()
    sums[...] = jnp.zeros_like(sums)
    bias[...] = jnp.zeros_like(bias)
    for copy in rows_of(1)[:2]:
        copy.wait()

    def back(m, fresh):
        return backward_parts(
            feed.at[1 + m], feed_t.at[1 + m], normed_t.at[m], act.at[m], slope.at[m], weights, width,
            outer, inner, grads.at[m], bias.at[0], fresh,
        )

    def forward(w, j, between=()):
        at = 0 if j == 1 else 3 + w
        forward_step(normed.at[w], weights, bi[j], act.at[at], slope.at[at], second.at[w], j * width, between)

    source.wait(weights, sem_w.at[0], width, 0)
    forward(1, 0)
    source.wait(weights, sem_w.at[1], width, width)
    for copy in rows_of(1)[2:] + rows_of(0):
        copy.wait()
    forward(1, 1)
    for copy in turned + [copy for m in range(2) for copy in back_rows(m)]:
        copy.wait()
    beside = back(1, True) + back(2, False)
    second_norm(second.at[1], og.at[1], vec, normed.at[1], feed.at[1], feed_t.at[1], sums)
    forward(0, 0, beside[:4])
    second_norm(second.at[0], og.at[0], vec, normed.at[0], feed.at[0], feed_t.at[0], sums)
    grads[0] = feed[1].astype(F32)
    writes = []
    for w in (1, 0):
        writes += [
            copy_of(act.at[3 + w], act_h.at[w], sem_act.at[0, w]),
            copy_of(slope.at[3 + w], slope_h.at[w], sem_act.at[1, w]),
            copy_of(normed.at[w], out_h.at[w], sem_out.at[0, w]),
            copy_of(feed.at[w], feed_h.at[w], sem_out.at[1, w]),
            copy_of(feed_t.at[w], feed_t_h.at[w], sem_out.at[2, w]),
        ]
    writes += [copy_of(grads.at[m], grad_h.at[m], sem_out.at[3, m]) for m in range(WIDTHS - 1)]
    for copy in writes[:10] + writes[11:12]:
        copy.start()
    for work in beside[4:]:
        work()
    writes[12].start()
    for work in back(0, False):
        work()
    writes[10].start()
    outer_b[...] = outer[...].astype(BF)
    inner_b[...] = inner[...].astype(BF)
    writes += give_halves(table[source.core], outer_b, inner_b, mine_h, other_h, sem_give)
    for copy in writes:
        copy.wait()


def feed_mid(source, normed, bi, second, og, vec, normed_t, act_1, slope_1, grad, act, slope, out, feed, feed_t):
    _, length, width = normed.shape
    four, four_t = (WIDTHS, length, width), (WIDTHS, width, length)
    two = (2, length, width)
    many = WIDTHS - 1
    first = 12 + len(source.arrays)
    return call(
        functools.partial(feed_mid_kernel, source),
        LIMIT,
        22,
        in_specs=[SCALARS, held(bi), held(vec)] + [ANY] * (9 + len(source.arrays) + 3),
        out_specs=[ANY] * 8 + [held(vec), held(vec)],
        out_shape=[
            shape_of(four, BF),
            shape_of(four, BF),
            shape_of(four, BF),
            shape_of(four, BF),
            shape_of(four_t, BF),
            shape_of((width, width), BF),
            shape_of((width, width), BF),
            shape_of((many, length, width), F32),
            shape_of((1, 1, width), F32),
            shape_of((8, width), F32),
        ],
        scratch_shapes=[
            pltpu.VMEM((width, 4 * width), BF),
            pltpu.VMEM(two, BF),
            pltpu.VMEM(two, F32),
            pltpu.VMEM(two, BF),
            pltpu.VMEM((many, width, length), BF),
            pltpu.VMEM((5, length, width), BF),
            pltpu.VMEM((5, length, width), BF),
            pltpu.VMEM(four, BF),
            pltpu.VMEM(four_t, BF),
            pltpu.VMEM((many, length, width), F32),
            pltpu.VMEM((width, width), F32),
            pltpu.VMEM((width, width), F32),
            pltpu.VMEM((width, width), BF),
            pltpu.VMEM((width, width), BF),
            pltpu.SemaphoreType.DMA((2, 2)),
            pltpu.SemaphoreType.DMA((4, many)),
            pltpu.SemaphoreType.DMA((5, 2)),
            pltpu.SemaphoreType.DMA((2, 2)),
            pltpu.SemaphoreType.DMA((4, many)),
            pltpu.SemaphoreType.DMA,
        ],
        input_output_aliases={10: 3, 11: 4, first: 0, first + 1: 1, first + 2: 2},
        name="feed_mid",
    )(source.table, bi, vec, normed, second, og, normed_t, act_1, slope_1, grad, feed, feed_t, *source.arrays, act, slope, out)


def feed_zero_kernel(source, table, vec, feed_h, feed_t_h, normed_t_h, act_h, slope_h, grad_in, hat_h, scale_h, att_h, wo_h, *refs):
    count = len(source.arrays)
    pieces, refs = refs[:count], refs[count:]
    mine_h, other_h, first_g_h, att_g_h, wo_g_h, bias, sums = refs[:7]
    weights, feed, feed_t, normed_t, act, slope, outer, inner, grads, outer_b, inner_b = refs[7:18]
    hat, scale, att, wo, att_g, total, wo_g, wo_g_b = refs[18:26]
    sem_w, sem_in, sem_g, sem_x, sem_out = refs[26:]
    length, width = feed.shape[1:]
    def reads(w):
        return (
            copy_of(feed_t_h.at[w], feed_t.at[w], sem_in.at[0, w]),
            copy_of(act_h.at[w], act.at[w], sem_in.at[1, w]),
            copy_of(feed_h.at[w], feed.at[w], sem_in.at[2, w]),
            copy_of(slope_h.at[w], slope.at[w], sem_in.at[3, w]),
            copy_of(normed_t_h.at[w], normed_t.at[w], sem_in.at[4, w]),
            copy_of(hat_h.at[w], hat.at[w], sem_in.at[5, w]),
            copy_of(scale_h.at[w], scale.at[w], sem_in.at[6, w]),
        )

    for w in reversed(range(WIDTHS)):
        for copy in reads(w)[:5]:
            copy.start()
        if w == WIDTHS - 1:
            source.start(table, pieces, weights, sem_w, 0, width, 0)
        if w > 0:
            copy_of(grad_in.at[w - 1], grads.at[w], sem_g.at[w]).start()
        if w == WIDTHS - 1:
            beside = (copy_of(att_h, att, sem_x.at[0]), copy_of(wo_h.at[:, pl.ds(width, width)], wo, sem_x.at[1]))
            for copy in beside:
                copy.start()
        for copy in reads(w)[5:]:
            copy.start()
    bias[...] = jnp.zeros_like(bias)
    sums[...] = jnp.zeros_like(sums)
    total[...] = jnp.zeros_like(total)
    wo_g[...] = jnp.zeros_like(wo_g)

    for w in reversed(range(WIDTHS)):
        if w == WIDTHS - 1:
            for copy in reads(w)[:2]:
                copy.wait()

        def ready(w=w):
            for copy in reads(w)[2:] + (reads(w - 1)[:2] if w else ()) + (beside if w == WIDTHS - 1 else ()):
                copy.wait()
            if w == WIDTHS - 1:
                source.wait(weights, sem_w, width, 0)
            if w == 0:
                grads[0] = feed[0].astype(F32)
            else:
                copy_of(grad_in.at[w - 1], grads.at[w], sem_g.at[w]).wait()

        backward_step(
            feed.at[w], feed_t.at[w], normed_t.at[w], act.at[w], slope.at[w], weights, 0, outer, inner, grads.at[w],
            bias.at[0], w == WIDTHS - 1, ready,
        )
        rough, factor = hat[w].astype(F32), scale[w]
        grad = grads[w]
        sums[0:1, :] += jnp.sum(grad * rough, axis=0, keepdims=True)
        sums[1:2, :] += jnp.sum(grad, axis=0, keepdims=True)
        first_g = norm_back(grad * vec[3:4, :], rough, factor)
        grads[w] = first_g
        copy_of(grads.at[w], first_g_h.at[w], sem_out.at[0]).start()
        low = first_g.astype(BF)
        wide = low.astype(F32)
        sums[2:3, :] += jnp.sum(wide, axis=0, keepdims=True)
        total[...] += wide
        kept = (w + 1) * 3 * HEAD_DIM
        columns = -(-kept // BLOCK) * BLOCK
        found = matmul(low, wo[:, :columns])
        if columns > kept:
            lane = lax.broadcasted_iota(jnp.int32, (length, columns), 1)
            found = jnp.where(lane < kept, found, 0.0)
        att_g[w, :, :columns] = found.astype(BF)
        if columns < width:
            att_g[w, :, columns:] = jnp.zeros((length, width - columns), BF)
        copy_of(att_g.at[w], att_g_h.at[w], sem_out.at[1]).start()
        start = BLOCK * window_at(w)
        part = jnp.where(chunk_mask(w, length), att[:, start : start + 2 * BLOCK].astype(F32), 0.0).astype(BF)
        wo_g[:, start : start + 2 * BLOCK] += matmul(total[...].astype(BF).T, part)
    outer_b[...] = outer[...].astype(BF)
    inner_b[...] = inner[...].astype(BF)
    writes = give_halves(table[source.core], outer_b, inner_b, mine_h, other_h, sem_out.at[2])
    wo_g_b[...] = wo_g[...].astype(BF)
    copy = copy_of(wo_g_b, wo_g_h, sem_out.at[2])
    copy.start()
    for copy in writes + [copy, copy_of(grads, first_g_h, sem_out.at[0]), copy_of(att_g, att_g_h, sem_out.at[1])]:
        copy.wait()


def feed_zero(source, vec, feed, feed_t, normed_t, act, slope, grad, hat, scale, att, wo):
    _, length, width = feed.shape
    four, four_t = (WIDTHS, length, width), (WIDTHS, width, length)
    return call(
        functools.partial(feed_zero_kernel, source),
        LIMIT,
        28,
        in_specs=[SCALARS, held(vec)] + [ANY] * (10 + len(source.arrays)),
        out_specs=[ANY] * 5 + [held(vec), held(vec)],
        out_shape=[
            shape_of((width, width), BF),
            shape_of((width, width), BF),
            shape_of(four, F32),
            shape_of(four, BF),
            shape_of((width, width), BF),
            shape_of((1, 1, width), F32),
            shape_of((8, width), F32),
        ],
        scratch_shapes=[
            pltpu.VMEM((width, 2 * width), BF),
            pltpu.VMEM(four, BF),
            pltpu.VMEM(four_t, BF),
            pltpu.VMEM(four_t, BF),
            pltpu.VMEM(four, BF),
            pltpu.VMEM(four, BF),
            pltpu.VMEM((width, width), F32),
            pltpu.VMEM((width, width), F32),
            pltpu.VMEM(four, F32),
            pltpu.VMEM((width, width), BF),
            pltpu.VMEM((width, width), BF),
            pltpu.VMEM(four, BF),
            pltpu.VMEM((WIDTHS, length, 1), F32),
            pltpu.VMEM((length, width), BF),
            pltpu.VMEM((width, width), BF),
            pltpu.VMEM(four, BF),
            pltpu.VMEM((length, width), F32),
            pltpu.VMEM((width, width), F32),
            pltpu.VMEM((width, width), BF),
            pltpu.SemaphoreType.DMA((2,)),
            pltpu.SemaphoreType.DMA((7, WIDTHS)),
            pltpu.SemaphoreType.DMA((WIDTHS,)),
            pltpu.SemaphoreType.DMA((2,)),
            pltpu.SemaphoreType.DMA((3,)),
        ],
        name="feed_zero",
    )(source.table, vec, feed, feed_t, normed_t, act, slope, grad, hat, scale, att, wo, *source.arrays)


def attend_back_kernel(first_pair, pairs, own, core, x_t, wo_g, q, k, v, p, g, *refs):
    dq_o, dk_o, dv_o, mine_o, other_o, sums_o, dk_t, dv_t = refs
    step = pl.program_id(0)
    pair = first_pair + step
    columns = pairs * BLOCK
    length = q.shape[0]
    spans = windows(length)
    factor = 1.0 / math.sqrt(HEAD_DIM)
    lane = lax.broadcasted_iota(jnp.int32, (BLOCK, BLOCK), 1)
    low_half = lane < HEAD_DIM
    masks = (
        jnp.where(low_half, 1.0, 0.0).astype(BF),
        jnp.where(low_half, 0.0, 1.0).astype(BF),
    )

    def run(first):
        widths = list(range(first, WIDTHS))
        many = len(widths)
        dk_t[...] = jnp.zeros_like(dk_t)
        dv_t[...] = jnp.zeros_like(dv_t)
        q_t = (q[...] * jnp.asarray(factor, BF)).T
        g_t = [g[w].T for w in widths]
        mask = jnp.concatenate([masks[0]] * many + [masks[1]] * many, axis=0)
        wide = jnp.concatenate([low_half] * many, axis=0)
        chance_g = []
        for i, (start, span) in enumerate(spans):
            g_here = jnp.concatenate([g[w, i * BLOCK : (i + 1) * BLOCK, :] for w in widths], axis=0)
            chance_g.append(matmul_last(jnp.concatenate([g_here, g_here], axis=0) * mask, v[start : start + span, :]))
        scores_g = []
        for i, (start, span) in enumerate(spans):
            lows = []
            for half in range(2):
                chances = p[half, i, :, :span].astype(F32)
                for n in range(many):
                    at = (half * many + n) * BLOCK
                    product = chances * chance_g[i][at : at + BLOCK, :]
                    row = jnp.sum(product, axis=1, keepdims=True)
                    lows.append((product - chances * row).astype(BF))
            scores_g.append(lows)
        for i, (start, span) in enumerate(spans):
            here = slice(i * BLOCK, (i + 1) * BLOCK)
            near = slice(start, start + span)
            lows = scores_g[i]
            found = matmul(jnp.concatenate(lows, axis=0), k[near, :] * jnp.asarray(factor, BF))
            dq = jnp.where(wide, found[: many * BLOCK], found[many * BLOCK :]).astype(BF)
            for n, w in enumerate(widths):
                dq_o[w, here, :] = dq[n * BLOCK : (n + 1) * BLOCK, :]
            for half in range(2):
                rows_of = slice(half * HEAD_DIM, (half + 1) * HEAD_DIM)
                for n, w in enumerate(widths):
                    dk_t[w, rows_of, near] += matmul(q_t[rows_of, here], lows[half * many + n])
                stacked = jnp.concatenate([g_t[n][rows_of, here] for n in range(many)], axis=0)
                values_g = matmul(stacked, p[half, i, :, :span])
                for n, w in enumerate(widths):
                    dv_t[w, rows_of, near] += values_g[n * HEAD_DIM : (n + 1) * HEAD_DIM, :]
        totals = [jnp.zeros((length, BLOCK), F32) for _ in range(3)]
        for w in range(WIDTHS):
            if w < first:
                for ref in (dq_o, dk_o, dv_o):
                    ref[w] = jnp.zeros((length, BLOCK), BF)
                continue
            dk_o[w] = dk_t[w].astype(BF).T
            dv_o[w] = dv_t[w].astype(BF).T
            for n, ref in enumerate((dq_o, dk_o, dv_o)):
                totals[n] += ref[w].astype(F32)
        here = pl.ds(pl.multiple_of(step * BLOCK, BLOCK), BLOCK)
        beside = pl.ds(pl.multiple_of(columns + step * BLOCK, BLOCK), BLOCK)
        sums_o[0:1, here] = jnp.sum(totals[0], axis=0, keepdims=True)
        sums_o[1:2, here] = jnp.sum(totals[2], axis=0, keepdims=True)
        parts = [matmul(x_t[...], total.astype(BF)).astype(BF) for total in totals]

        def fill(first, second):
            first[:, here] = parts[0]
            first[:, beside] = parts[1]
            second[:, here] = parts[2]
            second[:, beside] = wo_g[...]

        pl.when(core[0] == 0)(lambda: fill(mine_o, other_o))
        pl.when(core[0] != 0)(lambda: fill(other_o, mine_o))

    heads_each = HEADS // WIDTHS
    firsts = [(2 * n) // heads_each for n in range(HEADS // 2)]
    for first in sorted(set(firsts)):
        members = [n for n, f in enumerate(firsts) if f == first and first_pair <= n < first_pair + pairs]
        if not members:
            continue

        @pl.when((pair >= members[0]) & (pair <= members[-1]))
        def _(first=first):
            run(first)


def vector_rows(own, sums_o, given):
    sums_c, sums_a, sums_b, sums_b2, bias_0, bias_1, bias_hi = given
    width = sums_a.shape[1]
    rows = [
        jnp.concatenate([sums_c[0:1, :], sums_o[0:1, :]], axis=1),
        jnp.concatenate([sums_c[1:2, :], sums_o[1:2, :]], axis=1),
        sums_a[2:3, :],
        sums_a[0:1, :],
        sums_a[1:2, :],
        sums_b[2:3, :] + sums_b2[2:3, :],
        sums_b[0:1, :] + sums_b2[0:1, :],
        sums_b[1:2, :] + sums_b2[1:2, :],
        jnp.zeros((8, width), F32),
    ]
    for j in range(WIDTHS):
        rows += [(bias_0[0], bias_1[0], bias_hi[0], bias_hi[1])[j]] * WIDTHS
    rows.append(jnp.zeros((BLOCK - 16 - WIDTHS * WIDTHS, width), F32))
    turned = jnp.concatenate(rows, axis=0).T
    lane = lax.broadcasted_iota(jnp.int32, (own, BLOCK), 1)
    blocks = []
    each = width // (own * WIDTHS)
    for j in range(WIDTHS):
        for n in range(each):
            at = (j * each + n) * own
            block = jnp.where(lane < 8, turned[at : at + own, :], 0.0)
            for m in range(WIDTHS):
                start = (n * WIDTHS + m) * own
                block = jnp.where(lane == 16 + WIDTHS * j + m, turned[start : start + own, :], block)
            blocks.append(block.astype(BF))
    return jnp.concatenate(blocks, axis=0)


def attend_back_last_kernel(first_pair, pairs, own, *refs):
    given, rest = refs[8:-8], refs[-8:]
    attend_back_kernel(first_pair, pairs, own, *refs[:8], *rest)
    if given:
        mine_o, other_o, sums_o = rest[3:6]

        @pl.when(pl.program_id(0) == pairs - 1)
        def _():
            block = vector_rows(own, sums_o, given)
            mine_o[:, 2 * pairs * BLOCK :] = block
            other_o[:, 2 * pairs * BLOCK :] = block


def attend_backward(core, first_pair, pairs, own, x_t, wo_g, q, k, v, p, g, given):
    length, width = q.shape
    columns = pairs * BLOCK
    part = pl.BlockSpec((length, BLOCK), lambda n: (0, first_pair + n))
    wide = pl.BlockSpec((WIDTHS, length, BLOCK), lambda n: (0, 0, first_pair + n))
    wide_o = pl.BlockSpec((WIDTHS, length, BLOCK), lambda n: (0, 0, n))
    out = (width, 2 * columns + (BLOCK if given else 0))
    return call(
        functools.partial(attend_back_last_kernel, first_pair, pairs, own),
        LIMIT,
        12,
        grid=(pairs,),
        in_specs=[
            SCALARS,
            whole(x_t.shape),
            pl.BlockSpec((width, BLOCK), lambda n: (0, first_pair + n)),
            part,
            part,
            part,
            pl.BlockSpec((2,) + p.shape[1:], lambda n: (first_pair + n, 0, 0, 0)),
            wide,
        ]
        + [whole(entry.shape) for entry in given],
        out_specs=[wide_o] * 3 + [whole(out)] * 2 + [whole((8, columns))],
        out_shape=[shape_of((WIDTHS, length, columns), BF)] * 3
        + [shape_of(out, BF)] * 2
        + [shape_of((8, columns), F32)],
        scratch_shapes=[pltpu.VMEM((WIDTHS, BLOCK, length), F32)] * 2,
        name="attend_backward",
    )(jnp.full((1,), core, jnp.int32), x_t, wo_g, q, k, v, p, g, *given)


def input_kernel(some, first_g, dq_a, dk_a, dv_a, dq_b, dk_b, dv_b, wq, wk, wv, *refs):
    out = refs[-1]
    w = pl.program_id(0)
    split = dq_a.shape[2]
    for section in some:
        kept = -(-(section + 1) * 3 * HEAD_DIM // BLOCK) * BLOCK

        @pl.when(w == section - some[0])
        def _():
            total = first_g[0]
            for low, high, weight in ((dq_a, dq_b, wq), (dk_a, dk_b, wk), (dv_a, dv_b, wv)):
                near = min(kept, split)
                total += matmul_last(low[0, :, :near], weight[:, :near])
                if kept > split:
                    total += matmul_last(high[0, :, : kept - split], weight[:, split:kept])
            out[0] = total


def input_grads(some, first_g, low, high, query_key, value_output, earlier):
    _, length, width = first_g.shape
    base = some[0]
    per_width = pl.BlockSpec((1, length, width), lambda w: (w + base, 0, 0))
    part = pl.BlockSpec((1, length, low[0].shape[2]), lambda w: (w + base, 0, 0))
    last = pl.BlockSpec((1, length, high[0].shape[2]), lambda w: (jnp.maximum(w + base, WIDTHS // 2), 0, 0))
    given = [] if earlier is None else [earlier]

    def weight(n):
        return pl.BlockSpec((width, width), lambda w: (0, n))

    return call(
        functools.partial(input_kernel, some),
        LIMIT,
        8,
        grid=(len(some),),
        in_specs=[per_width] + [part] * 3 + [last] * 3 + [weight(0), weight(1), weight(0)] + [ANY] * len(given),
        out_specs=per_width,
        out_shape=shape_of(first_g.shape, F32),
        input_output_aliases={10: 0} if given else {},
        name="input_grads",
    )(first_g, *low, *high, query_key, query_key, value_output, *given)


def tie(*values):
    return lax.optimization_barrier(values)


class Ring:
    def __init__(self, mesh):
        self.dp = mesh.shape["dp"]
        self.fsdp = mesh.shape["fsdp"]
        self.square = self.fsdp == 8 and self.dp == 4
        index = lax.axis_index("fsdp")
        self.z = lax.axis_index("dp")
        self.y, self.x, self.c = index // 4, (index // 2) % 2, index % 2

    def swap(self, value, bit):
        total = self.dp * self.fsdp
        return lax.ppermute(value, AXES, [(i, i ^ bit) for i in range(total)])

    def shift(self, value, by):
        total = self.dp * self.fsdp
        return lax.ppermute(value, AXES, [(i, (i + by * self.fsdp) % total) for i in range(total)])

    def along(self, value, bit):
        total = self.dp * self.fsdp
        return lax.ppermute(value, AXES, [(i, i ^ (bit * self.fsdp)) for i in range(total)])

    def mine(self, first, second):
        return jnp.where(self.c == 0, first, second)


CORE, X_SIDE, Y_SIDE = 1, 2, 4


class Gather:
    def __init__(self, ring, halves):
        self.ring, self.halves = ring, halves
        self.shard = halves
        self.line = self.came = self.sides = self.corners = self.crossed = ()
        self.copies, self.table = self.places() if ring.square else ([], jnp.asarray(ring.c, jnp.int32).reshape(1))

    def start_core(self):
        ring = self.ring
        if ring.square:
            kept, sent = ring.mine(*self.halves), ring.mine(*self.halves[::-1])
            came = ring.swap(sent, CORE)
            self.shard = ring.mine(jnp.concatenate([kept, came], axis=0), jnp.concatenate([came, kept], axis=0))

    def keep(self, other, most):
        if self.ring.square:
            self.shard, other.shard = self.shard[:, :most], self.shard[:, most:]
        else:
            self.halves = tuple(half[:, :most] for half in self.halves)

    def start_line(self, first=0, columns=None):
        ring = self.ring
        if ring.square:
            part = self.shard[:, first : self.shard.shape[1] if columns is None else first + columns]
            self.came += (tuple(ring.shift(part, by) for by in range(1, ring.dp)),)

    def ready_line(self):
        if self.ring.square:
            came = [jnp.concatenate(parts, axis=1) for parts in zip(*self.came)]
            self.line = jnp.stack([self.shard] + came)

    def start_sides(self):
        ring = self.ring
        if ring.square:
            self.sides = (ring.swap(self.line, X_SIDE), ring.swap(self.line, Y_SIDE))

    def start_corners(self):
        ring, half = self.ring, self.ring.dp // 2
        if ring.square:
            self.corners = (
                ring.swap(self.sides[0][:half], Y_SIDE),
                ring.swap(self.sides[1][half:], X_SIDE),
            )

    def cross(self, *values):
        if self.ring.square:
            self.crossed += tuple(self.ring.swap(value, CORE) for value in values)

    def places(self):
        ring, half = self.ring, self.ring.dp // 2
        rows = 2 * self.halves[0].shape[0]
        own = (
            (ring.dp, 0, ring.y, ring.x),
            (ring.dp, 0, ring.y, 1 - ring.x),
            (ring.dp, 0, 1 - ring.y, ring.x),
            (half, 0, 1 - ring.y, 1 - ring.x),
            (half, half, 1 - ring.y, 1 - ring.x),
        )
        copies, at = [], []
        for n, (count, behind, y, x) in enumerate(own):
            for index in range(count):
                z = (ring.z + ring.dp - behind - index) % ring.dp
                copies.append((n, index))
                at.append(jnp.asarray(rows * ((z * 2 + y) * 2 + x), jnp.int32))
        return copies, jnp.stack(at + [jnp.asarray(ring.c, jnp.int32)])

    def pieces(self):
        return [self.line, *self.sides, *self.corners, *self.crossed]

    def source(self):
        return Source(self)


class PlaneFirst(Gather):
    def start_plane(self):
        ring = self.ring
        if ring.square:
            row = jnp.stack([self.shard, ring.swap(self.shard, X_SIDE)])
            self.sides = (row, ring.swap(row, Y_SIDE))

    def ready_line(self):
        if self.ring.square:
            self.line = jnp.concatenate(self.sides)

    def start_line(self):
        ring = self.ring
        if ring.square:
            self.came = tuple(ring.shift(self.line, by) for by in range(1, ring.dp))

    def places(self):
        ring = self.ring
        rows = 2 * self.halves[0].shape[0]
        copies, at = [], []
        for behind in range(ring.dp):
            z = (ring.z + ring.dp - behind) % ring.dp
            for index, (y, x) in enumerate(
                ((ring.y, ring.x), (ring.y, 1 - ring.x), (1 - ring.y, ring.x), (1 - ring.y, 1 - ring.x))
            ):
                copies.append((behind, index))
                at.append(jnp.asarray(rows * ((z * 2 + y) * 2 + x), jnp.int32))
        return copies, jnp.stack(at + [jnp.asarray(ring.c, jnp.int32)])

    def pieces(self):
        return [self.line, *self.came, *self.crossed]


class Source:
    def __init__(self, gather):
        ring = gather.ring
        self.square = ring.square
        self.columns = gather.halves[0].shape[1]
        if ring.square:
            self.rows = gather.shard.shape[0]
            self.arrays = gather.pieces()
        else:
            self.rows = gather.halves[0].shape[0] * ring.dp * ring.fsdp
            self.arrays = [lax.all_gather(half, AXES, axis=0, tiled=True) for half in gather.halves]
        self.copies, self.table = gather.copies, gather.table
        self.core = len(self.copies)

    def start(self, table, pieces, target, sems, first, columns, to):
        apart = target.shape[1] // 2
        if not self.square:
            for half in range(2):
                pltpu.make_async_copy(
                    pieces[half].at[:, pl.ds(first, columns)],
                    target.at[:, pl.ds(half * apart + to, columns)],
                    sems.at[half],
                ).start()
            return
        core = table[self.core]
        many = len(pieces) // 2
        for side in range(2):
            half = core if side == 0 else 1 - core
            for n, (piece, index) in enumerate(self.copies):
                row = pl.multiple_of(table[n], 16)
                pltpu.make_async_copy(
                    pieces[side * many + piece].at[index, :, pl.ds(first, columns)],
                    target.at[pl.ds(row, self.rows), pl.ds(pl.multiple_of(half * apart + to, BLOCK), columns)],
                    sems.at[half],
                ).start()

    def wait(self, target, sems, columns, to):
        for half in range(2):
            whole_half = target.at[:, pl.ds(half * (target.shape[1] // 2) + to, columns)]
            pltpu.make_async_copy(whole_half, whole_half, sems.at[half]).wait()


def place_rows(source, layout, beside):
    count = len(source.arrays)
    rows = source.rows * max(len(source.copies), 1)

    def kernel(table, *refs):
        pieces, outs = refs[:count], refs[count : count + len(layout)]
        sem = refs[-1]
        if not source.square:
            copies = [
                pltpu.make_async_copy(pieces[half].at[:, pl.ds(first, columns)], outs[n], sem.at[0])
                for n, (half, first, columns) in enumerate(layout)
            ]
            for copy in copies:
                copy.start()
            for copy in copies:
                copy.wait()
            return
        many = count // 2
        core = table[source.core]
        parts = [(half, first, columns, outs[n], 0) for n, (half, first, columns) in enumerate(layout)]
        if beside is not None:
            vec, bi, block = refs[count + len(layout) : -1]
            parts.insert(0, (0, beside, BLOCK, block, 1))

        def run(own):
            copies = []
            for half, first, columns, out, which in parts:
                for m, (piece, index) in enumerate(source.copies):
                    row = pl.multiple_of(table[m], 16)
                    copies.append(
                        (
                            which,
                            pltpu.make_async_copy(
                                pieces[piece + (0 if half == own else many)].at[index, :, pl.ds(first, columns)],
                                out.at[pl.ds(row, source.rows), :],
                                sem.at[which],
                            ),
                        )
                    )
            for _, copy in copies:
                copy.start()
            for which, copy in copies:
                if which == 1:
                    copy.wait()
            if beside is not None:
                vector_columns(block, vec, bi)
            for which, copy in copies:
                if which == 0:
                    copy.wait()

        for own in range(2):
            pl.when(core == own)(functools.partial(run, own))

    more = ([], [], [])
    if beside is not None:
        more = (
            [pl.BlockSpec(memory_space=pltpu.VMEM)] * 2,
            [shape_of((8, rows), F32), shape_of((WIDTHS, 1, rows), F32)],
            [pltpu.VMEM((rows, BLOCK), BF)],
        )
    return call(
        kernel,
        LIMIT_PLACE,
        5,
        in_specs=[SCALARS] + [ANY] * count,
        out_specs=[pl.BlockSpec(memory_space=pltpu.VMEM)] * len(layout) + more[0],
        out_shape=[shape_of((rows, columns), BF) for *_, columns in layout] + more[1],
        scratch_shapes=more[2] + [pltpu.SemaphoreType.DMA((2,))],
        name="place_rows",
    )(source.table, *source.arrays)


def vector_columns(block, vec, bi):
    full = block[...].astype(F32)
    width = full.shape[0]
    vec[...] = full.T[:8, :]
    each = 8
    own = width // (each * WIDTHS)
    lane = lax.broadcasted_iota(jnp.int32, (own, BLOCK), 1)
    pieces = []
    for n in range(each):
        for m in range(WIDTHS):
            piece = jnp.zeros((own, BLOCK), F32)
            for j in range(WIDTHS):
                start = (j * each + n) * own
                piece = jnp.where(lane == 16 + WIDTHS * j + m, full[start : start + own, :], piece)
            pieces.append(piece)
    turned = jnp.concatenate(pieces, axis=0).T
    for j in range(WIDTHS):
        at = 16 + WIDTHS * j
        bi[j] = jnp.sum(turned[at : at + WIDTHS, :], axis=0, keepdims=True)


class Scatter:
    def __init__(self, ring, mine, other):
        self.ring, self.kept, self.other = ring, mine, other
        self.came = self.sides = self.leaving = self.far = self.near = self.own = ()

    def start_core(self):
        if self.ring.square:
            self.came = self.ring.swap(self.other, CORE)

    def block(self, y, x):
        dp = self.ring.dp

        def pick(value):
            value = value.reshape(dp, 2, 2, value.shape[0] // (4 * dp), value.shape[1])
            value = lax.dynamic_index_in_dim(value, y, 1, keepdims=False)
            return lax.dynamic_index_in_dim(value, x, 1, keepdims=False)

        return pick(self.kept).astype(F32) + pick(self.came).astype(F32)

    def ready_sides(self):
        ring = self.ring
        if ring.square:
            to_x = self.block(ring.y, 1 - ring.x).astype(BF)
            to_y = self.block(1 - ring.y, ring.x).astype(BF)
            corner = self.block(1 - ring.y, 1 - ring.x).astype(BF)
            self.leaving = (corner, to_x, to_y)

    def start_sides(self):
        ring = self.ring
        if ring.square:
            corner, to_x, to_y = self.leaving
            self.sides = (ring.swap(corner, X_SIDE | Y_SIDE), ring.swap(to_x, X_SIDE), ring.swap(to_y, Y_SIDE))

    def ready_far(self):
        ring = self.ring
        if ring.square:
            line = self.block(ring.y, ring.x)
            for side in self.sides:
                line = line + side.astype(F32)
            line = line.reshape(2, 2, *line.shape[1:])
            self.leaving = lax.dynamic_index_in_dim(line, 1 - ring.z // 2, 0, keepdims=False).astype(BF)
            self.own = lax.dynamic_index_in_dim(line, ring.z // 2, 0, keepdims=False)

    def start_far(self):
        if self.ring.square:
            self.far = self.ring.along(self.leaving, 2)

    def ready_near(self):
        ring = self.ring
        if ring.square:
            pair = self.own + self.far.astype(F32)
            self.leaving = lax.dynamic_index_in_dim(pair, 1 - ring.z % 2, 0, keepdims=False).astype(BF)
            self.own = lax.dynamic_index_in_dim(pair, ring.z % 2, 0, keepdims=False)

    def start_near(self):
        if self.ring.square:
            self.near = (self.ring.along(self.leaving, 1),)

    def ready_last(self):
        ring = self.ring
        if ring.square:
            line = self.block(ring.y, ring.x)
            for side in self.sides:
                line = line + side.astype(F32)
            low = line.astype(BF)
            self.own = lax.dynamic_index_in_dim(line, ring.z, 0, keepdims=False)
            self.leaving = tuple(
                lax.dynamic_index_in_dim(low, (ring.z + by) % ring.dp, 0, keepdims=False) for by in range(1, ring.dp)
            )

    def start_last(self):
        ring = self.ring
        if ring.square:
            self.near = tuple(ring.shift(value, by) for by, value in enumerate(self.leaving, 1))


def finish(ring, groups):
    if not ring.square:
        halves = (
            jnp.concatenate([ring.mine(group.kept, group.other) for group in groups], axis=1),
            jnp.concatenate([ring.mine(group.other, group.kept) for group in groups], axis=1),
        )
        return tuple(lax.psum_scatter(half.astype(F32), AXES, scatter_dimension=0, tiled=True) for half in halves)
    total = jnp.concatenate(
        [functools.reduce(lambda sum_, part: sum_ + part.astype(F32), group.near, group.own) for group in groups], axis=1
    )
    rows = total.shape[0] // 2
    kept, sent = ring.mine(total[:rows], total[rows:]), ring.mine(total[rows:], total[:rows])
    came = ring.swap(sent, CORE)
    return ring.mine(kept, came), ring.mine(came, kept)


def solution(mesh):
    rows_split = P(AXES, None)
    vector_split = P(AXES)

    def per_device(
        tokens,
        segment_ids,
        output_grad,
        query_weight,
        query_bias,
        key_weight,
        value_weight,
        value_bias,
        output_weight,
        output_bias,
        first_gain,
        first_shift,
        inner_weight,
        inner_bias,
        outer_weight,
        outer_bias,
        second_gain,
        second_shift,
    ):
        ring = Ring(mesh)
        devices = ring.dp * ring.fsdp
        width = tokens.shape[1]
        hidden = inner_weight.shape[1]
        own = query_bias.shape[0]
        half = hidden // 2
        singles = (query_bias, value_bias, output_bias, first_gain, first_shift, outer_bias, second_gain, second_shift)
        count = len(singles)
        beside = ring.square and own % 8 == 0
        columns = []
        if beside:
            row = lax.broadcasted_iota(jnp.int32, (BLOCK, own), 0)
            block = jnp.zeros((BLOCK, own), BF)
            for n, vector in enumerate(singles):
                block = jnp.where(row == n, vector[None], block)
            chunk = (ring.z * ring.fsdp + lax.axis_index("fsdp")) // (devices // WIDTHS)
            for n in range(WIDTHS):
                quarter = inner_bias[n * own : (n + 1) * own]
                block = jnp.where(row == 16 + WIDTHS * chunk + n, quarter[None], block)
            columns = [block.T]

        def side(*parts):
            return jnp.concatenate(parts, axis=1)

        one = Gather(ring, (side(query_weight, key_weight, *columns), side(value_weight, output_weight, *columns)))
        most = hidden - width // 2
        two = Gather(ring, (inner_weight, outer_weight))
        three = PlaneFirst(ring, (inner_weight[:, most:], outer_weight[:, most:]))
        pair = 2 * width
        one.start_core()
        one.shard, two.halves = tie(one.shard, two.halves)
        one.start_line()
        two.start_core()
        two.keep(three, most)
        three.start_plane()
        segments = segment_ids[0].reshape(-1, 1)
        one.came, two.shard, three.sides, segments, one.table, three.table = tie(
            one.came, two.shard, three.sides, segments, one.table, three.table
        )
        two.table = one.table
        one.ready_line()
        one.start_sides()
        two.start_line(0, most // 2)
        one.line, one.sides, two.came = tie(one.line, one.sides, two.came)
        one.start_corners()
        two.start_line(most // 2, most - most // 2)
        one.line, one.sides, one.corners, two.came = tie(one.line, one.sides, one.corners, two.came)
        one.cross(one.line, *one.sides, *one.corners)
        two.ready_line()
        two.start_sides()
        source_one = one.source()
        three.sides, _ = tie(three.sides, source_one.arrays)
        three.ready_line()
        three.start_line()
        query_key, value_output, *vectors = place_rows(source_one, ((0, 0, pair), (1, 0, pair)), pair if beside else None)
        if beside:
            vec, bi = vectors
        else:
            vec = jnp.stack([lax.all_gather(entry, AXES, tiled=True) for entry in singles]).astype(F32)
            bi = lax.all_gather(inner_bias, AXES, tiled=True).astype(F32).reshape(WIDTHS, 1, width)
        q, k, v, att, p = attend(tokens, query_key, value_output, vec, segments, segment_ids)
        att, two.line, two.sides, three.line, three.came = tie(att, two.line, two.sides, three.line, three.came)
        two.start_corners()
        two.cross(two.line, *two.sides)
        hat, scale, normed, normed_t, second, x_t = first_norm(tokens, att, value_output, vec)
        normed, two.corners, two.crossed, three.line, three.came = tie(
            normed, two.corners, two.crossed, three.line, three.came
        )
        two.cross(*two.corners)
        three.cross(three.line, *three.came)
        source_two = two.source()

        act, slope, act_1, slope_1, out, feed, feed_t, mine, other, grad, bias_hi, sums_b = feed_high(
            (source_two, three.source()), normed, bi, second, output_grad, vec, normed_t
        )
        high = Scatter(ring, mine, other)
        high.start_core()
        grad, high.came = tie(grad, high.came)
        high.ready_sides()
        grad, high.leaving = tie(grad, high.leaving)
        high.start_sides()
        act, slope, out, feed, feed_t, mine, other, grad, bias_1, sums_b2 = feed_mid(
            source_two, normed, bi, second, output_grad, vec, normed_t, act_1, slope_1, grad, act, slope, out, feed, feed_t
        )
        grad, other, high.sides = tie(grad, other, high.sides)

        mid = Scatter(ring, mine, other)
        mid.start_core()
        high.ready_far()
        mid.ready_sides()
        grad, mid.leaving, high.leaving = tie(grad, mid.leaving, high.leaving)
        mid.start_sides()
        high.start_far()
        mine, other, first_g, att_g, wo_g, bias_0, sums_a = feed_zero(
            source_two, vec, feed, feed_t, normed_t, act, slope, grad, hat, scale, att, value_output
        )
        att_g, other, mid.sides, high.far = tie(att_g, other, mid.sides, high.far)

        low = Scatter(ring, mine, other)
        low.start_core()
        high.ready_near()
        mid.ready_far()
        low.ready_sides()
        att_g, low.leaving, mid.leaving, high.leaving = tie(att_g, low.leaving, mid.leaving, high.leaving)
        low.start_sides()
        mid.start_far()
        high.start_near()
        pairs = HEADS // 4
        *low_g, mine, other, sums_c = attend_backward(ring.c, 0, pairs, own, x_t, wo_g, q, k, v, p, att_g, ())
        att_g, other, low.sides, mid.far, high.near = tie(att_g, other, low.sides, mid.far, high.near)

        left = Scatter(ring, mine, other)
        left.start_core()
        mid.ready_near()
        low.ready_far()
        left.ready_sides()
        att_g, left.leaving, low.leaving, mid.leaving = tie(att_g, left.leaving, low.leaving, mid.leaving)
        left.start_sides()
        low.start_far()
        mid.start_near()
        given = (sums_c, sums_a, sums_b, sums_b2, bias_0, bias_1, bias_hi) if beside else ()
        *high_g, mine, other, sums_d = attend_backward(
            ring.c, pairs, pairs, own, x_t, wo_g, q, k, v, p, att_g, given
        )
        first_g, other, left.sides, low.far, mid.near = tie(first_g, other, left.sides, low.far, mid.near)

        right = Scatter(ring, mine, other)
        right.start_core()
        low.ready_near()
        left.ready_far()
        right.ready_sides()
        first_g, right.leaving, left.leaving, low.leaving = tie(first_g, right.leaving, left.leaving, low.leaving)
        right.start_sides()
        left.start_far()
        low.start_near()
        in_g = input_grads(tuple(range(WIDTHS)), first_g, low_g, high_g, query_key, value_output, None)
        in_g, right.sides, left.far, low.near = tie(in_g, right.sides, left.far, low.near)

        left.ready_near()
        right.ready_last()
        right.leaving, left.leaving = tie(right.leaving, left.leaving)
        right.start_last()
        left.start_near()
        outer_g, inner_g = finish(ring, (low, mid, high))
        right.near, left.near, outer_g = tie(right.near, left.near, outer_g)
        first_half, second_half = finish(ring, (left, right))
        split = pairs * BLOCK
        parts = [
            side(entry[:, at : at + split], entry[:, at + 2 * split : at + 3 * split])
            for entry in (first_half, second_half)
            for at in (0, split)
        ]
        wq_g, wk_g, wv_g, wo_g = parts
        if beside:
            last = first_half[:, 4 * split :]
            bias_g = last[:, 16 : 16 + WIDTHS * WIDTHS].reshape(own, WIDTHS, WIDTHS).sum(axis=1)
            vectors_g = [last[:, n] for n in range(count)] + [bias_g.T.reshape(own * WIDTHS)]
        else:
            attention_sums = jnp.concatenate([sums_c[:2], sums_d[:2]], axis=1)
            sums_b = sums_b + sums_b2
            rows = [*attention_sums, sums_a[2], sums_a[0], sums_a[1], sums_b[2], sums_b[0], sums_b[1]]
            rows.append(jnp.concatenate([bias_0, bias_1, bias_hi], axis=0).reshape(hidden))
            vectors_g = [lax.psum_scatter(entry, AXES, scatter_dimension=0, tiled=True) for entry in rows]
        bq_g, bv_g, bo_g, ga_g, sa_g, bu_g, gb_g, sb_g, bi_g = vectors_g
        return (
            out, in_g, wq_g, bq_g, wk_g, wv_g, bv_g, wo_g, bo_g, ga_g, sa_g, inner_g, bi_g, outer_g, bu_g, gb_g, sb_g,
        )

    layered = P(None, AXES, None)
    return jax.shard_map(
        per_device,
        mesh=mesh,
        in_specs=(
            rows_split, rows_split, layered, rows_split, vector_split, rows_split, rows_split, vector_split,
            rows_split, vector_split, vector_split, vector_split, rows_split, vector_split, rows_split,
            vector_split, vector_split, vector_split,
        ),
        out_specs=(
            layered, layered, rows_split, vector_split, rows_split, rows_split, vector_split, rows_split,
            vector_split, vector_split, vector_split, rows_split, vector_split, rows_split, vector_split,
            vector_split, vector_split,
        ),
        check_vma=False,
    )
```

```python
import functools
import math

import jax
import jax.numpy as jnp
from jax import lax
from jax.experimental import pallas as pl
from jax.experimental.pallas import tpu as pltpu
from jax.sharding import PartitionSpec as P

HEADS = 12
HEAD_DIM = 64
WIDTHS = 4
BLOCK = 128
AXES = ("dp", "fsdp")
BF = jnp.bfloat16
F32 = jnp.float32
MIB = 1024 * 1024
LIMIT = 60
LIMIT_PLACE = 60
LIMIT_ATTEND = 60
BYTES = 3.3e6


def matmul(left_side, right_side):
    return lax.dot_general(
        left_side, right_side, (((1,), (0,)), ((), ())), preferred_element_type=F32
    )


def matmul_last(left_side, right_side):
    return lax.dot_general(
        left_side, right_side, (((1,), (1,)), ((), ())), preferred_element_type=F32
    )


def windows(length):
    count = length // BLOCK
    spans = []
    for i in range(count):
        start = max(0, i - 1) * BLOCK
        spans.append((start, min(count, i + 2) * BLOCK - start))
    return spans


def call(kernel, limit, micros, **options):
    return pl.pallas_call(
        kernel,
        compiler_params=pltpu.CompilerParams(vmem_limit_bytes=limit * MIB),
        cost_estimate=pl.CostEstimate(flops=0, bytes_accessed=int(micros * BYTES), transcendentals=0),
        **options,
    )


def shape_of(shape, dtype):
    return jax.ShapeDtypeStruct(shape, dtype)


def whole(shape):
    return pl.BlockSpec(shape, lambda *_: (0,) * len(shape))


def attend_kernel(x, wq, wk, wv, vec, seg_col, seg_row, q_o, k_o, v_o, a_o, p_o, bias):
    spans = windows(x.shape[0])

    @pl.when(pl.program_id(0) == 0)
    def _():
        for i, (start, span) in enumerate(spans):
            same = seg_col[i * BLOCK : (i + 1) * BLOCK, :] == seg_row[:, start : start + span]
            bias[i, :, :span] = jnp.where(same, 0.0, -1e30)

    rows = x[...]
    q_o[...] = (matmul(rows, wq[...]) + vec[0:1, :]).astype(BF)
    k_o[...] = matmul(rows, wk[...]).astype(BF)
    v_o[...] = (matmul(rows, wv[...]) + vec[1:2, :]).astype(BF)
    lane = lax.broadcasted_iota(jnp.int32, (BLOCK, BLOCK), 1)
    low_half = lane < HEAD_DIM
    factor = 1.0 / math.sqrt(HEAD_DIM)
    mask = jnp.concatenate(
        [jnp.where(low_half, factor, 0.0).astype(BF), jnp.where(low_half, 0.0, factor).astype(BF)], axis=0
    )
    for pair in range(q_o.shape[1] // BLOCK):
        cols = slice(pair * BLOCK, (pair + 1) * BLOCK)
        scores = []
        for i, (start, span) in enumerate(spans):
            q_here = q_o[i * BLOCK : (i + 1) * BLOCK, cols]
            both = jnp.concatenate([q_here, q_here], axis=0) * mask
            scores.append(matmul_last(both, k_o[start : start + span, cols]))
        chances = []
        for i, (start, span) in enumerate(spans):
            blocked = bias[i, :, :span]
            score = scores[i] + jnp.concatenate([blocked, blocked], axis=0)
            shifted = jnp.exp(score - jnp.max(score, axis=1, keepdims=True))
            total = jnp.sum(shifted, axis=1, keepdims=True)
            chances.append((shifted * (1.0 / total)).astype(BF))
        for i, (start, span) in enumerate(spans):
            mixed = matmul(chances[i], v_o[start : start + span, cols])
            here = slice(i * BLOCK, (i + 1) * BLOCK)
            a_o[here, cols] = jnp.where(low_half, mixed[:BLOCK], mixed[BLOCK:]).astype(BF)
            p_o[2 * pair, i, :, :span] = chances[i][:BLOCK]
            p_o[2 * pair + 1, i, :, :span] = chances[i][BLOCK:]


def attend(x, query_key, value_output, vec, segments, segments_row):
    length, width = x.shape
    step = 256
    steps = width // step
    count = length // BLOCK
    part = pl.BlockSpec((length, step), lambda p: (0, p))
    heads = step // HEAD_DIM

    def weight(n):
        return pl.BlockSpec((width, step), lambda p: (0, n * steps + p))

    return call(
        attend_kernel,
        LIMIT_ATTEND,
        9.5,
        grid=(steps,),
        in_specs=[
            whole(x.shape),
            weight(0),
            weight(1),
            weight(0),
            pl.BlockSpec((vec.shape[0], step), lambda p: (0, p)),
            whole((length, 1)),
            whole((1, length)),
        ],
        out_specs=[part, part, part, part, pl.BlockSpec((heads, count, BLOCK, 3 * BLOCK), lambda p: (p, 0, 0, 0))],
        out_shape=[shape_of((length, width), BF)] * 4 + [shape_of((HEADS, count, BLOCK, 3 * BLOCK), BF)],
        scratch_shapes=[pltpu.VMEM((count, BLOCK, 3 * BLOCK), F32)],
        name="attend",
    )(x, query_key, query_key, value_output, vec, segments, segments_row)


def norm_parts(values):
    center = values - jnp.mean(values, axis=1, keepdims=True)
    scale = lax.rsqrt(jnp.mean(center * center, axis=1, keepdims=True) + 1e-12)
    return center * scale, scale


def norm_back(spread_grad, hat, scale):
    return scale * (
        spread_grad
        - jnp.mean(spread_grad, axis=1, keepdims=True)
        - hat * jnp.mean(spread_grad * hat, axis=1, keepdims=True)
    )


def chunk_mask(w, rows):
    lane = lax.broadcasted_iota(jnp.int32, (rows, 2 * BLOCK), 1)
    start = HEAD_DIM * (w % 2)
    return (lane >= start) & (lane < start + 3 * HEAD_DIM)


def window_at(w):
    return w + w // 2


def first_kernel(x, att_a, att_b, wo_a, wo_b, vec, hat_o, scale_o, normed_o, normed_t_o, second_o, x_t_o, branch):
    w = pl.program_id(0)

    @pl.when(w == 0)
    def _():
        branch[...] = x[...].astype(F32) + vec[2:3, :]
        x_t_o[...] = x[...].T

    kept = jnp.where(chunk_mask(w, x.shape[0]), jnp.concatenate([att_a[...], att_b[...]], axis=1).astype(F32), 0.0)
    weight = jnp.concatenate([wo_a[...], wo_b[...]], axis=1)
    first = branch[...] + matmul_last(kept.astype(BF), weight)
    branch[...] = first
    hat, scale = norm_parts(first)
    hat_o[0] = hat.astype(BF)
    scale_o[0] = scale
    normed = hat * vec[3:4, :] + vec[4:5, :]
    second_o[0] = normed + vec[5:6, :]
    low = normed.astype(BF)
    normed_o[0] = low
    normed_t_o[0] = low.T


def first_norm(x, att, weights, vec):
    length, width = x.shape
    base = width // BLOCK
    per_width = pl.BlockSpec((1, length, width), lambda w: (w, 0, 0))
    return call(
        first_kernel,
        LIMIT,
        9.7,
        grid=(WIDTHS,),
        in_specs=[
            whole(x.shape),
            pl.BlockSpec((length, BLOCK), lambda w: (0, window_at(w))),
            pl.BlockSpec((length, BLOCK), lambda w: (0, window_at(w) + 1)),
            pl.BlockSpec((width, BLOCK), lambda w: (0, base + window_at(w))),
            pl.BlockSpec((width, BLOCK), lambda w: (0, base + window_at(w) + 1)),
            whole(vec.shape),
        ],
        out_specs=[
            per_width,
            pl.BlockSpec((1, length, 1), lambda w: (w, 0, 0)),
            per_width,
            pl.BlockSpec((1, width, length), lambda w: (w, 0, 0)),
            per_width,
            whole((width, length)),
        ],
        out_shape=[
            shape_of((WIDTHS, length, width), BF),
            shape_of((WIDTHS, length, 1), F32),
            shape_of((WIDTHS, length, width), BF),
            shape_of((WIDTHS, width, length), BF),
            shape_of((WIDTHS, length, width), F32),
            shape_of((width, length), BF),
        ],
        scratch_shapes=[pltpu.VMEM((length, width), F32)],
        name="first_norm",
    )(x, att, att, weights, weights, vec)


ERF_T = 0.3275911 / math.sqrt(2.0)
BELL = 1.0 / math.sqrt(2.0 * math.pi)
ERF_A = tuple(
    0.5 * entry / BELL for entry in (0.254829592, -0.284496736, 1.421413741, -1.453152027, 1.061405429)
)
ROWS = 512


def gelu_pair(values):
    size = jnp.abs(values)
    bell = jnp.exp2(values * values * (-0.5 * math.log2(math.e)) + math.log2(BELL))
    t = pl.reciprocal(1.0 + ERF_T * size, approx=True)
    poly = ERF_A[4] * t + ERF_A[3]
    for entry in (ERF_A[2], ERF_A[1], ERF_A[0]):
        poly = poly * t + entry
    tail = poly * t * bell
    step = tail - size * bell
    return jnp.maximum(values, 0.0) - size * tail, jnp.where(values >= 0.0, 1.0 - step, step)


def feed_order(chunks):
    return [(j, w) for j in chunks for w in range(j, WIDTHS)]


def copy_of(source, target, sem):
    return pltpu.make_async_copy(source, target, sem)


def forward_step(normed, weights, bias, act, slope, second, column, between=()):
    length, width = normed.shape
    half = weights.shape[1] // 2
    between = list(between)
    for r in range(0, length, ROWS):
        rows = slice(r, r + ROWS)
        inner = matmul(normed[rows, :], weights[:, pl.ds(column, width)]) + bias
        if between:
            between.pop(0)()
        active, tilt = gelu_pair(inner)
        active = active.astype(BF)
        act[rows, :] = active
        slope[rows, :] = tilt.astype(BF)
        second[rows, :] += matmul_last(active, weights[:, pl.ds(half + column, width)])
    for work in between:
        work()


def second_norm(second, og, vec, out, feed, feed_t, sums):
    hat, scale = norm_parts(second[...])
    out[...] = (hat * vec[6:7, :] + vec[7:8, :]).astype(BF)
    grad = og[...].astype(F32)
    sums[0:1, :] += jnp.sum(grad * hat, axis=0, keepdims=True)
    sums[1:2, :] += jnp.sum(grad, axis=0, keepdims=True)
    low = norm_back(grad * vec[6:7, :], hat, scale).astype(BF)
    feed[...] = low
    feed_t[...] = low.T
    sums[2:3, :] += jnp.sum(low.astype(F32), axis=0, keepdims=True)


def backward_parts(feed, feed_t, normed_t, act, slope, weights, column, outer, inner, grads, bias, fresh):
    length, width = feed.shape
    half = weights.shape[1] // 2
    lows = []

    def first():
        part = matmul(feed_t[...], act[...])
        outer[...] = part if fresh else outer[...] + part

    def middle(r):
        rows = slice(r, r + ROWS)
        raw = matmul(feed[rows, :], weights[:, pl.ds(half + column, width)])
        low = (slope[rows, :].astype(F32) * raw).astype(BF)
        bias[...] += jnp.sum(low.astype(F32), axis=0, keepdims=True)
        grads[rows, :] += matmul_last(low, weights[:, pl.ds(column, width)])
        lows.append(low)

    def last():
        part = matmul(normed_t[...], jnp.concatenate(lows, axis=0))
        inner[...] = part if fresh else inner[...] + part

    return [first] + [functools.partial(middle, r) for r in range(0, length, ROWS)] + [last]


def backward_step(feed, feed_t, normed_t, act, slope, weights, column, outer, inner, grads, bias, fresh, ready=None):
    first, *others = backward_parts(
        feed, feed_t, normed_t, act, slope, weights, column, outer, inner, grads, bias, fresh
    )
    first()
    if ready is not None:
        ready()
    for work in others:
        work()


ANY = pl.BlockSpec(memory_space=pl.ANY)
SCALARS = pl.BlockSpec(memory_space=pltpu.SMEM)


def held(array):
    return pl.BlockSpec(memory_space=pltpu.VMEM)


def give_halves(core, outer, inner, mine_h, other_h, sem):
    @pl.when(core == 0)
    def _():
        copy_of(outer, mine_h, sem).start()
        copy_of(inner, other_h, sem).start()

    @pl.when(core != 0)
    def _():
        copy_of(inner, mine_h, sem).start()
        copy_of(outer, other_h, sem).start()

    return [copy_of(outer, mine_h, sem), copy_of(inner, other_h, sem)]


def feed_high_kernel(sources, table, table_b, bi, vec, normed_h, second_h, og_h, normed_t_h, *refs):
    source, count, last = sources[0], len(sources[0].arrays), len(sources[1].arrays)
    pieces, pieces_b, refs = refs[:count], refs[count : count + last], refs[count + last :]
    act_h, slope_h, act_1_h, slope_1_h, out_h, feed_h, feed_t_h, mine_h, other_h, grad_h, bias, sums = refs[:12]
    weights, normed, second, og, normed_t, act, slope, feed, feed_t, outer, inner, outer_b, inner_b = refs[12:25]
    sem_w, sem_n, sem_act, sem_out, sem_give = refs[25:]
    width = normed.shape[2]
    low = WIDTHS - 2

    def rows_of(n):
        return (
            copy_of(normed_h.at[low + n], normed.at[n], sem_n.at[0, n]),
            copy_of(second_h.at[low + n], second.at[n], sem_n.at[1, n]),
            copy_of(og_h.at[low + n], og.at[n], sem_n.at[2, n]),
            copy_of(normed_t_h.at[low + n], normed_t.at[n], sem_n.at[3, n]),
        )

    for copy in rows_of(1)[:2]:
        copy.start()
    source.start(table, pieces, weights, sem_w.at[0], 0, width, 0)

    def start_others():
        for j in range(1, WIDTHS):
            part = width if j < WIDTHS - 1 else width // 2
            source.start(table, pieces, weights, sem_w.at[j], j * width, part, j * width)
            if part < width:
                sources[1].start(table_b, pieces_b, weights, sem_w.at[j], 0, width - part, j * width + part)

    for copy in rows_of(1)[2:] + rows_of(0):
        copy.start()
    sums[...] = jnp.zeros_like(sums)
    bias[...] = jnp.zeros_like(bias)
    for copy in rows_of(1)[:2]:
        copy.wait()
    writes = []

    def norm(n):
        w, base = low + n, 4 * (1 - n)
        writes.extend(
            (
                copy_of(act.at[base], act_h.at[w], sem_act.at[n, 0]),
                copy_of(slope.at[base], slope_h.at[w], sem_act.at[n, 1]),
                copy_of(act.at[base + 1], act_1_h.at[n], sem_act.at[n, 2]),
                copy_of(slope.at[base + 1], slope_1_h.at[n], sem_act.at[n, 3]),
            )
        )
        second_norm(second.at[n], og.at[n], vec, normed.at[n], feed.at[n], feed_t.at[n], sums)
        writes.extend(
            (
                copy_of(normed.at[n], out_h.at[w], sem_out.at[0, n]),
                copy_of(feed.at[n], feed_h.at[w], sem_out.at[1, n]),
                copy_of(feed_t.at[n], feed_t_h.at[w], sem_out.at[2, n]),
            )
        )
        for copy in writes[-7:]:
            copy.start()
        second[n] = feed[n].astype(F32)

    def back(m, n, at):
        return backward_parts(
            feed.at[m], feed_t.at[m], normed_t.at[m], act.at[at], slope.at[at], weights, (low + n) * width,
            outer, inner, second.at[m], bias.at[n], m == n,
        )

    def give(n):
        outer_b[n] = outer[...].astype(BF)
        inner_b[n] = inner[...].astype(BF)
        columns = pl.ds(n * width, width)
        return give_halves(
            table[source.core], outer_b.at[n], inner_b.at[n], mine_h.at[:, columns], other_h.at[:, columns], sem_give.at[n]
        )

    for j in range(WIDTHS):
        if j < 2:
            source.wait(weights, sem_w.at[j], width, j * width)
        if j == 0:
            start_others()
        if j == 2:
            for later in (2, 3):
                source.wait(weights, sem_w.at[later], width, later * width)
            for copy in rows_of(1)[2:] + rows_of(0):
                copy.wait()
        forward_step(normed.at[1], weights, bi[j], act.at[j], slope.at[j], second.at[1], j * width)
    norm(1)
    beside = back(1, 1, 3)
    for j in range(WIDTHS - 1):
        take = 2 if j < 2 else 0
        forward_step(
            normed.at[0], weights, bi[j], act.at[4 + j], slope.at[4 + j], second.at[0], j * width, beside[:take]
        )
        beside = beside[take:]
    given = give(1)
    norm(0)
    for work in back(0, 0, 6) + back(1, 0, 2):
        work()
    given += give(0)
    end = copy_of(second, grad_h, sem_out.at[3, 0])
    end.start()
    for copy in writes + given + [end]:
        copy.wait()


def feed_high(sources, normed, bi, second, og, vec, normed_t):
    _, length, width = normed.shape
    four, four_t = (WIDTHS, length, width), (WIDTHS, width, length)
    two, two_t = (2, length, width), (2, width, length)
    slots = 7
    return call(
        functools.partial(feed_high_kernel, sources),
        LIMIT,
        35,
        in_specs=[SCALARS, SCALARS, held(bi), held(vec)]
        + [ANY] * (4 + len(sources[0].arrays) + len(sources[1].arrays)),
        out_specs=[ANY] * 10 + [held(vec), held(vec)],
        out_shape=[
            shape_of(four, BF),
            shape_of(four, BF),
            shape_of(two, BF),
            shape_of(two, BF),
            shape_of(four, BF),
            shape_of(four, BF),
            shape_of(four_t, BF),
            shape_of((width, 2 * width), BF),
            shape_of((width, 2 * width), BF),
            shape_of(two, F32),
            shape_of((2, 1, width), F32),
            shape_of((8, width), F32),
        ],
        scratch_shapes=[
            pltpu.VMEM((width, 8 * width), BF),
            pltpu.VMEM(two, BF),
            pltpu.VMEM(two, F32),
            pltpu.VMEM(two, BF),
            pltpu.VMEM(two_t, BF),
            pltpu.VMEM((slots, length, width), BF),
            pltpu.VMEM((slots, length, width), BF),
            pltpu.VMEM(two, BF),
            pltpu.VMEM(two_t, BF),
            pltpu.VMEM((width, width), F32),
            pltpu.VMEM((width, width), F32),
            pltpu.VMEM((2, width, width), BF),
            pltpu.VMEM((2, width, width), BF),
            pltpu.SemaphoreType.DMA((WIDTHS, 2)),
            pltpu.SemaphoreType.DMA((4, 2)),
            pltpu.SemaphoreType.DMA((2, 4)),
            pltpu.SemaphoreType.DMA((4, 2)),
            pltpu.SemaphoreType.DMA((2,)),
        ],
        name="feed_high",
    )(
        sources[0].table, sources[1].table, bi, vec, normed, second, og, normed_t, *sources[0].arrays, *sources[1].arrays
    )


def feed_mid_kernel(source, table, bi, vec, normed_h, second_h, og_h, normed_t_h, act_1_h, slope_1_h, grad_in, feed_in, feed_t_in, *refs):
    count = len(source.arrays)
    pieces, refs = refs[:count], refs[count + 3 :]
    act_h, slope_h, out_h, feed_h, feed_t_h, mine_h, other_h, grad_h, bias, sums = refs[:10]
    weights, normed, second, og, normed_t, act, slope, feed, feed_t, grads, outer, inner, outer_b, inner_b = refs[10:24]
    sem_w, sem_n, sem_b, sem_act, sem_out, sem_give = refs[24:]
    width = normed.shape[2]

    def rows_of(w):
        return (
            copy_of(normed_h.at[w], normed.at[w], sem_n.at[0, w]),
            copy_of(second_h.at[w], second.at[w], sem_n.at[1, w]),
            copy_of(og_h.at[w], og.at[w], sem_n.at[2, w]),
        )

    def back_rows(m):
        return (
            copy_of(feed_t_in.at[2 + m], feed_t.at[2 + m], sem_b.at[0, m]),
            copy_of(act_1_h.at[m], act.at[1 + m], sem_b.at[1, m]),
            copy_of(feed_in.at[2 + m], feed.at[2 + m], sem_b.at[2, m]),
            copy_of(slope_1_h.at[m], slope.at[1 + m], sem_b.at[3, m]),
            copy_of(grad_in.at[m], grads.at[1 + m], sem_b.at[4, m]),
        )

    turned = [copy_of(normed_t_h.at[w], normed_t.at[w - 1], sem_n.at[3, w - 1]) for w in range(1, WIDTHS)]
    for copy in rows_of(1)[:2]:
        copy.start()
    for j in range(2):
        source.start(table, pieces, weights, sem_w.at[j], j * width, width, j * width)
    for copy in rows_of(1)[2:] + rows_of(0) + (turned[0],) + back_rows(0) + (turned[1],) + back_rows(1) + (turned[2],):
        copy.start()
    sums[...] = jnp.zeros_like(sums)
    bias[...] = jnp.zeros_like(bias)
    for copy in rows_of(1)[:2]:
        copy.wait()

    def back(m, fresh):
        return backward_parts(
            feed.at[1 + m], feed_t.at[1 + m], normed_t.at[m], act.at[m], slope.at[m], weights, width,
            outer, inner, grads.at[m], bias.at[0], fresh,
        )

    def forward(w, j, between=()):
        at = 0 if j == 1 else 3 + w
        forward_step(normed.at[w], weights, bi[j], act.at[at], slope.at[at], second.at[w], j * width, between)

    source.wait(weights, sem_w.at[0], width, 0)
    forward(1, 0)
    source.wait(weights, sem_w.at[1], width, width)
    for copy in rows_of(1)[2:] + rows_of(0):
        copy.wait()
    forward(1, 1)
    for copy in turned + [copy for m in range(2) for copy in back_rows(m)]:
        copy.wait()
    beside = back(1, True) + back(2, False)
    second_norm(second.at[1], og.at[1], vec, normed.at[1], feed.at[1], feed_t.at[1], sums)
    forward(0, 0, beside[:4])
    second_norm(second.at[0], og.at[0], vec, normed.at[0], feed.at[0], feed_t.at[0], sums)
    grads[0] = feed[1].astype(F32)
    writes = []
    for w in (1, 0):
        writes += [
            copy_of(act.at[3 + w], act_h.at[w], sem_act.at[0, w]),
            copy_of(slope.at[3 + w], slope_h.at[w], sem_act.at[1, w]),
            copy_of(normed.at[w], out_h.at[w], sem_out.at[0, w]),
            copy_of(feed.at[w], feed_h.at[w], sem_out.at[1, w]),
            copy_of(feed_t.at[w], feed_t_h.at[w], sem_out.at[2, w]),
        ]
    writes += [copy_of(grads.at[m], grad_h.at[m], sem_out.at[3, m]) for m in range(WIDTHS - 1)]
    for copy in writes[:10] + writes[11:12]:
        copy.start()
    for work in beside[4:]:
        work()
    writes[12].start()
    for work in back(0, False):
        work()
    writes[10].start()
    outer_b[...] = outer[...].astype(BF)
    inner_b[...] = inner[...].astype(BF)
    writes += give_halves(table[source.core], outer_b, inner_b, mine_h, other_h, sem_give)
    for copy in writes:
        copy.wait()


def feed_mid(source, normed, bi, second, og, vec, normed_t, act_1, slope_1, grad, act, slope, out, feed, feed_t):
    _, length, width = normed.shape
    four, four_t = (WIDTHS, length, width), (WIDTHS, width, length)
    two = (2, length, width)
    many = WIDTHS - 1
    first = 12 + len(source.arrays)
    return call(
        functools.partial(feed_mid_kernel, source),
        LIMIT,
        22,
        in_specs=[SCALARS, held(bi), held(vec)] + [ANY] * (9 + len(source.arrays) + 3),
        out_specs=[ANY] * 8 + [held(vec), held(vec)],
        out_shape=[
            shape_of(four, BF),
            shape_of(four, BF),
            shape_of(four, BF),
            shape_of(four, BF),
            shape_of(four_t, BF),
            shape_of((width, width), BF),
            shape_of((width, width), BF),
            shape_of((many, length, width), F32),
            shape_of((1, 1, width), F32),
            shape_of((8, width), F32),
        ],
        scratch_shapes=[
            pltpu.VMEM((width, 4 * width), BF),
            pltpu.VMEM(two, BF),
            pltpu.VMEM(two, F32),
            pltpu.VMEM(two, BF),
            pltpu.VMEM((many, width, length), BF),
            pltpu.VMEM((5, length, width), BF),
            pltpu.VMEM((5, length, width), BF),
            pltpu.VMEM(four, BF),
            pltpu.VMEM(four_t, BF),
            pltpu.VMEM((many, length, width), F32),
            pltpu.VMEM((width, width), F32),
            pltpu.VMEM((width, width), F32),
            pltpu.VMEM((width, width), BF),
            pltpu.VMEM((width, width), BF),
            pltpu.SemaphoreType.DMA((2, 2)),
            pltpu.SemaphoreType.DMA((4, many)),
            pltpu.SemaphoreType.DMA((5, 2)),
            pltpu.SemaphoreType.DMA((2, 2)),
            pltpu.SemaphoreType.DMA((4, many)),
            pltpu.SemaphoreType.DMA,
        ],
        input_output_aliases={10: 3, 11: 4, first: 0, first + 1: 1, first + 2: 2},
        name="feed_mid",
    )(source.table, bi, vec, normed, second, og, normed_t, act_1, slope_1, grad, feed, feed_t, *source.arrays, act, slope, out)


def feed_zero_kernel(source, table, vec, feed_h, feed_t_h, normed_t_h, act_h, slope_h, grad_in, hat_h, scale_h, att_h, wo_h, *refs):
    count = len(source.arrays)
    pieces, refs = refs[:count], refs[count:]
    mine_h, other_h, first_g_h, att_g_h, wo_g_h, bias, sums = refs[:7]
    weights, feed, feed_t, normed_t, act, slope, outer, inner, grads, outer_b, inner_b = refs[7:18]
    hat, scale, att, wo, att_g, total, wo_g, wo_g_b = refs[18:26]
    sem_w, sem_in, sem_g, sem_x, sem_out = refs[26:]
    length, width = feed.shape[1:]
    def reads(w):
        return (
            copy_of(feed_t_h.at[w], feed_t.at[w], sem_in.at[0, w]),
            copy_of(act_h.at[w], act.at[w], sem_in.at[1, w]),
            copy_of(feed_h.at[w], feed.at[w], sem_in.at[2, w]),
            copy_of(slope_h.at[w], slope.at[w], sem_in.at[3, w]),
            copy_of(normed_t_h.at[w], normed_t.at[w], sem_in.at[4, w]),
            copy_of(hat_h.at[w], hat.at[w], sem_in.at[5, w]),
            copy_of(scale_h.at[w], scale.at[w], sem_in.at[6, w]),
        )

    for w in reversed(range(WIDTHS)):
        for copy in reads(w)[:5]:
            copy.start()
        if w == WIDTHS - 1:
            source.start(table, pieces, weights, sem_w, 0, width, 0)
        if w > 0:
            copy_of(grad_in.at[w - 1], grads.at[w], sem_g.at[w]).start()
        if w == WIDTHS - 1:
            beside = (copy_of(att_h, att, sem_x.at[0]), copy_of(wo_h.at[:, pl.ds(width, width)], wo, sem_x.at[1]))
            for copy in beside:
                copy.start()
        for copy in reads(w)[5:]:
            copy.start()
    bias[...] = jnp.zeros_like(bias)
    sums[...] = jnp.zeros_like(sums)
    total[...] = jnp.zeros_like(total)
    wo_g[...] = jnp.zeros_like(wo_g)

    for w in reversed(range(WIDTHS)):
        if w == WIDTHS - 1:
            for copy in reads(w)[:2]:
                copy.wait()

        def ready(w=w):
            for copy in reads(w)[2:] + (reads(w - 1)[:2] if w else ()) + (beside if w == WIDTHS - 1 else ()):
                copy.wait()
            if w == WIDTHS - 1:
                source.wait(weights, sem_w, width, 0)
            if w == 0:
                grads[0] = feed[0].astype(F32)
            else:
                copy_of(grad_in.at[w - 1], grads.at[w], sem_g.at[w]).wait()

        backward_step(
            feed.at[w], feed_t.at[w], normed_t.at[w], act.at[w], slope.at[w], weights, 0, outer, inner, grads.at[w],
            bias.at[0], w == WIDTHS - 1, ready,
        )
        rough, factor = hat[w].astype(F32), scale[w]
        grad = grads[w]
        sums[0:1, :] += jnp.sum(grad * rough, axis=0, keepdims=True)
        sums[1:2, :] += jnp.sum(grad, axis=0, keepdims=True)
        first_g = norm_back(grad * vec[3:4, :], rough, factor)
        grads[w] = first_g
        copy_of(grads.at[w], first_g_h.at[w], sem_out.at[0]).start()
        low = first_g.astype(BF)
        wide = low.astype(F32)
        sums[2:3, :] += jnp.sum(wide, axis=0, keepdims=True)
        total[...] += wide
        kept = (w + 1) * 3 * HEAD_DIM
        columns = -(-kept // BLOCK) * BLOCK
        found = matmul(low, wo[:, :columns])
        if columns > kept:
            lane = lax.broadcasted_iota(jnp.int32, (length, columns), 1)
            found = jnp.where(lane < kept, found, 0.0)
        att_g[w, :, :columns] = found.astype(BF)
        if columns < width:
            att_g[w, :, columns:] = jnp.zeros((length, width - columns), BF)
        copy_of(att_g.at[w], att_g_h.at[w], sem_out.at[1]).start()
        start = BLOCK * window_at(w)
        part = jnp.where(chunk_mask(w, length), att[:, start : start + 2 * BLOCK].astype(F32), 0.0).astype(BF)
        wo_g[:, start : start + 2 * BLOCK] += matmul(total[...].astype(BF).T, part)
    outer_b[...] = outer[...].astype(BF)
    inner_b[...] = inner[...].astype(BF)
    writes = give_halves(table[source.core], outer_b, inner_b, mine_h, other_h, sem_out.at[2])
    wo_g_b[...] = wo_g[...].astype(BF)
    copy = copy_of(wo_g_b, wo_g_h, sem_out.at[2])
    copy.start()
    for copy in writes + [copy, copy_of(grads, first_g_h, sem_out.at[0]), copy_of(att_g, att_g_h, sem_out.at[1])]:
        copy.wait()


def feed_zero(source, vec, feed, feed_t, normed_t, act, slope, grad, hat, scale, att, wo):
    _, length, width = feed.shape
    four, four_t = (WIDTHS, length, width), (WIDTHS, width, length)
    return call(
        functools.partial(feed_zero_kernel, source),
        LIMIT,
        28,
        in_specs=[SCALARS, held(vec)] + [ANY] * (10 + len(source.arrays)),
        out_specs=[ANY] * 5 + [held(vec), held(vec)],
        out_shape=[
            shape_of((width, width), BF),
            shape_of((width, width), BF),
            shape_of(four, F32),
            shape_of(four, BF),
            shape_of((width, width), BF),
            shape_of((1, 1, width), F32),
            shape_of((8, width), F32),
        ],
        scratch_shapes=[
            pltpu.VMEM((width, 2 * width), BF),
            pltpu.VMEM(four, BF),
            pltpu.VMEM(four_t, BF),
            pltpu.VMEM(four_t, BF),
            pltpu.VMEM(four, BF),
            pltpu.VMEM(four, BF),
            pltpu.VMEM((width, width), F32),
            pltpu.VMEM((width, width), F32),
            pltpu.VMEM(four, F32),
            pltpu.VMEM((width, width), BF),
            pltpu.VMEM((width, width), BF),
            pltpu.VMEM(four, BF),
            pltpu.VMEM((WIDTHS, length, 1), F32),
            pltpu.VMEM((length, width), BF),
            pltpu.VMEM((width, width), BF),
            pltpu.VMEM(four, BF),
            pltpu.VMEM((length, width), F32),
            pltpu.VMEM((width, width), F32),
            pltpu.VMEM((width, width), BF),
            pltpu.SemaphoreType.DMA((2,)),
            pltpu.SemaphoreType.DMA((7, WIDTHS)),
            pltpu.SemaphoreType.DMA((WIDTHS,)),
            pltpu.SemaphoreType.DMA((2,)),
            pltpu.SemaphoreType.DMA((3,)),
        ],
        name="feed_zero",
    )(source.table, vec, feed, feed_t, normed_t, act, slope, grad, hat, scale, att, wo, *source.arrays)


def attend_back_kernel(first_pair, pairs, own, core, x_t, wo_g, q, k, v, p, g, *refs):
    dq_o, dk_o, dv_o, mine_o, other_o, sums_o, dk_t, dv_t = refs
    step = pl.program_id(0)
    pair = first_pair + step
    columns = pairs * BLOCK
    length = q.shape[0]
    spans = windows(length)
    factor = 1.0 / math.sqrt(HEAD_DIM)
    lane = lax.broadcasted_iota(jnp.int32, (BLOCK, BLOCK), 1)
    low_half = lane < HEAD_DIM
    masks = (
        jnp.where(low_half, 1.0, 0.0).astype(BF),
        jnp.where(low_half, 0.0, 1.0).astype(BF),
    )

    def run(first):
        widths = list(range(first, WIDTHS))
        many = len(widths)
        dk_t[...] = jnp.zeros_like(dk_t)
        dv_t[...] = jnp.zeros_like(dv_t)
        q_t = (q[...] * jnp.asarray(factor, BF)).T
        g_t = [g[w].T for w in widths]
        mask = jnp.concatenate([masks[0]] * many + [masks[1]] * many, axis=0)
        wide = jnp.concatenate([low_half] * many, axis=0)
        chance_g = []
        for i, (start, span) in enumerate(spans):
            g_here = jnp.concatenate([g[w, i * BLOCK : (i + 1) * BLOCK, :] for w in widths], axis=0)
            chance_g.append(matmul_last(jnp.concatenate([g_here, g_here], axis=0) * mask, v[start : start + span, :]))
        scores_g = []
        for i, (start, span) in enumerate(spans):
            lows = []
            for half in range(2):
                chances = p[half, i, :, :span].astype(F32)
                for n in range(many):
                    at = (half * many + n) * BLOCK
                    product = chances * chance_g[i][at : at + BLOCK, :]
                    row = jnp.sum(product, axis=1, keepdims=True)
                    lows.append((product - chances * row).astype(BF))
            scores_g.append(lows)
        for i, (start, span) in enumerate(spans):
            here = slice(i * BLOCK, (i + 1) * BLOCK)
            near = slice(start, start + span)
            lows = scores_g[i]
            found = matmul(jnp.concatenate(lows, axis=0), k[near, :] * jnp.asarray(factor, BF))
            dq = jnp.where(wide, found[: many * BLOCK], found[many * BLOCK :]).astype(BF)
            for n, w in enumerate(widths):
                dq_o[w, here, :] = dq[n * BLOCK : (n + 1) * BLOCK, :]
            for half in range(2):
                rows_of = slice(half * HEAD_DIM, (half + 1) * HEAD_DIM)
                for n, w in enumerate(widths):
                    dk_t[w, rows_of, near] += matmul(q_t[rows_of, here], lows[half * many + n])
                stacked = jnp.concatenate([g_t[n][rows_of, here] for n in range(many)], axis=0)
                values_g = matmul(stacked, p[half, i, :, :span])
                for n, w in enumerate(widths):
                    dv_t[w, rows_of, near] += values_g[n * HEAD_DIM : (n + 1) * HEAD_DIM, :]
        totals = [jnp.zeros((length, BLOCK), F32) for _ in range(3)]
        for w in range(WIDTHS):
            if w < first:
                for ref in (dq_o, dk_o, dv_o):
                    ref[w] = jnp.zeros((length, BLOCK), BF)
                continue
            dk_o[w] = dk_t[w].astype(BF).T
            dv_o[w] = dv_t[w].astype(BF).T
            for n, ref in enumerate((dq_o, dk_o, dv_o)):
                totals[n] += ref[w].astype(F32)
        here = pl.ds(pl.multiple_of(step * BLOCK, BLOCK), BLOCK)
        beside = pl.ds(pl.multiple_of(columns + step * BLOCK, BLOCK), BLOCK)
        sums_o[0:1, here] = jnp.sum(totals[0], axis=0, keepdims=True)
        sums_o[1:2, here] = jnp.sum(totals[2], axis=0, keepdims=True)
        parts = [matmul(x_t[...], total.astype(BF)).astype(BF) for total in totals]

        def fill(first, second):
            first[:, here] = parts[0]
            first[:, beside] = parts[1]
            second[:, here] = parts[2]
            second[:, beside] = wo_g[...]

        pl.when(core[0] == 0)(lambda: fill(mine_o, other_o))
        pl.when(core[0] != 0)(lambda: fill(other_o, mine_o))

    heads_each = HEADS // WIDTHS
    firsts = [(2 * n) // heads_each for n in range(HEADS // 2)]
    for first in sorted(set(firsts)):
        members = [n for n, f in enumerate(firsts) if f == first and first_pair <= n < first_pair + pairs]
        if not members:
            continue

        @pl.when((pair >= members[0]) & (pair <= members[-1]))
        def _(first=first):
            run(first)


def vector_rows(own, sums_o, given):
    sums_c, sums_a, sums_b, sums_b2, bias_0, bias_1, bias_hi = given
    width = sums_a.shape[1]
    rows = [
        jnp.concatenate([sums_c[0:1, :], sums_o[0:1, :]], axis=1),
        jnp.concatenate([sums_c[1:2, :], sums_o[1:2, :]], axis=1),
        sums_a[2:3, :],
        sums_a[0:1, :],
        sums_a[1:2, :],
        sums_b[2:3, :] + sums_b2[2:3, :],
        sums_b[0:1, :] + sums_b2[0:1, :],
        sums_b[1:2, :] + sums_b2[1:2, :],
        jnp.zeros((8, width), F32),
    ]
    for j in range(WIDTHS):
        rows += [(bias_0[0], bias_1[0], bias_hi[0], bias_hi[1])[j]] * WIDTHS
    rows.append(jnp.zeros((BLOCK - 16 - WIDTHS * WIDTHS, width), F32))
    turned = jnp.concatenate(rows, axis=0).T
    lane = lax.broadcasted_iota(jnp.int32, (own, BLOCK), 1)
    blocks = []
    each = width // (own * WIDTHS)
    for j in range(WIDTHS):
        for n in range(each):
            at = (j * each + n) * own
            block = jnp.where(lane < 8, turned[at : at + own, :], 0.0)
            for m in range(WIDTHS):
                start = (n * WIDTHS + m) * own
                block = jnp.where(lane == 16 + WIDTHS * j + m, turned[start : start + own, :], block)
            blocks.append(block.astype(BF))
    return jnp.concatenate(blocks, axis=0)


def attend_back_last_kernel(first_pair, pairs, own, *refs):
    given, rest = refs[8:-8], refs[-8:]
    attend_back_kernel(first_pair, pairs, own, *refs[:8], *rest)
    if given:
        mine_o, other_o, sums_o = rest[3:6]

        @pl.when(pl.program_id(0) == pairs - 1)
        def _():
            block = vector_rows(own, sums_o, given)
            mine_o[:, 2 * pairs * BLOCK :] = block
            other_o[:, 2 * pairs * BLOCK :] = block


def attend_backward(core, first_pair, pairs, own, x_t, wo_g, q, k, v, p, g, given):
    length, width = q.shape
    columns = pairs * BLOCK
    part = pl.BlockSpec((length, BLOCK), lambda n: (0, first_pair + n))
    wide = pl.BlockSpec((WIDTHS, length, BLOCK), lambda n: (0, 0, first_pair + n))
    wide_o = pl.BlockSpec((WIDTHS, length, BLOCK), lambda n: (0, 0, n))
    out = (width, 2 * columns + (BLOCK if given else 0))
    return call(
        functools.partial(attend_back_last_kernel, first_pair, pairs, own),
        LIMIT,
        12,
        grid=(pairs,),
        in_specs=[
            SCALARS,
            whole(x_t.shape),
            pl.BlockSpec((width, BLOCK), lambda n: (0, first_pair + n)),
            part,
            part,
            part,
            pl.BlockSpec((2,) + p.shape[1:], lambda n: (first_pair + n, 0, 0, 0)),
            wide,
        ]
        + [whole(entry.shape) for entry in given],
        out_specs=[wide_o] * 3 + [whole(out)] * 2 + [whole((8, columns))],
        out_shape=[shape_of((WIDTHS, length, columns), BF)] * 3
        + [shape_of(out, BF)] * 2
        + [shape_of((8, columns), F32)],
        scratch_shapes=[pltpu.VMEM((WIDTHS, BLOCK, length), F32)] * 2,
        name="attend_backward",
    )(jnp.full((1,), core, jnp.int32), x_t, wo_g, q, k, v, p, g, *given)


def input_kernel(some, first_g, dq_a, dk_a, dv_a, dq_b, dk_b, dv_b, wq, wk, wv, *refs):
    out = refs[-1]
    w = pl.program_id(0)
    split = dq_a.shape[2]
    for section in some:
        kept = -(-(section + 1) * 3 * HEAD_DIM // BLOCK) * BLOCK

        @pl.when(w == section - some[0])
        def _():
            total = first_g[0]
            for low, high, weight in ((dq_a, dq_b, wq), (dk_a, dk_b, wk), (dv_a, dv_b, wv)):
                near = min(kept, split)
                total += matmul_last(low[0, :, :near], weight[:, :near])
                if kept > split:
                    total += matmul_last(high[0, :, : kept - split], weight[:, split:kept])
            out[0] = total


def input_grads(some, first_g, low, high, query_key, value_output, earlier):
    _, length, width = first_g.shape
    base = some[0]
    per_width = pl.BlockSpec((1, length, width), lambda w: (w + base, 0, 0))
    part = pl.BlockSpec((1, length, low[0].shape[2]), lambda w: (w + base, 0, 0))
    last = pl.BlockSpec((1, length, high[0].shape[2]), lambda w: (jnp.maximum(w + base, WIDTHS // 2), 0, 0))
    given = [] if earlier is None else [earlier]

    def weight(n):
        return pl.BlockSpec((width, width), lambda w: (0, n))

    return call(
        functools.partial(input_kernel, some),
        LIMIT,
        8,
        grid=(len(some),),
        in_specs=[per_width] + [part] * 3 + [last] * 3 + [weight(0), weight(1), weight(0)] + [ANY] * len(given),
        out_specs=per_width,
        out_shape=shape_of(first_g.shape, F32),
        input_output_aliases={10: 0} if given else {},
        name="input_grads",
    )(first_g, *low, *high, query_key, query_key, value_output, *given)


def tie(*values):
    return lax.optimization_barrier(values)


class Ring:
    def __init__(self, mesh):
        self.dp = mesh.shape["dp"]
        self.fsdp = mesh.shape["fsdp"]
        self.square = self.fsdp == 8 and self.dp == 4
        index = lax.axis_index("fsdp")
        self.z = lax.axis_index("dp")
        self.y, self.x, self.c = index // 4, (index // 2) % 2, index % 2

    def swap(self, value, bit):
        total = self.dp * self.fsdp
        return lax.ppermute(value, AXES, [(i, i ^ bit) for i in range(total)])

    def shift(self, value, by):
        total = self.dp * self.fsdp
        return lax.ppermute(value, AXES, [(i, (i + by * self.fsdp) % total) for i in range(total)])

    def along(self, value, bit):
        total = self.dp * self.fsdp
        return lax.ppermute(value, AXES, [(i, i ^ (bit * self.fsdp)) for i in range(total)])

    def mine(self, first, second):
        return jnp.where(self.c == 0, first, second)


CORE, X_SIDE, Y_SIDE = 1, 2, 4


class Gather:
    def __init__(self, ring, halves):
        self.ring, self.halves = ring, halves
        self.shard = halves
        self.line = self.came = self.sides = self.corners = self.crossed = ()
        self.copies, self.table = self.places() if ring.square else ([], jnp.asarray(ring.c, jnp.int32).reshape(1))

    def start_core(self):
        ring = self.ring
        if ring.square:
            kept, sent = ring.mine(*self.halves), ring.mine(*self.halves[::-1])
            came = ring.swap(sent, CORE)
            self.shard = ring.mine(jnp.concatenate([kept, came], axis=0), jnp.concatenate([came, kept], axis=0))

    def keep(self, other, most):
        if self.ring.square:
            self.shard, other.shard = self.shard[:, :most], self.shard[:, most:]
        else:
            self.halves = tuple(half[:, :most] for half in self.halves)

    def start_line(self, first=0, columns=None):
        ring = self.ring
        if ring.square:
            part = self.shard[:, first : self.shard.shape[1] if columns is None else first + columns]
            self.came += (tuple(ring.shift(part, by) for by in range(1, ring.dp)),)

    def ready_line(self):
        if self.ring.square:
            came = [jnp.concatenate(parts, axis=1) for parts in zip(*self.came)]
            self.line = jnp.stack([self.shard] + came)

    def start_sides(self):
        ring = self.ring
        if ring.square:
            self.sides = (ring.swap(self.line, X_SIDE), ring.swap(self.line, Y_SIDE))

    def start_corners(self):
        ring, half = self.ring, self.ring.dp // 2
        if ring.square:
            self.corners = (
                ring.swap(self.sides[0][:half], Y_SIDE),
                ring.swap(self.sides[1][half:], X_SIDE),
            )

    def cross(self, *values):
        if self.ring.square:
            self.crossed += tuple(self.ring.swap(value, CORE) for value in values)

    def places(self):
        ring, half = self.ring, self.ring.dp // 2
        rows = 2 * self.halves[0].shape[0]
        own = (
            (ring.dp, 0, ring.y, ring.x),
            (ring.dp, 0, ring.y, 1 - ring.x),
            (ring.dp, 0, 1 - ring.y, ring.x),
            (half, 0, 1 - ring.y, 1 - ring.x),
            (half, half, 1 - ring.y, 1 - ring.x),
        )
        copies, at = [], []
        for n, (count, behind, y, x) in enumerate(own):
            for index in range(count):
                z = (ring.z + ring.dp - behind - index) % ring.dp
                copies.append((n, index))
                at.append(jnp.asarray(rows * ((z * 2 + y) * 2 + x), jnp.int32))
        return copies, jnp.stack(at + [jnp.asarray(ring.c, jnp.int32)])

    def pieces(self):
        return [self.line, *self.sides, *self.corners, *self.crossed]

    def source(self):
        return Source(self)


class PlaneFirst(Gather):
    def start_plane(self):
        ring = self.ring
        if ring.square:
            row = jnp.stack([self.shard, ring.swap(self.shard, X_SIDE)])
            self.sides = (row, ring.swap(row, Y_SIDE))

    def ready_line(self):
        if self.ring.square:
            self.line = jnp.concatenate(self.sides)

    def start_line(self):
        ring = self.ring
        if ring.square:
            self.came = tuple(ring.shift(self.line, by) for by in range(1, ring.dp))

    def places(self):
        ring = self.ring
        rows = 2 * self.halves[0].shape[0]
        copies, at = [], []
        for behind in range(ring.dp):
            z = (ring.z + ring.dp - behind) % ring.dp
            for index, (y, x) in enumerate(
                ((ring.y, ring.x), (ring.y, 1 - ring.x), (1 - ring.y, ring.x), (1 - ring.y, 1 - ring.x))
            ):
                copies.append((behind, index))
                at.append(jnp.asarray(rows * ((z * 2 + y) * 2 + x), jnp.int32))
        return copies, jnp.stack(at + [jnp.asarray(ring.c, jnp.int32)])

    def pieces(self):
        return [self.line, *self.came, *self.crossed]


class Source:
    def __init__(self, gather):
        ring = gather.ring
        self.square = ring.square
        self.columns = gather.halves[0].shape[1]
        if ring.square:
            self.rows = gather.shard.shape[0]
            self.arrays = gather.pieces()
        else:
            self.rows = gather.halves[0].shape[0] * ring.dp * ring.fsdp
            self.arrays = [lax.all_gather(half, AXES, axis=0, tiled=True) for half in gather.halves]
        self.copies, self.table = gather.copies, gather.table
        self.core = len(self.copies)

    def start(self, table, pieces, target, sems, first, columns, to):
        apart = target.shape[1] // 2
        if not self.square:
            for half in range(2):
                pltpu.make_async_copy(
                    pieces[half].at[:, pl.ds(first, columns)],
                    target.at[:, pl.ds(half * apart + to, columns)],
                    sems.at[half],
                ).start()
            return
        core = table[self.core]
        many = len(pieces) // 2
        for side in range(2):
            half = core if side == 0 else 1 - core
            for n, (piece, index) in enumerate(self.copies):
                row = pl.multiple_of(table[n], 16)
                pltpu.make_async_copy(
                    pieces[side * many + piece].at[index, :, pl.ds(first, columns)],
                    target.at[pl.ds(row, self.rows), pl.ds(pl.multiple_of(half * apart + to, BLOCK), columns)],
                    sems.at[half],
                ).start()

    def wait(self, target, sems, columns, to):
        for half in range(2):
            whole_half = target.at[:, pl.ds(half * (target.shape[1] // 2) + to, columns)]
            pltpu.make_async_copy(whole_half, whole_half, sems.at[half]).wait()


def place_rows(source, layout, beside):
    count = len(source.arrays)
    rows = source.rows * max(len(source.copies), 1)

    def kernel(table, *refs):
        pieces, outs = refs[:count], refs[count : count + len(layout)]
        sem = refs[-1]
        if not source.square:
            copies = [
                pltpu.make_async_copy(pieces[half].at[:, pl.ds(first, columns)], outs[n], sem.at[0])
                for n, (half, first, columns) in enumerate(layout)
            ]
            for copy in copies:
                copy.start()
            for copy in copies:
                copy.wait()
            return
        many = count // 2
        core = table[source.core]
        parts = [(half, first, columns, outs[n], 0) for n, (half, first, columns) in enumerate(layout)]
        if beside is not None:
            vec, bi, block = refs[count + len(layout) : -1]
            parts.insert(0, (0, beside, BLOCK, block, 1))

        def run(own):
            copies = []
            for half, first, columns, out, which in parts:
                for m, (piece, index) in enumerate(source.copies):
                    row = pl.multiple_of(table[m], 16)
                    copies.append(
                        (
                            which,
                            pltpu.make_async_copy(
                                pieces[piece + (0 if half == own else many)].at[index, :, pl.ds(first, columns)],
                                out.at[pl.ds(row, source.rows), :],
                                sem.at[which],
                            ),
                        )
                    )
            for _, copy in copies:
                copy.start()
            for which, copy in copies:
                if which == 1:
                    copy.wait()
            if beside is not None:
                vector_columns(block, vec, bi)
            for which, copy in copies:
                if which == 0:
                    copy.wait()

        for own in range(2):
            pl.when(core == own)(functools.partial(run, own))

    more = ([], [], [])
    if beside is not None:
        more = (
            [pl.BlockSpec(memory_space=pltpu.VMEM)] * 2,
            [shape_of((8, rows), F32), shape_of((WIDTHS, 1, rows), F32)],
            [pltpu.VMEM((rows, BLOCK), BF)],
        )
    return call(
        kernel,
        LIMIT_PLACE,
        5,
        in_specs=[SCALARS] + [ANY] * count,
        out_specs=[pl.BlockSpec(memory_space=pltpu.VMEM)] * len(layout) + more[0],
        out_shape=[shape_of((rows, columns), BF) for *_, columns in layout] + more[1],
        scratch_shapes=more[2] + [pltpu.SemaphoreType.DMA((2,))],
        name="place_rows",
    )(source.table, *source.arrays)


def vector_columns(block, vec, bi):
    full = block[...].astype(F32)
    width = full.shape[0]
    vec[...] = full.T[:8, :]
    each = 8
    own = width // (each * WIDTHS)
    lane = lax.broadcasted_iota(jnp.int32, (own, BLOCK), 1)
    pieces = []
    for n in range(each):
        for m in range(WIDTHS):
            piece = jnp.zeros((own, BLOCK), F32)
            for j in range(WIDTHS):
                start = (j * each + n) * own
                piece = jnp.where(lane == 16 + WIDTHS * j + m, full[start : start + own, :], piece)
            pieces.append(piece)
    turned = jnp.concatenate(pieces, axis=0).T
    for j in range(WIDTHS):
        at = 16 + WIDTHS * j
        bi[j] = jnp.sum(turned[at : at + WIDTHS, :], axis=0, keepdims=True)


class Scatter:
    def __init__(self, ring, mine, other):
        self.ring, self.kept, self.other = ring, mine, other
        self.came = self.sides = self.leaving = self.far = self.near = self.own = ()

    def start_core(self):
        if self.ring.square:
            self.came = self.ring.swap(self.other, CORE)

    def block(self, y, x):
        dp = self.ring.dp

        def pick(value):
            value = value.reshape(dp, 2, 2, value.shape[0] // (4 * dp), value.shape[1])
            value = lax.dynamic_index_in_dim(value, y, 1, keepdims=False)
            return lax.dynamic_index_in_dim(value, x, 1, keepdims=False)

        return pick(self.kept).astype(F32) + pick(self.came).astype(F32)

    def ready_sides(self):
        ring = self.ring
        if ring.square:
            to_x = self.block(ring.y, 1 - ring.x).astype(BF)
            to_y = self.block(1 - ring.y, ring.x).astype(BF)
            corner = self.block(1 - ring.y, 1 - ring.x).astype(BF)
            self.leaving = (corner, to_x, to_y)

    def start_sides(self):
        ring = self.ring
        if ring.square:
            corner, to_x, to_y = self.leaving
            self.sides = (ring.swap(corner, X_SIDE | Y_SIDE), ring.swap(to_x, X_SIDE), ring.swap(to_y, Y_SIDE))

    def ready_far(self):
        ring = self.ring
        if ring.square:
            line = self.block(ring.y, ring.x)
            for side in self.sides:
                line = line + side.astype(F32)
            line = line.reshape(2, 2, *line.shape[1:])
            self.leaving = lax.dynamic_index_in_dim(line, 1 - ring.z // 2, 0, keepdims=False).astype(BF)
            self.own = lax.dynamic_index_in_dim(line, ring.z // 2, 0, keepdims=False)

    def start_far(self):
        if self.ring.square:
            self.far = self.ring.along(self.leaving, 2)

    def ready_near(self):
        ring = self.ring
        if ring.square:
            pair = self.own + self.far.astype(F32)
            self.leaving = lax.dynamic_index_in_dim(pair, 1 - ring.z % 2, 0, keepdims=False).astype(BF)
            self.own = lax.dynamic_index_in_dim(pair, ring.z % 2, 0, keepdims=False)

    def start_near(self):
        if self.ring.square:
            self.near = (self.ring.along(self.leaving, 1),)

    def ready_last(self):
        ring = self.ring
        if ring.square:
            line = self.block(ring.y, ring.x)
            for side in self.sides:
                line = line + side.astype(F32)
            low = line.astype(BF)
            self.own = lax.dynamic_index_in_dim(line, ring.z, 0, keepdims=False)
            self.leaving = tuple(
                lax.dynamic_index_in_dim(low, (ring.z + by) % ring.dp, 0, keepdims=False) for by in range(1, ring.dp)
            )

    def start_last(self):
        ring = self.ring
        if ring.square:
            self.near = tuple(ring.shift(value, by) for by, value in enumerate(self.leaving, 1))


def finish(ring, groups):
    if not ring.square:
        halves = (
            jnp.concatenate([ring.mine(group.kept, group.other) for group in groups], axis=1),
            jnp.concatenate([ring.mine(group.other, group.kept) for group in groups], axis=1),
        )
        return tuple(lax.psum_scatter(half.astype(F32), AXES, scatter_dimension=0, tiled=True) for half in halves)
    total = jnp.concatenate(
        [functools.reduce(lambda sum_, part: sum_ + part.astype(F32), group.near, group.own) for group in groups], axis=1
    )
    rows = total.shape[0] // 2
    kept, sent = ring.mine(total[:rows], total[rows:]), ring.mine(total[rows:], total[:rows])
    came = ring.swap(sent, CORE)
    return ring.mine(kept, came), ring.mine(came, kept)


def solution(mesh):
    rows_split = P(AXES, None)
    vector_split = P(AXES)

    def per_device(
        tokens,
        segment_ids,
        output_grad,
        query_weight,
        query_bias,
        key_weight,
        value_weight,
        value_bias,
        output_weight,
        output_bias,
        first_gain,
        first_shift,
        inner_weight,
        inner_bias,
        outer_weight,
        outer_bias,
        second_gain,
        second_shift,
    ):
        ring = Ring(mesh)
        devices = ring.dp * ring.fsdp
        width = tokens.shape[1]
        hidden = inner_weight.shape[1]
        own = query_bias.shape[0]
        half = hidden // 2
        singles = (query_bias, value_bias, output_bias, first_gain, first_shift, outer_bias, second_gain, second_shift)
        count = len(singles)
        beside = ring.square and own % 8 == 0
        columns = []
        if beside:
            row = lax.broadcasted_iota(jnp.int32, (BLOCK, own), 0)
            block = jnp.zeros((BLOCK, own), BF)
            for n, vector in enumerate(singles):
                block = jnp.where(row == n, vector[None], block)
            chunk = (ring.z * ring.fsdp + lax.axis_index("fsdp")) // (devices // WIDTHS)
            for n in range(WIDTHS):
                quarter = inner_bias[n * own : (n + 1) * own]
                block = jnp.where(row == 16 + WIDTHS * chunk + n, quarter[None], block)
            columns = [block.T]

        def side(*parts):
            return jnp.concatenate(parts, axis=1)

        one = Gather(ring, (side(query_weight, key_weight, *columns), side(value_weight, output_weight, *columns)))
        most = hidden - width // 2
        two = Gather(ring, (inner_weight, outer_weight))
        three = PlaneFirst(ring, (inner_weight[:, most:], outer_weight[:, most:]))
        pair = 2 * width
        one.start_core()
        one.shard, two.halves = tie(one.shard, two.halves)
        one.start_line()
        two.start_core()
        two.keep(three, most)
        three.start_plane()
        segments = segment_ids[0].reshape(-1, 1)
        one.came, two.shard, three.sides, segments, one.table, three.table = tie(
            one.came, two.shard, three.sides, segments, one.table, three.table
        )
        two.table = one.table
        one.ready_line()
        one.start_sides()
        two.start_line(0, most // 2)
        one.line, one.sides, two.came = tie(one.line, one.sides, two.came)
        one.start_corners()
        two.start_line(most // 2, most - most // 2)
        one.line, one.sides, one.corners, two.came = tie(one.line, one.sides, one.corners, two.came)
        one.cross(one.line, *one.sides, *one.corners)
        two.ready_line()
        two.start_sides()
        source_one = one.source()
        three.sides, _ = tie(three.sides, source_one.arrays)
        three.ready_line()
        three.start_line()
        query_key, value_output, *vectors = place_rows(source_one, ((0, 0, pair), (1, 0, pair)), pair if beside else None)
        if beside:
            vec, bi = vectors
        else:
            vec = jnp.stack([lax.all_gather(entry, AXES, tiled=True) for entry in singles]).astype(F32)
            bi = lax.all_gather(inner_bias, AXES, tiled=True).astype(F32).reshape(WIDTHS, 1, width)
        q, k, v, att, p = attend(tokens, query_key, value_output, vec, segments, segment_ids)
        att, two.line, two.sides, three.line, three.came = tie(att, two.line, two.sides, three.line, three.came)
        two.start_corners()
        two.cross(two.line, *two.sides)
        hat, scale, normed, normed_t, second, x_t = first_norm(tokens, att, value_output, vec)
        normed, two.corners, two.crossed, three.line, three.came = tie(
            normed, two.corners, two.crossed, three.line, three.came
        )
        two.cross(*two.corners)
        three.cross(three.line, *three.came)
        source_two = two.source()

        act, slope, act_1, slope_1, out, feed, feed_t, mine, other, grad, bias_hi, sums_b = feed_high(
            (source_two, three.source()), normed, bi, second, output_grad, vec, normed_t
        )
        high = Scatter(ring, mine, other)
        high.start_core()
        grad, high.came = tie(grad, high.came)
        high.ready_sides()
        grad, high.leaving = tie(grad, high.leaving)
        high.start_sides()
        act, slope, out, feed, feed_t, mine, other, grad, bias_1, sums_b2 = feed_mid(
            source_two, normed, bi, second, output_grad, vec, normed_t, act_1, slope_1, grad, act, slope, out, feed, feed_t
        )
        grad, other, high.sides = tie(grad, other, high.sides)

        mid = Scatter(ring, mine, other)
        mid.start_core()
        high.ready_far()
        mid.ready_sides()
        grad, mid.leaving, high.leaving = tie(grad, mid.leaving, high.leaving)
        mid.start_sides()
        high.start_far()
        mine, other, first_g, att_g, wo_g, bias_0, sums_a = feed_zero(
            source_two, vec, feed, feed_t, normed_t, act, slope, grad, hat, scale, att, value_output
        )
        att_g, other, mid.sides, high.far = tie(att_g, other, mid.sides, high.far)

        low = Scatter(ring, mine, other)
        low.start_core()
        high.ready_near()
        mid.ready_far()
        low.ready_sides()
        att_g, low.leaving, mid.leaving, high.leaving = tie(att_g, low.leaving, mid.leaving, high.leaving)
        low.start_sides()
        mid.start_far()
        high.start_near()
        pairs = HEADS // 4
        *low_g, mine, other, sums_c = attend_backward(ring.c, 0, pairs, own, x_t, wo_g, q, k, v, p, att_g, ())
        att_g, other, low.sides, mid.far, high.near = tie(att_g, other, low.sides, mid.far, high.near)

        left = Scatter(ring, mine, other)
        left.start_core()
        mid.ready_near()
        low.ready_far()
        left.ready_sides()
        att_g, left.leaving, low.leaving, mid.leaving = tie(att_g, left.leaving, low.leaving, mid.leaving)
        left.start_sides()
        low.start_far()
        mid.start_near()
        given = (sums_c, sums_a, sums_b, sums_b2, bias_0, bias_1, bias_hi) if beside else ()
        *high_g, mine, other, sums_d = attend_backward(
            ring.c, pairs, pairs, own, x_t, wo_g, q, k, v, p, att_g, given
        )
        first_g, other, left.sides, low.far, mid.near = tie(first_g, other, left.sides, low.far, mid.near)

        right = Scatter(ring, mine, other)
        right.start_core()
        low.ready_near()
        left.ready_far()
        right.ready_sides()
        first_g, right.leaving, left.leaving, low.leaving = tie(first_g, right.leaving, left.leaving, low.leaving)
        right.start_sides()
        left.start_far()
        low.start_near()
        in_g = input_grads(tuple(range(WIDTHS)), first_g, low_g, high_g, query_key, value_output, None)
        in_g, right.sides, left.far, low.near = tie(in_g, right.sides, left.far, low.near)

        left.ready_near()
        right.ready_last()
        right.leaving, left.leaving = tie(right.leaving, left.leaving)
        right.start_last()
        left.start_near()
        outer_g, inner_g = finish(ring, (low, mid, high))
        right.near, left.near, outer_g = tie(right.near, left.near, outer_g)
        first_half, second_half = finish(ring, (left, right))
        split = pairs * BLOCK
        parts = [
            side(entry[:, at : at + split], entry[:, at + 2 * split : at + 3 * split])
            for entry in (first_half, second_half)
            for at in (0, split)
        ]
        wq_g, wk_g, wv_g, wo_g = parts
        if beside:
            last = first_half[:, 4 * split :]
            bias_g = last[:, 16 : 16 + WIDTHS * WIDTHS].reshape(own, WIDTHS, WIDTHS).sum(axis=1)
            vectors_g = [last[:, n] for n in range(count)] + [bias_g.T.reshape(own * WIDTHS)]
        else:
            attention_sums = jnp.concatenate([sums_c[:2], sums_d[:2]], axis=1)
            sums_b = sums_b + sums_b2
            rows = [*attention_sums, sums_a[2], sums_a[0], sums_a[1], sums_b[2], sums_b[0], sums_b[1]]
            rows.append(jnp.concatenate([bias_0, bias_1, bias_hi], axis=0).reshape(hidden))
            vectors_g = [lax.psum_scatter(entry, AXES, scatter_dimension=0, tiled=True) for entry in rows]
        bq_g, bv_g, bo_g, ga_g, sa_g, bu_g, gb_g, sb_g, bi_g = vectors_g
        return (
            out, in_g, wq_g, bq_g, wk_g, wv_g, bv_g, wo_g, bo_g, ga_g, sa_g, inner_g, bi_g, outer_g, bu_g, gb_g, sb_g,
        )

    layered = P(None, AXES, None)
    return jax.shard_map(
        per_device,
        mesh=mesh,
        in_specs=(
            rows_split, rows_split, layered, rows_split, vector_split, rows_split, rows_split, vector_split,
            rows_split, vector_split, vector_split, vector_split, rows_split, vector_split, rows_split,
            vector_split, vector_split, vector_split,
        ),
        out_specs=(
            layered, layered, rows_split, vector_split, rows_split, rows_split, vector_split, rows_split,
            vector_split, vector_split, vector_split, rows_split, vector_split, rows_split, vector_split,
            vector_split, vector_split,
        ),
        check_vma=False,
    )
```
